32 devices in a mesh: dp: 8 (over y, x, core), head: 4 (over z).
Axes of the slice: x: 2, y: 2, z: 4, core: 2. Of those that a mesh axis runs over, the one named last changes fastest.
Arguments:
- inputs: bfloat16 [16384, 768], P(('dp', 'head')), may hold values from -6 to 6
- segment_ids: int32 [8, 2048], P('dp'), may hold values from 0 to 47, never falling along the last dimension, each value on 1 to 64 neighbouring positions
- features: bfloat16 [2, 12, 32, 64], P(None, 'head'), may hold values from -4 to 4
- norm_gain: float32 [2, 2, 768], replicated, may hold values from 0.5 to 1.5
- query_key_value: bfloat16 [2, 3, 768, 768], P(None, None, 'dp', 'head'), may hold values from -0.21875 to 0.21875
- output_weight: bfloat16 [2, 768, 768], P(None, 'dp', 'head'), may hold values from -0.875 to 0.875
- up_weight: bfloat16 [2, 3072, 768], P(None, 'dp', 'head'), may hold values from -0.21875 to 0.21875
- down_weight: bfloat16 [2, 3072, 768], P(None, 'dp', 'head'), may hold values from -0.15625 to 0.15625
- cotangent: bfloat16 [16384, 768], P(('dp', 'head')), may hold values from -6 to 6
Outputs:
- outputs: bfloat16 [16384, 768], P(('dp', 'head'))
- input_grad: float32 [16384, 768], P(('dp', 'head'))
- gain_grad: float32 [2, 768], replicated
- middle_gain_grad: float32 [2, 768], replicated
- query_key_value_grad: float32 [2, 3, 768, 768], P(None, None, 'dp', 'head')
- output_weight_grad: float32 [2, 768, 768], P(None, 'dp', 'head')
- up_weight_grad: float32 [2, 3072, 768], P(None, 'dp', 'head')
- down_weight_grad: float32 [2, 3072, 768], P(None, 'dp', 'head')
The draws below stay inside these ranges and needn't reach their ends.
Inputs may be any that keep to these rules, and one draw needn't show every extreme that they name: `segment_ids`: along each packed sequence the ids never fall; each of 0 to 47 labels one run of 1 to 64 rows, and some run has exactly 64 rows.
All inputs are finite; a program needn't handle non-finite values.
Results may differ from the reference program's by a relative error of at most 0.04.
The reference program's roundings to bfloat16 on the way count: a program that leaves them out, or rounds other values in their place, can miss the bound.
Values may be sent and summed in bfloat16 or wider, within the bound.
No kernel may reach another device: no remote copies, remote signals or barrier semaphores. Data moves between devices by JAX's collectives and lax.ppermute only.
A program may use at most 256 MiB of HBM per device.

```python
import functools
import math
import jax
import jax.numpy as jnp
import numpy as np
from jax import lax

D = 768
HEADS = 12
HEAD_DIM = 64
FF = 3072
FEATS = 32
LAYERS = 2
SEQ_LEN = 2048
SEGS = 48
MOST = 64
SEQS = 8
TOKENS = 16384


def shard_levels(stream_key, extent, cuts, least, largest):
    level = 1.0
    for axis_at, blocks in cuts:
        draws = jax.random.uniform(jax.random.fold_in(jax.random.fold_in(stream_key, 6), axis_at), (blocks,), jnp.float32, least / len(cuts), largest / len(cuts))
        level = level * jnp.repeat(jnp.exp(draws), extent[axis_at] // blocks).reshape((-1,) + (1,) * (len(extent) - 1 - axis_at))
    return level


def split_up(count, total, bound, slope):
    weights = [(1 << 20) // math.isqrt(standing ** slope) + 1 for standing in range(2, count + 1)]
    spare, counts = total - bound - (count - 1), [1] * (count - 1)
    while spare > 0:
        candidates = [i for i in range(count - 1) if counts[i] < bound]
        mass, budget = sum([weights[i] for i in candidates]), spare
        for i in candidates:
            extra = min(bound - counts[i], max(1, budget * weights[i] // mass), spare)
            counts[i] = counts[i] + extra
            spare = spare - extra
    return np.array([bound] + counts)


def ragged_sizes(rng, count, total, most, lean):
    if count == 2:
        one = jax.random.randint(rng, (), max(1, total - most), min(most, total - 1) + 1)
        return jnp.stack([one, total - one])
    tallies = jnp.asarray(split_up(count, total, most, lean), jnp.int32)
    couples = (count - 1) // 2
    source_of, sink = tallies[1:1 + 2 * couples:2], tallies[2:2 + 2 * couples:2]
    margin = jnp.minimum(source_of - 1, most - sink)
    moved = jax.random.randint(jax.random.fold_in(rng, 1), (couples,), 0, 1 << 20) % (margin + 1)
    tallies = tallies.at[1:1 + 2 * couples:2].set(source_of - moved).at[2:2 + 2 * couples:2].set(sink + moved)
    return tallies[jax.random.permutation(jax.random.fold_in(rng, 2), count)]


def scatter_about(rng, extent, deviation, reach, split=(), kind=jnp.bfloat16):
    factor_of = shard_levels(rng, extent, split, -0.22, 0.18) if split else 1.0
    values = jax.random.normal(rng, extent, jnp.float32) * deviation * factor_of
    return jnp.minimum(jnp.maximum(values, -reach), reach).astype(kind)


def setup_inputs(seed: int = 0) -> dict:
    key_of = jax.random.split(jax.random.key(seed), 10)
    return {
        "inputs": scatter_about(key_of[0], (TOKENS, D), 1.0, 6.0, ((0, 32),)),
        "segment_ids": jax.vmap(lambda own: jnp.searchsorted(jnp.cumsum(ragged_sizes(own, SEGS, SEQ_LEN, MOST, 1)), jnp.arange(SEQ_LEN), side="right"))(jax.random.split(key_of[1], SEQS)).reshape((SEQS, SEQ_LEN)).astype(jnp.int32),
        "features": scatter_about(key_of[2], (LAYERS, HEADS, FEATS, HEAD_DIM), 1.0, 4.0, ((1, 4),)),
        "norm_gain": jnp.clip(1.0 + 0.1 * jax.random.normal(key_of[3], (LAYERS, 2, D), jnp.float32), 0.5, 1.5),
        "query_key_value": scatter_about(key_of[4], (LAYERS, 3, D, D), D ** -0.5, 0.21875, ((2, 8), (3, 4))),
        "output_weight": scatter_about(key_of[5], (LAYERS, D, D), (D // 16) ** -0.5, 0.875, ((1, 8), (2, 4))),
        "up_weight": scatter_about(key_of[6], (LAYERS, FF, D), D ** -0.5, 0.21875, ((1, 8), (2, 4))),
        "down_weight": scatter_about(key_of[7], (LAYERS, FF, D), (FF // 2) ** -0.5, 0.15625, ((1, 8), (2, 4))),
        "cotangent": scatter_about(key_of[8], (TOKENS, D), 1.0, 6.0, ((0, 32),)),
    }


EPSILON = 1e-05
FINEST_PRECISION = lax.Precision.HIGHEST

@jax.custom_vjp
def low(v):
    return lax.optimization_barrier(v.astype(jnp.bfloat16)).astype(jnp.float32)

@jax.custom_vjp
def low_back(v):
    return v

def low_keep(v):
    return (low(v), None)

def low_pass(kept, grad):
    return (grad,)

def back_keep(v):
    return (v, None)

def back_low(kept, grad):
    return (low(grad),)
low.defvjp(low_keep, low_pass)
low_back.defvjp(back_keep, back_low)

def layer_norm(values, gain_row):
    centred = values - lax.optimization_barrier(jnp.mean(values, axis=-1, keepdims=True))
    inverse = lax.rsqrt(lax.optimization_barrier(jnp.mean(centred * centred, axis=-1, keepdims=True)) + EPSILON)
    return centred * inverse * gain_row

def rotary_tables(segment_ids, head_width):
    seq_count, seq_width = segment_ids.shape
    places = jnp.arange(seq_width, dtype=jnp.int32)
    starts = jnp.concatenate([jnp.ones((seq_count, 1), jnp.bool_), segment_ids[:, 1:] != segment_ids[:, :-1]], axis=1)
    first_place = lax.cummax(jnp.where(starts, places[None, :], 0), axis=1)
    position = (places[None, :] - first_place).astype(jnp.float32).reshape(-1)
    halves = head_width // 2
    frequency = jnp.exp(jnp.arange(halves, dtype=jnp.float32) * (-2.0 * math.log(10000.0) / head_width))
    angles = position[:, None] * frequency[None, :]
    cosine = jnp.concatenate([jnp.cos(angles), jnp.cos(angles)], axis=1)[:, None, :]
    sine_table = jnp.concatenate([jnp.sin(angles), jnp.sin(angles)], axis=1)[:, None, :]
    return (cosine, sine_table)

def rotate(values, cosine, sine_table):
    halves = values.shape[-1] // 2
    turned = jnp.concatenate([-values[..., halves:], values[..., :halves]], axis=-1)
    return values * cosine + turned * sine_table

def feature_map(row_values, random_feature_table):
    score_logits = jnp.einsum('raw,axw->rax', row_values, random_feature_table, precision=FINEST_PRECISION)
    squares = lax.optimization_barrier(jnp.sum(row_values * row_values, axis=-1, keepdims=True))
    return jnp.exp(score_logits - 0.5 * squares) / math.sqrt(random_feature_table.shape[1])

def sequence_attention(random_feature_table, pieces):
    query_rows, key_rows, value_rows, seq_ids = pieces
    cosine, sine_table = rotary_tables(seq_ids[None, :], HEAD_DIM)
    scale_factor = HEAD_DIM ** (-0.25)
    queries = rotate(query_rows, cosine, sine_table) * scale_factor
    keys_turned = rotate(key_rows, cosine, sine_table) * scale_factor
    phi_query = low(feature_map(queries, random_feature_table))
    phi_key = low(feature_map(keys_turned, random_feature_table))
    same_segment = (seq_ids[:, None] == seq_ids[None, :]).astype(jnp.float32)
    scores = low_back(jnp.einsum('qhm,khm->hqk', phi_query, phi_key, precision=FINEST_PRECISION) * same_segment[None])
    totals = lax.optimization_barrier(jnp.sum(scores, axis=-1, keepdims=True))
    weights = low(scores / totals)
    mixed_heads = jnp.einsum('hqk,khd->qhd', weights, low(value_rows), precision=FINEST_PRECISION)
    return low(low_back(mixed_heads)).reshape(SEQ_LEN, D)

def residual_block(residual, gain_pair, qkv_weight, out_weight, up_matrix, down_matrix, random_feature_table, segment_ids):
    normed_a = low(layer_norm(residual, gain_pair[0]))
    projected = low_back(jnp.einsum('td,cde->cte', normed_a, qkv_weight, precision=FINEST_PRECISION))
    shaped = projected.reshape(3, SEQS, SEQ_LEN, HEADS, HEAD_DIM)
    attend = jax.checkpoint(functools.partial(sequence_attention, random_feature_table))
    mixed = lax.map(attend, (shaped[0], shaped[1], shaped[2], segment_ids)).reshape(TOKENS, D)
    middle = residual + low_back(jnp.einsum('te,de->td', mixed, out_weight, precision=FINEST_PRECISION))
    normed_c = low(layer_norm(middle, gain_pair[1]))
    hidden = low_back(jnp.einsum('td,fd->tf', normed_c, up_matrix, precision=FINEST_PRECISION))
    activated = low(jax.nn.gelu(hidden, approximate=False))
    return middle + low_back(jnp.dot(activated, down_matrix, precision=FINEST_PRECISION))

def reference(inputs, segment_ids, features, norm_gain, query_key_value, output_weight, up_weight, down_weight, cotangent):
    tables = features.astype(jnp.float32)

    def forward(residual, gains, qkv_all, out_all, up_all, down_all):
        for layer_index in range(LAYERS):
            residual = residual_block(residual, gains[layer_index], qkv_all[layer_index], out_all[layer_index], up_all[layer_index], down_all[layer_index], tables[layer_index], segment_ids)
        return residual
    result, pullback = jax.vjp(forward, inputs.astype(jnp.float32), norm_gain, query_key_value.astype(jnp.float32), output_weight.astype(jnp.float32), up_weight.astype(jnp.float32), down_weight.astype(jnp.float32))
    gradients = pullback(cotangent.astype(jnp.float32))
    gain_all = gradients[1]
    return (result.astype(jnp.bfloat16), gradients[0], gain_all[:, 0], gain_all[:, 1], gradients[2], gradients[3], gradients[4], gradients[5])
```

```python
import functools
import math

import jax
import jax.numpy as jnp
from jax import lax
from jax.experimental import pallas as pl
from jax.experimental.pallas import tpu as pltpu
from jax.sharding import PartitionSpec as P

MOST = 64
EPSILON = 1e-05
QUERY_ROWS = 128
KEY_ROWS = QUERY_ROWS + 2 * MOST
GROUP = 4
VMEM_BYTES = 60 * 2**20

BF16 = jnp.bfloat16
F32 = jnp.float32
CONTRACT_LAST = (((1,), (1,)), ((), ()))
CONTRACT_FIRST = (((0,), (0,)), ((), ()))
CONTRACT_MIDDLE = (((1,), (0,)), ((), ()))

ERF_TOP = (
    0.00022905065861350646,
    0.0034082910107109506,
    0.050955695062380861,
    0.18520832239976145,
    1.128379143519084,
)
ERF_BOTTOM = (
    -1.1791602954361697e-7,
    0.000023547966471313185,
    0.0010179625278914885,
    0.014070470171167667,
    0.11098505178285362,
    0.49746925110067538,
    1.0,
)


def dot(left, right, dims=CONTRACT_MIDDLE):
    return lax.dot_general(left, right, dims, preferred_element_type=F32)


def polynomial(terms, at):
    total = jnp.full_like(at, terms[0])
    for term in terms[1:]:
        total = total * at + term
    return total


def erf(values):
    values = jnp.clip(values, -3.832506856900711, 3.832506856900711)
    square = values * values
    return values * polynomial(ERF_TOP, square) / polynomial(ERF_BOTTOM, square)


def gelu_and_slope(hidden):
    cumulative = 0.5 * (1.0 + erf(hidden * (1.0 / math.sqrt(2.0))))
    density = jnp.exp(-0.5 * hidden * hidden) * (1.0 / math.sqrt(2.0 * math.pi))
    return hidden * cumulative, cumulative + hidden * density


def normalised(values):
    centred = values - jnp.mean(values, axis=-1, keepdims=True)
    inverse = lax.rsqrt(jnp.mean(centred * centred, axis=-1, keepdims=True) + EPSILON)
    return centred * inverse, inverse


def norm_back(grad_out, gain, hat, inverse):
    scaled = grad_out * gain
    first_mean = jnp.mean(scaled, axis=-1, keepdims=True)
    second_mean = jnp.mean(scaled * hat, axis=-1, keepdims=True)
    return inverse * (scaled - first_mean - hat * second_mean)


def each_block(count, size, step):
    def run(index, carry):
        step(pl.ds(pl.multiple_of(index * size, size), size), index)
        return carry

    lax.fori_loop(0, count, run, 0)


def swap_halves(values, half):
    width = values.shape[-1]
    lane = lax.broadcasted_iota(jnp.int32, values.shape, len(values.shape) - 1)
    ahead = pltpu.roll(values, width - half, 1)
    behind = pltpu.roll(values, half, 1)
    return jnp.where(lane % (2 * half) < half, ahead, behind)


def two_parts(values):
    high = values.astype(BF16)
    return high, (values - high.astype(F32)).astype(BF16)


def phi_of(rows, table, ones):
    high, low = two_parts(rows)
    square_high, square_low = two_parts(rows * rows)
    logits = dot(high, table) + dot(low, table)
    squares = dot(square_high, ones) + dot(square_low, ones)
    return jnp.exp(logits - 0.5 * squares) * (1.0 / math.sqrt(table.shape[1] // GROUP))


def head_masks(width, dtype):
    lane = lax.broadcasted_iota(jnp.int32, (1, width), 1) // (width // GROUP)
    return [jnp.where(lane == head, 1.0, 0.0).astype(dtype) for head in range(GROUP)]


def spread_heads(values):
    return jnp.concatenate([values * mask for mask in head_masks(values.shape[1], BF16)], axis=0)


def gather_heads(values):
    masks = head_masks(values.shape[-1], F32)
    total = values[0] * masks[0]
    for head in range(1, GROUP):
        total = total + values[head] * masks[head]
    return total


def block_scores(phi_q, phi_k, ids_column, ids_row):
    scores = dot(phi_q, phi_k, CONTRACT_LAST)
    same = (ids_column == ids_row).astype(F32)
    scores = scores.reshape(GROUP, QUERY_ROWS, KEY_ROWS) * same[None]
    totals = jnp.sum(scores, axis=-1, keepdims=True)
    inverse = jnp.where(totals > 0.0, 1.0 / totals, 0.0)
    return scores * inverse, inverse, same


def key_start(index, rows):
    start = jnp.clip(index * QUERY_ROWS - MOST, 0, rows - KEY_ROWS)
    return pl.multiple_of(start, MOST)


def attention_forward(
    scale,
    state,
    gain_1,
    gain_2,
    qkv,
    out_weight,
    table,
    ones,
    cosine,
    sine,
    ids_column,
    ids_row,
    normed_a,
    query,
    key,
    value,
    mixed,
    middle,
    normed_c,
    total,
    phi_q,
    phi_k,
):
    group = pl.program_id(0)
    rows = state.shape[0]
    half = cosine.shape[1] // GROUP // 2

    @pl.when(group == 0)
    def _():
        def step(block, index):
            hat, _ = normalised(state[block, :])
            normed_a[block, :] = (hat * gain_1[...]).astype(BF16)
            total[block, :] = state[block, :]

        each_block(rows // 64, 64, step)

    for part, (held, phi) in enumerate(((query, phi_q), (key, phi_k))):
        projected = dot(normed_a[...], qkv[part])
        turned = (projected * cosine[...] + swap_halves(projected, half) * sine[...]) * scale
        held[...] = turned
        phi[...] = phi_of(turned, table[0], ones[...]).astype(BF16)
    value[...] = dot(normed_a[...], qkv[2]).astype(BF16)

    def step(block, index):
        keys = pl.ds(key_start(index, rows), KEY_ROWS)
        weights, _, _ = block_scores(
            spread_heads(phi_q[block, :]), phi_k[keys, :], ids_column[block, :], ids_row[index]
        )
        weights = weights.reshape(GROUP * QUERY_ROWS, KEY_ROWS).astype(BF16)
        found = dot(weights, value[keys, :])
        mixed[block, :] = gather_heads(found.reshape(GROUP, QUERY_ROWS, -1)).astype(BF16)

    each_block(rows // QUERY_ROWS, QUERY_ROWS, step)
    total[...] += dot(mixed[...], out_weight[...], CONTRACT_LAST)

    @pl.when(group == pl.num_programs(0) - 1)
    def _():
        def step(block, index):
            middle[block, :] = total[block, :]
            hat, _ = normalised(total[block, :])
            normed_c[block, :] = (hat * gain_2[...]).astype(BF16)

        each_block(rows // 64, 64, step)


def attention_backward(
    scale,
    grad_middle,
    state,
    gain_1,
    qkv,
    out_weight,
    table,
    ones,
    cosine,
    sine,
    ids_column,
    ids_row,
    normed_a,
    query,
    key,
    value,
    mixed,
    grad_state,
    grad_gain,
    grad_qkv,
    grad_out,
    total,
    branch,
    grad_mixed,
    phi_q,
    phi_k,
    grad_phi_q,
    grad_phi_k,
    grad_value,
):
    group = pl.program_id(0)
    rows = state.shape[0]
    half = cosine.shape[1] // GROUP // 2
    own = pl.ds(MOST, rows - 2 * MOST)

    @pl.when(group == 0)
    def _():
        branch[...] = grad_middle[...].astype(BF16)
        total[...] = jnp.zeros_like(total)

    grad_mixed[...] = dot(branch[...], out_weight[...]).astype(BF16)
    grad_out[...] = dot(branch[own, :], mixed[own, :], CONTRACT_FIRST).astype(BF16)
    phi_q[...] = phi_of(query[...], table[0], ones[...])
    phi_k[...] = phi_of(key[...], table[0], ones[...])
    grad_phi_k[...] = jnp.zeros_like(grad_phi_k)
    grad_value[...] = jnp.zeros_like(grad_value)

    def step(block, index):
        keys = pl.ds(key_start(index, rows), KEY_ROWS)
        spread_q = spread_heads(phi_q[block, :].astype(BF16))
        spread_grad = spread_heads(grad_mixed[block, :])
        keys_phi = phi_k[keys, :].astype(BF16)
        weights, inverse, same = block_scores(
            spread_q, keys_phi, ids_column[block, :], ids_row[index]
        )
        flat = (GROUP * QUERY_ROWS, KEY_ROWS)
        grad_weights = dot(spread_grad, value[keys, :], CONTRACT_LAST)
        grad_value[keys, :] += dot(
            weights.reshape(flat).astype(BF16), spread_grad, CONTRACT_FIRST
        )
        grad_weights = grad_weights.reshape(weights.shape)
        inner = jnp.sum(grad_weights * weights, axis=-1, keepdims=True)
        grad_scores = ((grad_weights - inner) * inverse * same[None]).astype(BF16).reshape(flat)
        found = dot(grad_scores, keys_phi)
        grad_phi_q[block, :] = gather_heads(found.reshape(GROUP, QUERY_ROWS, -1))
        grad_phi_k[keys, :] += dot(grad_scores, spread_q, CONTRACT_FIRST)

    each_block(rows // QUERY_ROWS, QUERY_ROWS, step)

    def through_map(grad_phi, phi, held):
        high, low = two_parts(grad_phi[...] * phi[...])
        along = dot(high, table[0], CONTRACT_LAST) + dot(low, table[0], CONTRACT_LAST)
        summed = dot(high, ones[...], CONTRACT_LAST) + dot(low, ones[...], CONTRACT_LAST)
        grad_rows = (along - held[...] * summed) * scale
        turned = grad_rows * cosine[...] + swap_halves(grad_rows * sine[...], half)
        return turned.astype(BF16)

    for part in range(3):
        if part == 0:
            gradient = through_map(grad_phi_q, phi_q, query)
        elif part == 1:
            gradient = through_map(grad_phi_k, phi_k, key)
        else:
            gradient = grad_value[...].astype(BF16)
        grad_mixed[...] = gradient
        grad_qkv[part] = dot(normed_a[own, :], grad_mixed[own, :], CONTRACT_FIRST).astype(BF16)
        total[...] += dot(grad_mixed[...], qkv[part], CONTRACT_LAST)

    @pl.when(group == pl.num_programs(0) - 1)
    def _():
        grad_gain[...] = jnp.zeros_like(grad_gain)

        def step(block, index):
            hat, inverse = normalised(state[block, :])
            back = norm_back(total[block, :], gain_1[...], hat, inverse)
            grad_state[block, :] = grad_middle[block, :] + back

            @pl.when((index > 0) & (index < rows // 64 - 1))
            def _():
                grad_gain[...] += jnp.sum(total[block, :] * hat, axis=0, keepdims=True)

        each_block(rows // 64, 64, step)


def feed_forward(middle, normed_c, up, down, activated, slope, state, total, hidden):
    chunk = pl.program_id(0)
    rows = middle.shape[0]

    @pl.when(chunk == 0)
    def _():
        total[...] = middle[...]

    hidden[...] = dot(normed_c[...], up[...], CONTRACT_LAST)

    def step(block, index):
        value, back = gelu_and_slope(hidden[block, :])
        activated[block, :] = value.astype(BF16)
        slope[block, :] = back.astype(BF16)

    each_block(rows // 32, 32, step)
    total[...] += dot(activated[...], down[...])

    @pl.when(chunk == pl.num_programs(0) - 1)
    def _():
        state[...] = total[...]


def feed_back(
    gradient,
    middle,
    gain_2,
    normed_c,
    activated,
    slope,
    up,
    down,
    grad_middle,
    grad_gain,
    grad_up,
    grad_down,
    total,
    branch,
    grad_hidden,
    grad_act,
):
    chunk = pl.program_id(0)
    rows = middle.shape[0]
    own = pl.ds(MOST, rows - 2 * MOST)

    @pl.when(chunk == 0)
    def _():
        branch[...] = gradient[...].astype(BF16)
        total[...] = jnp.zeros_like(total)

    grad_act[...] = dot(branch[...], down[...], CONTRACT_LAST)

    def step(block, index):
        grad_hidden[block, :] = (grad_act[block, :] * slope[block, :].astype(F32)).astype(BF16)

    each_block(rows // 32, 32, step)
    grad_down[...] = dot(activated[own, :], branch[own, :], CONTRACT_FIRST).astype(BF16)
    grad_up[...] = dot(grad_hidden[own, :], normed_c[own, :], CONTRACT_FIRST).astype(BF16)
    total[...] += dot(grad_hidden[...], up[...])

    @pl.when(chunk == pl.num_programs(0) - 1)
    def _():
        grad_gain[...] = jnp.zeros_like(grad_gain)

        def step(block, index):
            hat, inverse = normalised(middle[block, :])
            back = norm_back(total[block, :], gain_2[...], hat, inverse)
            grad_middle[block, :] = gradient[block, :] + back

            @pl.when((index > 0) & (index < rows // 64 - 1))
            def _():
                grad_gain[...] += jnp.sum(total[block, :] * hat, axis=0, keepdims=True)

        each_block(rows // 64, 64, step)


def whole(shape):
    return pl.BlockSpec(shape, lambda step: (0,) * len(shape))


def columns(rows, width):
    return pl.BlockSpec((rows, width), lambda step: (0, step))


def leading(shape):
    return pl.BlockSpec(shape, lambda step: (step,) + (0,) * (len(shape) - 1))


def parts_columns(parts, rows, width):
    return pl.BlockSpec((parts, rows, width), lambda step: (0, 0, step))


def struct(shape, dtype):
    return jax.ShapeDtypeStruct(shape, dtype)


def kernel_call(kernel, steps, in_specs, out_specs, out_shape, scratch, flops):
    return pl.pallas_call(
        kernel,
        grid=(steps,),
        in_specs=in_specs,
        out_specs=out_specs,
        out_shape=out_shape,
        scratch_shapes=scratch,
        compiler_params=pltpu.CompilerParams(vmem_limit_bytes=VMEM_BYTES),
        cost_estimate=pl.CostEstimate(flops=flops, bytes_accessed=flops // 600, transcendentals=0),
    )


def run_attention_forward(state, gains, qkv, out_weight, table, ones, tables, ids, scale):
    rows, width = state.shape
    wide = table.shape[1]
    small = table.shape[2]
    blocks = rows // QUERY_ROWS
    return kernel_call(
        functools.partial(attention_forward, scale),
        width // wide,
        [
            whole((rows, width)),
            whole((1, width)),
            whole((1, width)),
            parts_columns(3, width, wide),
            columns(width, wide),
            leading((1, wide, small)),
            whole((wide, small)),
            whole((rows, wide)),
            whole((rows, wide)),
            whole((rows, 1)),
            whole((blocks, 1, KEY_ROWS)),
        ],
        [
            whole((rows, width)),
            columns(rows, wide),
            columns(rows, wide),
            columns(rows, wide),
            columns(rows, wide),
            whole((rows, width)),
            whole((rows, width)),
        ],
        [
            struct((rows, width), BF16),
            struct((rows, width), F32),
            struct((rows, width), F32),
            struct((rows, width), BF16),
            struct((rows, width), BF16),
            struct((rows, width), F32),
            struct((rows, width), BF16),
        ],
        [
            pltpu.VMEM((rows, width), F32),
            pltpu.VMEM((rows, small), BF16),
            pltpu.VMEM((rows, small), BF16),
        ],
        2 * rows * width * width * 5,
    )(state, gains[0][None], gains[1][None], qkv, out_weight, table, ones, *tables, *ids)


def run_attention_backward(
    grad_middle, state, gain, qkv, out_weight, table, ones, tables, ids, kept, scale
):
    rows, width = state.shape
    wide = table.shape[1]
    small = table.shape[2]
    blocks = rows // QUERY_ROWS
    return kernel_call(
        functools.partial(attention_backward, scale),
        width // wide,
        [
            whole((rows, width)),
            whole((rows, width)),
            whole((1, width)),
            parts_columns(3, width, wide),
            columns(width, wide),
            leading((1, wide, small)),
            whole((wide, small)),
            whole((rows, wide)),
            whole((rows, wide)),
            whole((rows, 1)),
            whole((blocks, 1, KEY_ROWS)),
            whole((rows, width)),
            columns(rows, wide),
            columns(rows, wide),
            columns(rows, wide),
            columns(rows, wide),
        ],
        [
            whole((rows, width)),
            whole((1, width)),
            parts_columns(3, width, wide),
            columns(width, wide),
        ],
        [
            struct((rows, width), F32),
            struct((1, width), F32),
            struct((3, width, width), BF16),
            struct((width, width), BF16),
        ],
        [
            pltpu.VMEM((rows, width), F32),
            pltpu.VMEM((rows, width), BF16),
            pltpu.VMEM((rows, wide), BF16),
            pltpu.VMEM((rows, small), F32),
            pltpu.VMEM((rows, small), F32),
            pltpu.VMEM((rows, small), F32),
            pltpu.VMEM((rows, small), F32),
            pltpu.VMEM((rows, wide), F32),
        ],
        2 * rows * width * width * 10,
    )(grad_middle, state, gain[None], qkv, out_weight, table, ones, *tables, *ids, *kept)


def hidden_chunk(count):
    return 512 if count % 512 == 0 else count


def run_feed_forward(middle, normed_c, up, down):
    rows, width = middle.shape
    count = up.shape[0]
    chunk = hidden_chunk(count)
    return kernel_call(
        feed_forward,
        count // chunk,
        [
            whole((rows, width)),
            whole((rows, width)),
            leading((chunk, width)),
            leading((chunk, width)),
        ],
        [columns(rows, chunk), columns(rows, chunk), whole((rows, width))],
        [
            struct((rows, count), BF16),
            struct((rows, count), BF16),
            struct((rows, width), F32),
        ],
        [pltpu.VMEM((rows, width), F32), pltpu.VMEM((rows, chunk), F32)],
        4 * rows * width * count,
    )(middle, normed_c, up, down)


def run_feed_back(gradient, middle, gain, normed_c, activated, slope, up, down):
    rows, width = middle.shape
    count = up.shape[0]
    chunk = hidden_chunk(count)
    return kernel_call(
        feed_back,
        count // chunk,
        [
            whole((rows, width)),
            whole((rows, width)),
            whole((1, width)),
            whole((rows, width)),
            columns(rows, chunk),
            columns(rows, chunk),
            leading((chunk, width)),
            leading((chunk, width)),
        ],
        [
            whole((rows, width)),
            whole((1, width)),
            leading((chunk, width)),
            leading((chunk, width)),
        ],
        [
            struct((rows, width), F32),
            struct((1, width), F32),
            struct((count, width), BF16),
            struct((count, width), BF16),
        ],
        [
            pltpu.VMEM((rows, width), F32),
            pltpu.VMEM((rows, width), BF16),
            pltpu.VMEM((rows, chunk), BF16),
            pltpu.VMEM((rows, chunk), F32),
        ],
        8 * rows * width * count,
    )(gradient, middle, gain[None], normed_c, activated, slope, up, down)


def gather_weight(weight, dim):
    wide = lax.all_gather(weight, "head", axis=dim + 1, tiled=True)
    return lax.all_gather(wide, "dp", axis=dim, tiled=True)


def scatter_grad(gradient, dim):
    part = lax.psum_scatter(gradient, "dp", scatter_dimension=dim, tiled=True)
    return lax.psum_scatter(part, "head", scatter_dimension=dim + 1, tiled=True).astype(F32)


def with_halo(inputs, cotangent):
    count = lax.axis_size("head")
    both = jnp.concatenate([inputs, cotangent], axis=1)
    before = lax.ppermute(both[-MOST:], "head", [(i, i + 1) for i in range(count - 1)])
    after = lax.ppermute(both[:MOST], "head", [(i + 1, i) for i in range(count - 1)])
    joined = jnp.concatenate([before, both, after], axis=0).astype(F32)
    return joined[:, : inputs.shape[1]], joined[:, inputs.shape[1] :]


def window_ids(segment_ids, own_rows):
    padded = jnp.pad(segment_ids[0], (MOST, MOST), constant_values=-1)
    begin = lax.axis_index("head") * own_rows
    ids = lax.dynamic_slice(padded, (begin,), (own_rows + 2 * MOST,))
    place = jnp.arange(ids.shape[0])
    earlier = (ids[:, None] == ids[None, :]) & (place[None, :] < place[:, None])
    position = jnp.sum(earlier.astype(F32), axis=1)
    used = (ids >= ids[MOST]) & (ids <= ids[MOST + own_rows - 1])
    column = jnp.where(used, ids, -1)[:, None]
    row = jnp.where(used, ids, -2)
    starts = [
        min(max(b * QUERY_ROWS - MOST, 0), ids.shape[0] - KEY_ROWS)
        for b in range(ids.shape[0] // QUERY_ROWS)
    ]
    rows = jnp.stack([row[start : start + KEY_ROWS] for start in starts])[:, None, :]
    return position, (column, rows)


def rotary_tables(position, head_width):
    halves = head_width // 2
    frequency = jnp.exp(jnp.arange(halves, dtype=F32) * (-2.0 * math.log(10000.0) / head_width))
    angles = position[:, None] * frequency[None, :]
    cosine, sine = jnp.cos(angles), jnp.sin(angles)
    return (
        jnp.tile(jnp.concatenate([cosine, cosine], axis=1), (1, GROUP)),
        jnp.tile(jnp.concatenate([-sine, sine], axis=1), (1, GROUP)),
    )


def body(
    inputs,
    segment_ids,
    features,
    norm_gain,
    query_key_value,
    output_weight,
    up_weight,
    down_weight,
    cotangent,
):
    layer_count = norm_gain.shape[0]
    own_rows = inputs.shape[0]
    head_width = features.shape[3]
    feature_count = features.shape[2]
    scale = head_width ** (-0.25)
    own = slice(MOST, MOST + own_rows)

    state, gradient = with_halo(inputs, cotangent)
    position, ids = window_ids(segment_ids, own_rows)
    tables = rotary_tables(position, head_width)
    all_features = lax.all_gather(features, "head", axis=1, tiled=True)
    shaped = all_features.reshape(layer_count, -1, GROUP, feature_count, head_width)
    eye = jnp.eye(GROUP, dtype=BF16)
    blocks = jnp.einsum("lghmw,hk->lghwkm", shaped, eye).reshape(
        layer_count, -1, GROUP * head_width, GROUP * feature_count
    )
    ones = jnp.kron(eye, jnp.ones((head_width, feature_count), BF16))

    weights = [
        (
            gather_weight(query_key_value[layer], 1),
            gather_weight(output_weight[layer], 0),
            gather_weight(up_weight[layer], 0),
            gather_weight(down_weight[layer], 0),
        )
        for layer in range(layer_count)
    ]
    stored = []
    for layer in range(layer_count):
        qkv, out_weight, up, down = weights[layer]
        normed_a, query, key, value, mixed, middle, normed_c = run_attention_forward(
            state, norm_gain[layer], qkv, out_weight, blocks[layer], ones, tables, ids, scale
        )
        activated, slope, after = run_feed_forward(middle, normed_c, up, down)
        stored.append((state, (normed_a, query, key, value, mixed), middle, normed_c, activated, slope))
        state = after
    outputs = state[own].astype(BF16)
    gains = [None] * layer_count
    shares = [None] * layer_count
    for layer in reversed(range(layer_count)):
        qkv, out_weight, up, down = weights[layer]
        before, kept, middle, normed_c, activated, slope = stored[layer]
        grad_middle, gain_c, grad_up, grad_down = run_feed_back(
            gradient, middle, norm_gain[layer, 1], normed_c, activated, slope, up, down
        )
        gradient, gain_a, grad_qkv, grad_out = run_attention_backward(
            grad_middle,
            before,
            norm_gain[layer, 0],
            qkv,
            out_weight,
            blocks[layer],
            ones,
            tables,
            ids,
            kept,
            scale,
        )
        gains[layer] = jnp.concatenate([gain_a, gain_c])
        shares[layer] = (
            scatter_grad(grad_qkv, 1),
            scatter_grad(grad_out, 0),
            scatter_grad(grad_up, 0),
            scatter_grad(grad_down, 0),
        )
    gain_total = lax.psum(jnp.stack(gains), ("dp", "head"))
    return (
        outputs,
        gradient[own],
        gain_total[:, 0],
        gain_total[:, 1],
        *(jnp.stack(list(kind)) for kind in zip(*shares)),
    )


def solution(mesh):
    in_specs = (
        P(("dp", "head"), None),
        P("dp", None),
        P(None, "head", None, None),
        P(),
        P(None, None, "dp", "head"),
        P(None, "dp", "head"),
        P(None, "dp", "head"),
        P(None, "dp", "head"),
        P(("dp", "head"), None),
    )
    out_specs = (
        P(("dp", "head"), None),
        P(("dp", "head"), None),
        P(),
        P(),
        P(None, None, "dp", "head"),
        P(None, "dp", "head"),
        P(None, "dp", "head"),
        P(None, "dp", "head"),
    )
    return jax.shard_map(body, mesh=mesh, in_specs=in_specs, out_specs=out_specs, check_vma=False)
```

```python
import functools
import math

import jax
import jax.numpy as jnp
from jax import lax
from jax.experimental import pallas as pl
from jax.experimental.pallas import tpu as pltpu
from jax.sharding import PartitionSpec as P

MOST = 64
EPSILON = 1e-05
QUERY_ROWS = 128
KEY_ROWS = QUERY_ROWS + 2 * MOST
GROUP = 4
VMEM_BYTES = 60 * 2**20

BF16 = jnp.bfloat16
F32 = jnp.float32
CONTRACT_LAST = (((1,), (1,)), ((), ()))
CONTRACT_FIRST = (((0,), (0,)), ((), ()))
CONTRACT_MIDDLE = (((1,), (0,)), ((), ()))

TAIL_SCALE = 0.3275911 / math.sqrt(2.0)
TAIL_TERMS = (1.061405429, -1.453152027, 1.421413741, -0.284496736, 0.254829592)


def dot(left, right, dims=CONTRACT_MIDDLE):
    return lax.dot_general(left, right, dims, preferred_element_type=F32)


def gelu_and_slope(hidden):
    bell = jnp.exp(hidden * hidden * -0.5)
    below = 1.0 + jnp.abs(hidden) * TAIL_SCALE
    guess = pl.reciprocal(below, approx=True)
    inverse = guess * (2.0 - below * guess)
    tail = 0.5 * TAIL_TERMS[0]
    for term in TAIL_TERMS[1:]:
        tail = tail * inverse + 0.5 * term
    tail = tail * inverse * bell
    cumulative = jnp.where(hidden > 0.0, 1.0 - tail, tail)
    return hidden * cumulative, cumulative + hidden * (bell * (1.0 / math.sqrt(2.0 * math.pi)))


def normalised(values):
    centred = values - jnp.mean(values, axis=-1, keepdims=True)
    inverse = lax.rsqrt(jnp.mean(centred * centred, axis=-1, keepdims=True) + EPSILON)
    return centred * inverse, inverse


def norm_back(grad_out, gain, hat, inverse):
    scaled = grad_out * gain
    first_mean = jnp.mean(scaled, axis=-1, keepdims=True)
    second_mean = jnp.mean(scaled * hat, axis=-1, keepdims=True)
    return inverse * (scaled - first_mean - hat * second_mean)


def each_block(count, size, step):
    def run(index, carry):
        step(pl.ds(pl.multiple_of(index * size, size), size), index)
        return carry

    lax.fori_loop(0, count, run, 0)


def swap_halves(values, half):
    width = values.shape[-1]
    lane = lax.broadcasted_iota(jnp.int32, values.shape, len(values.shape) - 1)
    ahead = pltpu.roll(values, width - half, 1)
    behind = pltpu.roll(values, half, 1)
    return jnp.where(lane % (2 * half) < half, ahead, behind)


def two_parts(values):
    high = values.astype(BF16)
    return high, (values - high.astype(F32)).astype(BF16)


def phi_of(rows, table, ones):
    high, low = two_parts(rows)
    square_high, square_low = two_parts(rows * rows)
    logits = dot(high, table) + dot(low, table)
    squares = dot(square_high, ones) + dot(square_low, ones)
    return jnp.exp(logits - 0.5 * squares) * (1.0 / math.sqrt(table.shape[1] // GROUP))


def head_masks(width, dtype):
    lane = lax.broadcasted_iota(jnp.int32, (1, width), 1) // (width // GROUP)
    return [jnp.where(lane == head, 1.0, 0.0).astype(dtype) for head in range(GROUP)]


def spread_heads(values):
    return jnp.concatenate([values * mask for mask in head_masks(values.shape[1], BF16)], axis=0)


def gather_heads(values):
    masks = head_masks(values.shape[-1], F32)
    total = values[0] * masks[0]
    for head in range(1, GROUP):
        total = total + values[head] * masks[head]
    return total


def block_scores(phi_q, phi_k, ids_column, ids_row):
    scores = dot(phi_q, phi_k, CONTRACT_LAST)
    same = (ids_column == ids_row).astype(F32)
    scores = scores.reshape(GROUP, QUERY_ROWS, KEY_ROWS) * same[None]
    totals = jnp.sum(scores, axis=-1, keepdims=True)
    inverse = jnp.where(totals > 0.0, 1.0 / totals, 0.0)
    return scores * inverse, inverse, same


def key_start(index, rows):
    start = jnp.clip(index * QUERY_ROWS - MOST, 0, rows - KEY_ROWS)
    return pl.multiple_of(start, MOST)


def attention_forward(
    scale,
    piece_count,
    places,
    state,
    gain_1,
    gain_2,
    table,
    ones,
    cosine,
    sine,
    ids_column,
    ids_row,
    *others,
):
    pieces = others[:piece_count]
    (weights, normed_a, query, key, value, mixed, middle, normed_c, total, phi_q, phi_k, arrived) = (
        others[piece_count:]
    )
    group = pl.program_id(0)
    rows = state.shape[0]
    width = state.shape[1]
    wide = query.shape[1]
    half = cosine.shape[1] // GROUP // 2

    def copies():
        for index, piece in enumerate(pieces):
            place = pl.ds(pl.multiple_of(places[index], 16), piece.shape[0])
            yield pltpu.make_async_copy(piece, weights.at[place, :], arrived.at[index])

    def part_of(part):
        return weights[:, pl.ds(pl.multiple_of(part * width + group * wide, wide), wide)]

    @pl.when(group == 0)
    def _():
        for copy in copies():
            copy.start()

        def step(block, index):
            hat, _ = normalised(state[block, :])
            normed_a[block, :] = (hat * gain_1[...]).astype(BF16)
            total[block, :] = state[block, :]

        each_block(rows // 64, 64, step)
        for copy in copies():
            copy.wait()

    for part, (held, phi) in enumerate(((query, phi_q), (key, phi_k))):
        projected = dot(normed_a[...], part_of(part))
        turned = (projected * cosine[...] + swap_halves(projected, half) * sine[...]) * scale
        held[...] = turned
        phi[...] = phi_of(turned, table[0], ones[...]).astype(BF16)
    value[...] = dot(normed_a[...], part_of(2)).astype(BF16)

    def step(block, index):
        keys = pl.ds(key_start(index, rows), KEY_ROWS)
        weights, _, _ = block_scores(
            spread_heads(phi_q[block, :]), phi_k[keys, :], ids_column[block, :], ids_row[index]
        )
        weights = weights.reshape(GROUP * QUERY_ROWS, KEY_ROWS).astype(BF16)
        found = dot(weights, value[keys, :])
        mixed[block, :] = gather_heads(found.reshape(GROUP, QUERY_ROWS, -1)).astype(BF16)

    each_block(rows // QUERY_ROWS, QUERY_ROWS, step)
    total[...] += dot(mixed[...], part_of(3), CONTRACT_LAST)

    @pl.when(group == pl.num_programs(0) - 1)
    def _():
        def step(block, index):
            middle[block, :] = total[block, :]
            hat, _ = normalised(total[block, :])
            normed_c[block, :] = (hat * gain_2[...]).astype(BF16)

        each_block(rows // 64, 64, step)


def attention_backward(
    scale,
    places,
    grad_middle,
    state,
    gain_1,
    weight_q,
    weight_k,
    weight_v,
    out_weight,
    table,
    ones,
    cosine,
    sine,
    ids_column,
    ids_row,
    normed_a,
    query,
    key,
    value,
    mixed,
    grad_state,
    grad_gain,
    grad_far,
    grad_near,
    grad_weight,
    leaving,
    total,
    branch,
    grad_mixed,
    phi_q,
    phi_k,
    grad_phi_q,
    grad_phi_k,
    grad_value,
):
    group = pl.program_id(0)
    rows = state.shape[0]
    half = cosine.shape[1] // GROUP // 2
    own = pl.ds(MOST, rows - 2 * MOST)
    width = state.shape[1]
    wide = query.shape[1]

    def part_of(part):
        return pl.ds(pl.multiple_of(part * width + group * wide, wide), wide)

    @pl.when(group == 0)
    def _():
        branch[...] = grad_middle[...].astype(BF16)
        total[...] = jnp.zeros_like(total)

    grad_mixed[...] = dot(branch[...], out_weight[...]).astype(BF16)
    grad_weight[:, part_of(3)] = dot(branch[own, :], mixed[own, :], CONTRACT_FIRST).astype(BF16)
    phi_q[...] = phi_of(query[...], table[0], ones[...])
    phi_k[...] = phi_of(key[...], table[0], ones[...])
    grad_phi_k[...] = jnp.zeros_like(grad_phi_k)
    grad_value[...] = jnp.zeros_like(grad_value)

    def step(block, index):
        keys = pl.ds(key_start(index, rows), KEY_ROWS)
        spread_q = spread_heads(phi_q[block, :].astype(BF16))
        spread_grad = spread_heads(grad_mixed[block, :])
        keys_phi = phi_k[keys, :].astype(BF16)
        weights, inverse, same = block_scores(
            spread_q, keys_phi, ids_column[block, :], ids_row[index]
        )
        flat = (GROUP * QUERY_ROWS, KEY_ROWS)
        grad_weights = dot(spread_grad, value[keys, :], CONTRACT_LAST)
        grad_value[keys, :] += dot(
            weights.reshape(flat).astype(BF16), spread_grad, CONTRACT_FIRST
        )
        grad_weights = grad_weights.reshape(weights.shape)
        inner = jnp.sum(grad_weights * weights, axis=-1, keepdims=True)
        grad_scores = ((grad_weights - inner) * inverse * same[None]).astype(BF16).reshape(flat)
        found = dot(grad_scores, keys_phi)
        grad_phi_q[block, :] = gather_heads(found.reshape(GROUP, QUERY_ROWS, -1))
        grad_phi_k[keys, :] += dot(grad_scores, spread_q, CONTRACT_FIRST)

    each_block(rows // QUERY_ROWS, QUERY_ROWS, step)

    def through_map(grad_phi, phi, held):
        high, low = two_parts(grad_phi[...] * phi[...])
        along = dot(high, table[0], CONTRACT_LAST) + dot(low, table[0], CONTRACT_LAST)
        summed = dot(high, ones[...], CONTRACT_LAST) + dot(low, ones[...], CONTRACT_LAST)
        grad_rows = (along - held[...] * summed) * scale
        turned = grad_rows * cosine[...] + swap_halves(grad_rows * sine[...], half)
        return turned.astype(BF16)

    for part in range(3):
        if part == 0:
            gradient = through_map(grad_phi_q, phi_q, query)
        elif part == 1:
            gradient = through_map(grad_phi_k, phi_k, key)
        else:
            gradient = grad_value[...].astype(BF16)
        grad_mixed[...] = gradient
        found = dot(normed_a[own, :], grad_mixed[own, :], CONTRACT_FIRST)
        grad_weight[:, part_of(part)] = found.astype(BF16)
        weight = (weight_q, weight_k, weight_v)[part]
        total[...] += dot(grad_mixed[...], weight[...], CONTRACT_LAST)

    def copies():
        count = leaving.shape[0]
        size = width // count
        for index in range(count):
            place = pl.ds(pl.multiple_of(places[index], 16), size)
            target = grad_far if index < count // 2 else grad_near
            to = pl.ds(index % (count // 2) * size, size)
            yield pltpu.make_async_copy(grad_weight.at[place, :], target.at[to, :], leaving.at[index])

    @pl.when(group == pl.num_programs(0) - 1)
    def _():
        for copy in copies():
            copy.start()
        grad_gain[...] = jnp.zeros_like(grad_gain)

        def step(block, index):
            hat, inverse = normalised(state[block, :])
            back = norm_back(total[block, :], gain_1[...], hat, inverse)
            grad_state[block, :] = grad_middle[block, :] + back

            @pl.when((index > 0) & (index < rows // 64 - 1))
            def _():
                grad_gain[...] += jnp.sum(total[block, :] * hat, axis=0, keepdims=True)

        each_block(rows // 64, 64, step)
        for copy in copies():
            copy.wait()


def arriving(pieces, held, arrived, step, chunk):
    begin = 0
    begins = []
    for piece in pieces:
        begins.append(begin)
        begin += piece.shape[0]

    def copy(index):
        place = pl.ds(begins[index], pieces[index].shape[0])
        return pltpu.make_async_copy(pieces[index], held.at[place, :], arrived.at[index])

    @pl.when(step == 0)
    def _():
        for index in range(len(pieces)):
            copy(index).start()

    for at in range(held.shape[0] // chunk):
        fresh = [
            index
            for index in range(len(pieces))
            if at * chunk <= begins[index] < (at + 1) * chunk
        ]
        if fresh:

            @pl.when(step == at)
            def _(fresh=fresh):
                for index in fresh:
                    copy(index).wait()


def feed_forward(chunk, piece_count, carried, normed_c, *others):
    pieces = others[:piece_count]
    activated, slope, state, held, total, hidden, arrived = others[piece_count:]
    step_at = pl.program_id(0)
    rows, width = carried.shape
    arriving(pieces, held, arrived, step_at, chunk)
    place = pl.ds(pl.multiple_of(step_at * chunk, chunk), chunk)

    @pl.when(step_at == 0)
    def _():
        total[...] = carried[...]

    hidden[...] = dot(normed_c[...], held[place, :width], CONTRACT_LAST)

    def step(block, index):
        value, back = gelu_and_slope(hidden[block, :])
        activated[block, :] = value.astype(BF16)
        slope[block, :] = back.astype(BF16)

    each_block(rows // 32, 32, step)
    total[...] += dot(activated[...], held[place, width:])

    @pl.when(step_at == pl.num_programs(0) - 1)
    def _():
        state[...] = total[...]


def feed_back(
    first,
    last,
    chunk,
    side_steps,
    piece_count,
    gradient,
    middle,
    gain_2,
    normed_c,
    side_activated,
    side_slope,
    corner_activated,
    corner_slope,
    *others,
):
    if not first:
        carried, *others = others
    pieces = others[:piece_count]
    grad_weight, grad_middle, *others = others[piece_count:]
    if last:
        grad_gain, *others = others
    held, total, branch, grad_hidden, grad_act, arrived = others
    step_at = pl.program_id(0)
    rows, width = middle.shape
    own = pl.ds(MOST, rows - 2 * MOST)
    arriving(pieces, held, arrived, step_at, chunk)
    place = pl.ds(pl.multiple_of(step_at * chunk, chunk), chunk)

    @pl.when(step_at == 0)
    def _():
        branch[...] = gradient[...].astype(BF16)
        total[...] = jnp.zeros_like(total) if first else carried[...]

    def work(activated, slope):
        grad_act[...] = dot(branch[...], held[place, width:], CONTRACT_LAST)

        def step(block, index):
            grad_hidden[block, :] = (grad_act[block, :] * slope[block, :].astype(F32)).astype(BF16)

        each_block(rows // 32, 32, step)
        grad_up = dot(grad_hidden[own, :], normed_c[own, :], CONTRACT_FIRST)
        grad_down = dot(activated[own, :], branch[own, :], CONTRACT_FIRST)
        grad_weight[:, :width] = grad_up.astype(BF16)
        grad_weight[:, width:] = grad_down.astype(BF16)
        total[...] += dot(grad_hidden[...], held[place, :width])

    @pl.when(step_at < side_steps)
    def _():
        work(side_activated, side_slope)

    @pl.when(step_at >= side_steps)
    def _():
        work(corner_activated, corner_slope)

    @pl.when(step_at == pl.num_programs(0) - 1)
    def _():
        if not last:
            grad_middle[...] = total[...]
            return
        grad_gain[...] = jnp.zeros_like(grad_gain)

        def step(block, index):
            hat, inverse = normalised(middle[block, :])
            back = norm_back(total[block, :], gain_2[...], hat, inverse)
            grad_middle[block, :] = gradient[block, :] + back

            @pl.when((index > 0) & (index < rows // 64 - 1))
            def _():
                grad_gain[...] += jnp.sum(total[block, :] * hat, axis=0, keepdims=True)

        each_block(rows // 64, 64, step)


def joining(parts, rows, source, joined):
    count, _, width = source.shape
    for part in range(parts):
        side = [source[at, part * rows : (part + 1) * rows, :] for at in range(count)]
        joined[:, part * count * width : (part + 1) * count * width] = jnp.concatenate(side, axis=1)


def tabulating(begin, source, tables):
    layers, groups, wide, small = tables.shape
    deep, feats = wide // GROUP, small // GROUP
    own_heads = groups * GROUP // source.shape[0]
    tables[...] = jnp.zeros_like(tables)
    for layer in range(layers):
        for index in range(groups * GROUP):
            group, place = index // GROUP, index % GROUP
            column = (layer * own_heads + index % own_heads) * feats
            tables[
                layer,
                group,
                place * deep : (place + 1) * deep,
                place * feats : (place + 1) * feats,
            ] = source[index // own_heads, begin : begin + deep, column : column + feats]


def parting(parts, *others):
    *sources, target = others
    count, rows, width = target.shape
    rows = rows // parts
    for part in range(parts):
        for at in range(count):
            begin = (part * count + at) * width
            total = sources[0][:, begin : begin + width].astype(F32)
            for source in sources[1:]:
                total = total + source[:, begin : begin + width].astype(F32)
            target[at, part * rows : (part + 1) * rows, :] = total.astype(target.dtype)


def adding_corner(near, far, to_x, to_y):
    half = to_x.shape[0]
    for target, place in ((to_x, slice(0, half)), (to_y, slice(half, 2 * half))):
        target[...] = (near[place, :].astype(F32) + far[place, :].astype(F32)).astype(BF16)


def adding_sides(near_x, far_x, near_y, far_y, from_x, from_y, to_x, to_y):
    half = from_x.shape[0]
    top, bottom = slice(0, half), slice(half, 2 * half)
    for near, far, place, more, target in (
        (near_x, far_x, top, None, to_x),
        (near_x, far_x, bottom, from_y, to_x),
        (near_y, far_y, top, from_x, to_y),
        (near_y, far_y, bottom, None, to_y),
    ):
        total = near[place, :].astype(F32) + far[place, :].astype(F32)
        if more is not None:
            total = total + more[...].astype(F32)
        target[place, :] = total.astype(BF16)


def whole(shape):
    return pl.BlockSpec(shape, lambda step, *_: (0,) * len(shape))


def columns(rows, width):
    return pl.BlockSpec((rows, width), lambda step, *_: (0, step))


def leading(shape):
    return pl.BlockSpec(shape, lambda step, *_: (step,) + (0,) * (len(shape) - 1))


def struct(shape, dtype):
    return jax.ShapeDtypeStruct(shape, dtype)


ANYWHERE = pl.BlockSpec(memory_space=pl.ANY)


def kernel_call(kernel, steps, in_specs, out_specs, out_shape, scratch, flops, prefetch=0):
    return pl.pallas_call(
        kernel,
        grid_spec=pltpu.PrefetchScalarGridSpec(
            num_scalar_prefetch=prefetch,
            grid=(steps,),
            in_specs=in_specs,
            out_specs=out_specs,
            scratch_shapes=scratch,
        ),
        out_shape=out_shape,
        compiler_params=pltpu.CompilerParams(vmem_limit_bytes=VMEM_BYTES),
        cost_estimate=pl.CostEstimate(flops=flops, bytes_accessed=flops // 600, transcendentals=0),
    )


def run_attention_forward(state, gains, pieces, places, table, ones, *, tables, ids, scale):
    rows, width = state.shape
    wide = table.shape[1]
    small = table.shape[2]
    blocks = rows // QUERY_ROWS
    return kernel_call(
        functools.partial(attention_forward, scale, len(pieces)),
        width // wide,
        [
            whole((rows, width)),
            whole((1, width)),
            whole((1, width)),
            leading((1, wide, small)),
            whole((wide, small)),
            whole((rows, wide)),
            whole((rows, wide)),
            whole((rows, 1)),
            whole((blocks, 1, KEY_ROWS)),
            *[ANYWHERE for _ in pieces],
        ],
        [
            whole((width, 4 * width)),
            whole((rows, width)),
            columns(rows, wide),
            columns(rows, wide),
            columns(rows, wide),
            columns(rows, wide),
            whole((rows, width)),
            whole((rows, width)),
        ],
        [
            struct((width, 4 * width), BF16),
            struct((rows, width), BF16),
            struct((rows, width), F32),
            struct((rows, width), F32),
            struct((rows, width), BF16),
            struct((rows, width), BF16),
            struct((rows, width), F32),
            struct((rows, width), BF16),
        ],
        [
            pltpu.VMEM((rows, width), F32),
            pltpu.VMEM((rows, small), BF16),
            pltpu.VMEM((rows, small), BF16),
            pltpu.SemaphoreType.DMA((len(pieces),)),
        ],
        FORWARD_COST,
        1,
    )(places, state, gains[0][None], gains[1][None], table, ones, *tables, *ids, *pieces)


def run_attention_backward(
    grad_middle, *, state, gain, weights, places, table, ones, tables, ids, kept, scale
):
    rows, width = state.shape
    wide = table.shape[1]
    small = table.shape[2]
    blocks = rows // QUERY_ROWS
    per_part = width // wide

    def weight_part(part):
        return pl.BlockSpec((width, wide), lambda step, _: (0, part * per_part + step))

    return kernel_call(
        functools.partial(attention_backward, scale),
        per_part,
        [
            whole((rows, width)),
            whole((rows, width)),
            whole((1, width)),
            *[weight_part(part) for part in range(4)],
            leading((1, wide, small)),
            whole((wide, small)),
            whole((rows, wide)),
            whole((rows, wide)),
            whole((rows, 1)),
            whole((blocks, 1, KEY_ROWS)),
            whole((rows, width)),
            columns(rows, wide),
            columns(rows, wide),
            columns(rows, wide),
            columns(rows, wide),
        ],
        [whole((rows, width)), whole((1, width)), ANYWHERE, ANYWHERE],
        [
            struct((rows, width), F32),
            struct((1, width), F32),
            struct((width // 2, 4 * width), BF16),
            struct((width // 2, 4 * width), BF16),
        ],
        [
            pltpu.VMEM((width, 4 * width), BF16),
            pltpu.SemaphoreType.DMA(places.shape),
            pltpu.VMEM((rows, width), F32),
            pltpu.VMEM((rows, width), BF16),
            pltpu.VMEM((rows, wide), BF16),
            pltpu.VMEM((rows, small), F32),
            pltpu.VMEM((rows, small), F32),
            pltpu.VMEM((rows, small), F32),
            pltpu.VMEM((rows, small), F32),
            pltpu.VMEM((rows, wide), F32),
        ],
        BACKWARD_COST,
        1,
    )(places, grad_middle, state, gain[None], *[weights] * 4, table, ones, *tables, *ids, *kept)


def run_feed_forward(carried, normed_c, pieces):
    rows, width = carried.shape
    count = sum(piece.shape[0] for piece in pieces)
    return kernel_call(
        functools.partial(feed_forward, CHUNK, len(pieces)),
        count // CHUNK,
        [whole((rows, width)), whole((rows, width)), *[ANYWHERE for _ in pieces]],
        [columns(rows, CHUNK), columns(rows, CHUNK), whole((rows, width))],
        [
            struct((rows, count), BF16),
            struct((rows, count), BF16),
            struct((rows, width), F32),
        ],
        [
            pltpu.VMEM((count, 2 * width), BF16),
            pltpu.VMEM((rows, width), F32),
            pltpu.VMEM((rows, CHUNK), F32),
            pltpu.SemaphoreType.DMA((len(pieces),)),
        ],
        FORWARD_COST // 3,
    )(carried, normed_c, *pieces)


def run_feed_back(gradient, middle, gain, normed_c, kept, pieces, side, carried):
    rows, width = middle.shape
    count = sum(piece.shape[0] for piece in pieces)
    chunk = CHUNK
    steps = count // chunk
    first, last = carried is None, carried is not None
    sides, corners = kept
    side_steps = sides[side][0].shape[1] // chunk
    corner_begin = side * (steps - side_steps)
    side_columns = pl.BlockSpec((rows, chunk), lambda step: (0, jnp.minimum(step, side_steps - 1)))
    corner_columns = pl.BlockSpec(
        (rows, chunk), lambda step: (0, corner_begin + jnp.maximum(step - side_steps, 0))
    )
    return kernel_call(
        functools.partial(feed_back, first, last, chunk, side_steps, len(pieces)),
        steps,
        [
            whole((rows, width)),
            whole((rows, width)),
            whole((1, width)),
            whole((rows, width)),
            side_columns,
            side_columns,
            corner_columns,
            corner_columns,
            *([] if first else [whole((rows, width))]),
            *[ANYWHERE for _ in pieces],
        ],
        [
            leading((chunk, 2 * width)),
            whole((rows, width)),
            *([whole((1, width))] if last else []),
        ],
        [
            struct((count, 2 * width), BF16),
            struct((rows, width), F32),
            *([struct((1, width), F32)] if last else []),
        ],
        [
            pltpu.VMEM((count, 2 * width), BF16),
            pltpu.VMEM((rows, width), F32),
            pltpu.VMEM((rows, width), BF16),
            pltpu.VMEM((rows, chunk), BF16),
            pltpu.VMEM((rows, chunk), F32),
            pltpu.SemaphoreType.DMA((len(pieces),)),
        ],
        FORWARD_COST // 2,
    )(
        gradient,
        middle,
        gain[None],
        normed_c,
        *sides[side],
        *corners,
        *([] if first else [carried]),
        *pieces,
    )


HEAD_DEVICES = 4
CHUNK = 384
X, Y, CORE = 2, 4, 1
FORWARD_COST = 29_000_000_000
BACKWARD_COST = 40_000_000_000


def hop(values, bit):
    count = lax.axis_size("dp")
    return lax.ppermute(values, "dp", [(i, i ^ bit) for i in range(count)])


def exchange(values):
    return lax.all_to_all(values, "head", split_axis=0, concat_axis=0, tiled=True)


def together(*values):
    return lax.optimization_barrier(values)


def by_permutes():
    return lax.axis_size("dp") == 8 and lax.axis_size("head") == HEAD_DEVICES


def join_columns(source, parts, rows):
    count, _, width = source.shape
    return kernel_call(
        functools.partial(joining, parts, rows),
        1,
        [whole(source.shape)],
        whole((rows, parts * count * width)),
        struct((rows, parts * count * width), BF16),
        [],
        1_000_000,
    )(source)


def feature_tables(source, begin, shape):
    return kernel_call(
        functools.partial(tabulating, begin),
        1,
        [whole(source.shape)],
        whole(shape),
        struct(shape, BF16),
        [],
        1_000_000,
    )(source)


def block_of(rows, columns_all, index):
    return pl.BlockSpec((rows, columns_all), lambda *_: (index, 0))


def part_columns(near, far, from_x, from_y, parts):
    rows, columns_all = from_x.shape
    shape = (HEAD_DEVICES, parts * rows, columns_all // parts // HEAD_DEVICES)
    return kernel_call(
        functools.partial(parting, parts),
        1,
        [block_of(rows, columns_all, 0) for _ in range(4)],
        whole(shape),
        struct(shape, BF16),
        [],
        1_000_000,
    )(near, far, from_x, from_y)


def next_chips(own):
    return hop(own, X), hop(own, Y), hop(own, CORE)


def halves_to_pass(over_x, over_y):
    half = over_x.shape[0] // 2
    return over_x[:half], over_y[half:]


def chip_across(passed):
    to_y, to_x = passed
    return hop(to_y, Y), hop(to_x, X)


def other_core(pieces):
    return tuple(hop(piece, CORE) for piece in pieces)


def piece_places(rows):
    own = lax.axis_index("dp")
    bits = [(0, 0), (X, 0), (Y, 0), (X | Y, 0), (X | Y, rows // 2)]
    return jnp.stack(
        [(own ^ (bit | core)) * rows + begin for core in (0, CORE) for bit, begin in bits]
    ).astype(jnp.int32)


def block_places(rows):
    own = lax.axis_index("dp")
    return jnp.stack(
        [(own ^ (bit | core)) * rows for core in (CORE, 0) for bit in (0, X, Y, X | Y)]
    ).astype(jnp.int32)


class Reduction:
    def __init__(self, far, near, parts):
        self.near, self.parts = near, parts
        self.rows, self.width = near.shape[0] // 4, near.shape[1]
        self.came = hop(far, CORE)

    def corner(self):
        self.far = self.came
        shape = (self.rows // 2, self.width)
        self.sent = kernel_call(
            adding_corner,
            1,
            [block_of(self.rows, self.width, 3)] * 2,
            [whole(shape)] * 2,
            [struct(shape, BF16)] * 2,
            [],
            1_000_000,
        )(self.near, self.far)

    def sides(self):
        half, shape = (self.rows // 2, self.width), (self.rows, self.width)
        self.sent = kernel_call(
            adding_sides,
            1,
            [block_of(self.rows, self.width, index) for index in (1, 1, 2, 2)] + [whole(half)] * 2,
            [whole(shape)] * 2,
            [struct(shape, BF16)] * 2,
            [],
            1_000_000,
        )(self.near, self.far, self.near, self.far, *self.came)

    def heads(self):
        self.sent = part_columns(self.near, self.far, *self.came, self.parts)

    def send(self):
        to_x, to_y = self.sent
        self.came = hop(to_x, X), hop(to_y, Y)

    def send_heads(self):
        self.came = exchange(self.sent)

    def result(self):
        total = jnp.sum(self.came.astype(F32), axis=0)
        return total.reshape(self.parts, -1, total.shape[1])


def summed_share(far, near, parts):
    joined = jnp.concatenate([near, far])
    joined = joined.reshape(joined.shape[0], parts, -1)
    part = lax.psum_scatter(joined, "dp", scatter_dimension=0, tiled=True)
    part = lax.psum_scatter(part, "head", scatter_dimension=2, tiled=True)
    return part.swapaxes(0, 1).astype(F32)


def sum_over_all(values):
    if not by_permutes():
        return lax.psum(values, ("dp", "head"))
    for bit in (CORE, X, Y):
        values = values + hop(values, bit)
    for bit in (1, 2):
        values = values + lax.ppermute(values, "head", [(i, i ^ bit) for i in range(HEAD_DEVICES)])
    return values


def with_halo(inputs, cotangent):
    count = lax.axis_size("head")
    both = jnp.concatenate([inputs, cotangent], axis=1)
    before = lax.ppermute(both[-MOST:], "head", [(i, i + 1) for i in range(count - 1)])
    after = lax.ppermute(both[:MOST], "head", [(i + 1, i) for i in range(count - 1)])
    joined = jnp.concatenate([before, both, after], axis=0).astype(F32)
    return joined[:, : inputs.shape[1]], joined[:, inputs.shape[1] :]


def window_ids(segment_ids, own_rows):
    padded = jnp.pad(segment_ids[0], (MOST, MOST), constant_values=-1)
    begin = lax.axis_index("head") * own_rows
    ids = lax.dynamic_slice(padded, (begin,), (own_rows + 2 * MOST,))
    place = jnp.arange(ids.shape[0])
    earlier = (ids[:, None] == ids[None, :]) & (place[None, :] < place[:, None])
    position = jnp.sum(earlier.astype(F32), axis=1)
    used = (ids >= ids[MOST]) & (ids <= ids[MOST + own_rows - 1])
    column = jnp.where(used, ids, -1)[:, None]
    row = jnp.where(used, ids, -2)
    starts = [
        min(max(b * QUERY_ROWS - MOST, 0), ids.shape[0] - KEY_ROWS)
        for b in range(ids.shape[0] // QUERY_ROWS)
    ]
    rows = jnp.stack([row[start : start + KEY_ROWS] for start in starts])[:, None, :]
    return position, (column, rows)


def rotary_tables(position, head_width):
    halves = head_width // 2
    frequency = jnp.exp(jnp.arange(halves, dtype=F32) * (-2.0 * math.log(10000.0) / head_width))
    angles = position[:, None] * frequency[None, :]
    cosine, sine = jnp.cos(angles), jnp.sin(angles)
    return (
        jnp.tile(jnp.concatenate([cosine, cosine], axis=1), (1, GROUP)),
        jnp.tile(jnp.concatenate([-sine, sine], axis=1), (1, GROUP)),
    )


def body(
    inputs,
    segment_ids,
    features,
    norm_gain,
    query_key_value,
    output_weight,
    up_weight,
    down_weight,
    cotangent,
):
    layer_count = norm_gain.shape[0]
    own_rows = inputs.shape[0]
    head_width = features.shape[3]
    feature_count = features.shape[2]
    scale = head_width ** (-0.25)
    own_place = slice(MOST, MOST + own_rows)

    state, gradient = with_halo(inputs, cotangent)
    position, ids = window_ids(segment_ids, own_rows)
    tables = rotary_tables(position, head_width)
    in_rows, part_width = output_weight.shape[1:]
    groups = state.shape[1] // (GROUP * head_width)
    table_shape = (layer_count, groups, GROUP * head_width, GROUP * feature_count)
    chunks = []
    for layer in range(layer_count):
        chunks.append((4, query_key_value[layer].reshape(-1, part_width), output_weight[layer]))
        chunks.append((2, up_weight[layer], down_weight[layer]))
    attend = functools.partial(
        run_attention_forward, tables=tables, ids=ids, scale=scale
    )
    ones = jnp.kron(
        jnp.eye(GROUP, dtype=BF16), jnp.ones((head_width, feature_count), BF16)
    )
    stored = []
    if by_permutes():
        attention_places = piece_places(in_rows)
        grad_places = block_places(in_rows)
        feature_rows = jnp.moveaxis(features, 3, 0).reshape(head_width, -1)

        def to_send(index):
            _, *weights = chunks[index]
            sent = jnp.concatenate(weights + [feature_rows] if index == 0 else weights)
            return jnp.broadcast_to(sent[None], (HEAD_DEVICES,) + sent.shape)

        def join(index, came):
            parts, *weights = chunks[index]
            return join_columns(came, parts, weights[-1].shape[0])

        came = exchange(to_send(0))
        own = join(0, came)
        blocks = feature_tables(came, 4 * in_rows, table_shape)
        own, sent = together(own, to_send(1))
        came = exchange(sent)
        over_x, over_y, over_core = next_chips(own)
        passed = halves_to_pass(over_x, over_y)
        across = chip_across(passed)
        own_feed = join(1, came)
        for layer in range(layer_count):
            more = layer + 1 < layer_count
            near = (own, over_x, over_y) + tuple(across)
            far = (over_core,) + other_core(near[1:])
            attention_pieces = near + far
            own = own_feed
            state, own = together(state, own)
            over_x, over_y, over_core = next_chips(own)
            weights, *kept, middle, normed_c = attend(
                state,
                norm_gain[layer],
                attention_pieces,
                attention_places,
                blocks[layer],
                ones,
            )

            middle, over_x, over_y, over_core = together(middle, over_x, over_y, over_core)
            sides = own, over_x, over_y
            passed = halves_to_pass(over_x, over_y)
            carried, passed, sent = together(middle, passed, to_send(2 * layer + 2) if more else ())
            across = chip_across(passed)
            far_sides = (over_core,) + other_core(sides[1:])
            came = exchange(sent) if more else ()
            near_kept = run_feed_forward(carried, normed_c, sides)

            carried, across, far_sides, came = together(near_kept[2], across, far_sides, came)
            far_across = other_core(across)
            if more:
                own = join(2 * layer + 2, came)
                carried, own, sent = together(carried, own, to_send(2 * layer + 3))
                over_x, over_y, over_core = next_chips(own)
                came = exchange(sent)
            near_pieces, last_pieces = sides + across, across + far_across
            far_pieces = far_sides + far_across
            far_kept = run_feed_forward(carried, normed_c, far_sides)

            carried = far_kept[2]
            if more:
                carried, over_x, over_y, over_core = together(carried, over_x, over_y, over_core)
                passed = halves_to_pass(over_x, over_y)
                carried, passed = together(carried, passed)
                across = chip_across(passed)
            last_kept = run_feed_forward(carried, normed_c, last_pieces)
            hidden_kept = (near_kept[:2], far_kept[:2]), last_kept[:2]
            stored.append(
                (state, weights, kept, middle, normed_c, hidden_kept, near_pieces, far_pieces)
            )
            state = last_kept[2]
            if more:
                state, across, came = together(state, across, came)
                own_feed = join(2 * layer + 3, came)
    else:
        all_features = lax.all_gather(features, "head", axis=1, tiled=True)
        shaped = all_features.reshape(layer_count, -1, GROUP, feature_count, head_width)
        blocks = jnp.einsum("lghmw,hk->lghwkm", shaped, jnp.eye(GROUP, dtype=BF16)).reshape(
            table_shape
        )
        owned = []
        for parts, *weights in chunks:
            rows = weights[-1].shape[0]
            joined = jnp.concatenate(weights).reshape(parts, rows, part_width)
            joined = lax.all_gather(joined, "head", axis=2, tiled=True)
            joined = lax.all_gather(joined, "dp", axis=1, tiled=True)
            owned.append(joined.swapaxes(0, 1).reshape(joined.shape[1], -1))
        middle_row = inputs.shape[1] // 2
        attention_places = jnp.array([0, middle_row], jnp.int32)
        grad_places = jnp.array([middle_row, 0], jnp.int32)
        for layer in range(layer_count):
            own_attention, own_feed = owned[2 * layer], owned[2 * layer + 1]
            weights, *kept, middle, normed_c = attend(
                state,
                norm_gain[layer],
                (own_attention[:middle_row], own_attention[middle_row:]),
                attention_places,
                blocks[layer],
                ones,
            )
            size = own_feed.shape[0] // 8
            near_pieces, far_pieces = (own_feed[: 4 * size],), (own_feed[4 * size :],)
            near_kept = run_feed_forward(middle, normed_c, (own_feed[: 3 * size],))
            far_kept = run_feed_forward(near_kept[2], normed_c, (own_feed[4 * size : 7 * size],))
            last = (own_feed[3 * size : 4 * size], own_feed[7 * size :])
            last_kept = run_feed_forward(far_kept[2], normed_c, last)
            hidden_kept = (near_kept[:2], far_kept[:2]), last_kept[:2]
            stored.append(
                (state, weights, kept, middle, normed_c, hidden_kept, near_pieces, far_pieces)
            )
            state = last_kept[2]
    outputs = state[own_place].astype(BF16)

    gains = [None] * layer_count
    sums = [None] * layer_count
    for layer in reversed(range(layer_count)):
        before, weights, kept, middle, normed_c, hidden_kept, near_pieces, far_pieces = stored[layer]
        feed = (middle, norm_gain[layer, 1], normed_c, hidden_kept)
        attention_back = functools.partial(
            run_attention_backward,
            state=before,
            gain=norm_gain[layer, 0],
            weights=weights,
            places=grad_places,
            table=blocks[layer],
            ones=ones,
            tables=tables,
            ids=ids,
            kept=kept,
            scale=scale,
        )
        if not by_permutes():
            feed_far, carried = run_feed_back(gradient, *feed, far_pieces, 1, None)
            feed_near, grad_middle, gain_c = run_feed_back(gradient, *feed, near_pieces, 0, carried)
            gradient, gain_a, far, near = attention_back(grad_middle)
            gains[layer] = jnp.concatenate([gain_a, gain_c])
            sums[layer] = summed_share(feed_far, feed_near, 2), summed_share(far, near, 4)
            continue
        later = sums[layer + 1] if layer + 1 < layer_count else None
        if later:
            later_feed, later_attention = later
            later_feed.sides()
            gradient, later_feed.sent = together(gradient, later_feed.sent)
            later_feed.send()
        feed_far, carried = run_feed_back(gradient, *feed, far_pieces, 1, None)

        feed_came = None
        if later:
            carried, feed_far, later_attention.came = together(carried, feed_far, later_attention.came)
            later_attention.corner()
            carried, later_attention.sent = together(carried, later_attention.sent)
            later_attention.send()
        far_hop = hop(feed_far, CORE)
        feed_near, grad_middle, gain_c = run_feed_back(gradient, *feed, near_pieces, 0, carried)

        feed_sum = Reduction(feed_far, feed_near, 2)
        grad_middle, feed_near, feed_sum.came = together(grad_middle, feed_near, far_hop)
        feed_sum.near = feed_near
        feed_sum.corner()
        grad_middle, feed_sum.sent = together(grad_middle, feed_sum.sent)
        if later:
            grad_middle, later_attention.came, later_feed.came = together(
                grad_middle, later_attention.came, later_feed.came
            )
            later_attention.sides()
            later_feed.heads()
            grad_middle, later_attention.sent, later_feed.sent = together(
                grad_middle, later_attention.sent, later_feed.sent
            )
            later_attention.send()
            later_feed.send_heads()
        feed_sum.send()
        gradient, gain_a, far, near = attention_back(grad_middle)

        gains[layer] = jnp.concatenate([gain_a, gain_c])
        gradient, far, near, gains[layer], feed_sum.came = together(
            gradient, far, near, gains[layer], feed_sum.came
        )
        if later:
            gradient, far, near, later_attention.came, later_feed.came = together(
                gradient, far, near, later_attention.came, later_feed.came
            )
            later_attention.heads()
        sums[layer] = feed_sum, Reduction(far, near, 4)
    if by_permutes():
        feed_sum, attention_sum = sums[0]
        feed_sum.sides()
        feed_sum.send()
        gain_all, attention_sum.came, feed_sent = together(
            jnp.stack(gains), attention_sum.came, feed_sum.sent
        )
        attention_sum.corner()
        attention_sum.send()
        for layer in range(1, layer_count):
            later_attention = sums[layer][1]
            later_attention.sent, attention_sent = together(
                later_attention.sent, attention_sum.sent
            )
            later_attention.send_heads()
        gain_all, attention_sum.came = together(gain_all, attention_sum.came)
        attention_sum.sides()
        attention_sum.send()
        feed_sum.came, attention_sent = together(feed_sum.came, attention_sum.sent)
        feed_sum.heads()
        feed_sum.send_heads()
        gain_all, attention_sum.came, feed_sent = together(
            gain_all, attention_sum.came, feed_sum.sent
        )
        attention_sum.heads()
        attention_sum.send_heads()
        gain_total = sum_over_all(gain_all)
        sums = [(feed_sum.result(), attention_sum.result()) for feed_sum, attention_sum in sums]
    else:
        gain_total = sum_over_all(jnp.stack(gains))
    results = [
        (attention_share[:3], attention_share[3], feed_share[0], feed_share[1])
        for feed_share, attention_share in sums
    ]
    return (
        outputs,
        gradient[own_place],
        gain_total[:, 0],
        gain_total[:, 1],
        *(jnp.stack(list(kind)) for kind in zip(*results)),
    )


def solution(mesh):
    in_specs = (
        P(("dp", "head"), None),
        P("dp", None),
        P(None, "head", None, None),
        P(),
        P(None, None, "dp", "head"),
        P(None, "dp", "head"),
        P(None, "dp", "head"),
        P(None, "dp", "head"),
        P(("dp", "head"), None),
    )
    out_specs = (
        P(("dp", "head"), None),
        P(("dp", "head"), None),
        P(),
        P(),
        P(None, None, "dp", "head"),
        P(None, "dp", "head"),
        P(None, "dp", "head"),
        P(None, "dp", "head"),
    )
    return jax.shard_map(body, mesh=mesh, in_specs=in_specs, out_specs=out_specs, check_vma=False)
```

```python
import functools
import math

import jax
import jax.numpy as jnp
from jax import lax
from jax.experimental import pallas as pl
from jax.experimental.pallas import tpu as pltpu
from jax.sharding import PartitionSpec as P

MOST = 64
EPSILON = 1e-05
QUERY_ROWS = 128
KEY_ROWS = QUERY_ROWS + 2 * MOST
GROUP = 4
VMEM_BYTES = 60 * 2**20

BF16 = jnp.bfloat16
F32 = jnp.float32
CONTRACT_LAST = (((1,), (1,)), ((), ()))
CONTRACT_FIRST = (((0,), (0,)), ((), ()))
CONTRACT_MIDDLE = (((1,), (0,)), ((), ()))

TAIL_SCALE = 0.3275911 / math.sqrt(2.0)
TAIL_TERMS = (1.061405429, -1.453152027, 1.421413741, -0.284496736, 0.254829592)


def dot(left, right, dims=CONTRACT_MIDDLE):
    return lax.dot_general(left, right, dims, preferred_element_type=F32)


def gelu_and_slope(hidden):
    bell = jnp.exp(hidden * hidden * -0.5)
    below = 1.0 + jnp.abs(hidden) * TAIL_SCALE
    guess = pl.reciprocal(below, approx=True)
    inverse = guess * (2.0 - below * guess)
    tail = 0.5 * TAIL_TERMS[0]
    for term in TAIL_TERMS[1:]:
        tail = tail * inverse + 0.5 * term
    tail = tail * inverse * bell
    cumulative = jnp.where(hidden > 0.0, 1.0 - tail, tail)
    return hidden * cumulative, cumulative + hidden * (bell * (1.0 / math.sqrt(2.0 * math.pi)))


def normalised(values):
    centred = values - jnp.mean(values, axis=-1, keepdims=True)
    inverse = lax.rsqrt(jnp.mean(centred * centred, axis=-1, keepdims=True) + EPSILON)
    return centred * inverse, inverse


def norm_back(grad_out, gain, hat, inverse):
    scaled = grad_out * gain
    first_mean = jnp.mean(scaled, axis=-1, keepdims=True)
    second_mean = jnp.mean(scaled * hat, axis=-1, keepdims=True)
    return inverse * (scaled - first_mean - hat * second_mean)


def each_block(rows, size, step):
    for block in row_blocks(rows, size):
        step(block)


def own_block(block, rows):
    return MOST <= block.start and block.stop <= rows - MOST


def swap_halves(values, half):
    width = values.shape[-1]
    lane = lax.broadcasted_iota(jnp.int32, values.shape, len(values.shape) - 1)
    ahead = pltpu.roll(values, width - half, 1)
    behind = pltpu.roll(values, half, 1)
    return jnp.where(lane % (2 * half) < half, ahead, behind)


def two_parts(values):
    high = values.astype(BF16)
    return high, (values - high.astype(F32)).astype(BF16)


def row_blocks(rows, size):
    return [slice(begin, begin + size) for begin in range(0, rows, size)]


def spread_parts(rows, target, place):
    width = rows.shape[1]
    for index, part in enumerate((*two_parts(rows), *two_parts(rows * rows))):
        target[place, index * width : (index + 1) * width] = part


def phi_of(parts, table):
    return jnp.exp(dot(parts, table)) * (1.0 / math.sqrt(table.shape[1] // GROUP))


def head_masks(width, dtype):
    lane = lax.broadcasted_iota(jnp.int32, (1, width), 1) // (width // GROUP)
    return [jnp.where(lane == head, 1.0, 0.0).astype(dtype) for head in range(GROUP)]


def spread_heads(values):
    return jnp.concatenate([values * mask for mask in head_masks(values.shape[1], BF16)], axis=0)


def gather_heads(values):
    masks = head_masks(values.shape[-1], F32)
    total = values[0] * masks[0]
    for head in range(1, GROUP):
        total = total + values[head] * masks[head]
    return total


def block_scores(phi_q, phi_k, ids_column, ids_row):
    scores = dot(phi_q, phi_k, CONTRACT_LAST)
    same = (ids_column == ids_row).astype(F32)
    scores = scores.reshape(GROUP, QUERY_ROWS, KEY_ROWS) * same[None]
    totals = jnp.sum(scores, axis=-1, keepdims=True)
    inverse = jnp.where(totals > 0.0, 1.0 / totals, 0.0)
    return scores * inverse, inverse, same


def query_blocks(rows):
    for index, block in enumerate(row_blocks(rows, QUERY_ROWS)):
        begin = min(max(block.start - MOST, 0), rows - KEY_ROWS)
        yield index, block, slice(begin, begin + KEY_ROWS)


def attention_forward(
    scale,
    piece_count,
    places,
    state,
    gain_1,
    gain_2,
    table,
    cosine,
    sine,
    ids_column,
    ids_row,
    *others,
):
    pieces = others[:piece_count]
    weights_out, normed_a, query, key, value, mixed, middle, normed_c, *others = others[piece_count:]
    weights, total, projected, parts, phi, arrived, leaving = others
    group = pl.program_id(0)
    groups = weights.shape[0]
    rows = state.shape[0]
    wide = query.shape[1]
    deep = weights.shape[2]
    half = cosine.shape[1] // GROUP // 2

    def columns_of(at):
        return pl.ds(at * deep, deep)

    def arriving_at(at):
        for index, piece in enumerate(pieces):
            place = pl.ds(pl.multiple_of(places[index], 16), piece.shape[0])
            yield pltpu.make_async_copy(
                piece.at[:, columns_of(at)], weights.at[at, place, :], arrived.at[at, index]
            )

    def leaving_at(at):
        return pltpu.make_async_copy(
            weights.at[at], weights_out.at[:, columns_of(at)], leaving.at[at]
        )

    @pl.when(group == 0)
    def _():
        for at in range(groups):
            for copy in arriving_at(at):
                copy.start()

        def step(block):
            hat, _ = normalised(state[block, :])
            normed_a[block, :] = (hat * gain_1[...]).astype(BF16)
            total[block, :] = state[block, :]

        each_block(rows, 64, step)

    for at in range(groups):

        @pl.when(group == at)
        def _(at=at):
            for copy in arriving_at(at):
                copy.wait()
            leaving_at(at).start()

    projected[...] = dot(normed_a[...], weights[group, :, : 3 * wide])
    for block in row_blocks(rows, 64):
        for part, held in enumerate((query, key)):
            values = projected[block, part * wide : (part + 1) * wide]
            turned = values * cosine[block, :] + swap_halves(values, half) * sine[block, :]
            turned = turned * scale
            held[block, :] = turned
            spread_parts(turned, parts, slice(part * rows + block.start, part * rows + block.stop))
        value[block, :] = projected[block, 2 * wide :].astype(BF16)
    phi[...] = phi_of(parts[...], table[0]).astype(BF16)

    for index, block, keys in query_blocks(rows):
        scores, _, _ = block_scores(
            spread_heads(phi[block, :]),
            phi[rows + keys.start : rows + keys.stop, :],
            ids_column[block, :],
            ids_row[index],
        )
        scores = scores.reshape(GROUP * QUERY_ROWS, KEY_ROWS).astype(BF16)
        found = dot(scores, value[keys, :])
        mixed[block, :] = gather_heads(found.reshape(GROUP, QUERY_ROWS, -1)).astype(BF16)

    total[...] += dot(mixed[...], weights[group, :, 3 * wide :], CONTRACT_LAST)

    @pl.when(group == groups - 1)
    def _():
        def step(block):
            middle[block, :] = total[block, :]
            hat, _ = normalised(total[block, :])
            normed_c[block, :] = (hat * gain_2[...]).astype(BF16)

        each_block(rows, 64, step)
        for at in range(groups):
            leaving_at(at).wait()


class Arrivals:
    def __init__(self, semaphores):
        self.semaphores, self.copies = semaphores, []

    def start(self, source, target):
        copy = pltpu.make_async_copy(source, target, self.semaphores.at[len(self.copies)])
        copy.start()
        self.copies.append(copy)
        return copy


def attention_backward(first, last, scale, groups, split, places, branch_in, weights_in, mixed_in, query_in, key_in, value_in, *others):
    normed_in, cosine_in, sine_in, *others = others
    if not first:
        total_in, *others = others
    if last:
        grad_middle, state, gain_1, *others = others
    table, back_table, ids_column, ids_row, *others = others
    if last:
        grad_state, grad_gain, *others = others
    else:
        total_out, *others = others
    grad_targets, others = others[: 1 + split], others[1 + split :]
    (
        branch,
        weights,
        mixed,
        query,
        key,
        value,
        normed_a,
        cosine,
        sine,
        total,
        grad_weight,
        grad_mixed,
        parts,
        phi,
        grad_phi,
        grad_value,
        grad_parts,
        grad_projected,
        arrived,
        leaving,
    ) = others
    _, rows, wide = query.shape
    half = wide // GROUP // 2
    own_rows = rows - 2 * MOST
    own = pl.ds(MOST, own_rows)
    small = phi.shape[1]
    deep = weights.shape[2]
    arrivals = Arrivals(arrived)
    got_branch = arrivals.start(branch_in, branch)
    got = []
    for at, group in enumerate(groups):
        columns_in = pl.ds(group * wide, wide)
        got.append(
            (
                arrivals.start(
                    weights_in.at[:, pl.ds(group * deep + 3 * wide, wide)],
                    weights.at[at, :, pl.ds(3 * wide, wide)],
                ),
                arrivals.start(query_in.at[:, columns_in], query.at[at]),
                arrivals.start(key_in.at[:, columns_in], key.at[at]),
                arrivals.start(mixed_in.at[own, columns_in], mixed.at[at]),
                arrivals.start(value_in.at[:, columns_in], value.at[at]),
                arrivals.start(
                    weights_in.at[:, pl.ds(group * deep, 3 * wide)],
                    weights.at[at, :, pl.ds(0, 3 * wide)],
                ),
            )
        )
        if at == 0:
            got_shared = [
                arrivals.start(cosine_in, cosine),
                arrivals.start(sine_in, sine),
                arrivals.start(normed_in.at[own, :], normed_a),
            ]
    if not first:
        got_total = arrivals.start(total_in, total)
    got_branch.wait()
    count = leaving.shape[1]
    size = grad_weight.shape[1] // count
    copies = []
    for at in range(len(groups)):
        got_last, *got_rows, got_first = got[at]
        got_last.wait()
        for copy in got_rows:
            copy.wait()
        grad_mixed[...] = dot(branch[...], weights[at, :, 3 * wide :]).astype(BF16)
        for block in row_blocks(rows, 64):
            for part, held in enumerate((query, key)):
                place = slice(part * rows + block.start, part * rows + block.stop)
                spread_parts(held[at, block, :], parts, place)
        phi[...] = phi_of(parts[...], table[at])
        grad_phi[rows:, :] = jnp.zeros((rows, small), F32)
        grad_value[...] = jnp.zeros_like(grad_value)
        found = dot(branch[own, :], mixed[at], CONTRACT_FIRST)
        grad_weight[at, :, 3 * wide :] = found.astype(BF16)

        for index, block, keys in query_blocks(rows):
            far_keys = slice(rows + keys.start, rows + keys.stop)
            spread_q = spread_heads(phi[block, :].astype(BF16))
            spread_grad = spread_heads(grad_mixed[block, :])
            keys_phi = phi[far_keys, :].astype(BF16)
            scores, inverse, same = block_scores(
                spread_q, keys_phi, ids_column[block, :], ids_row[index]
            )
            flat = (GROUP * QUERY_ROWS, KEY_ROWS)
            grad_scores = dot(spread_grad, value[at, keys, :], CONTRACT_LAST)
            grad_value[keys, :] += dot(
                scores.reshape(flat).astype(BF16), spread_grad, CONTRACT_FIRST
            )
            grad_scores = grad_scores.reshape(scores.shape)
            inner = jnp.sum(grad_scores * scores, axis=-1, keepdims=True)
            grad_scores = ((grad_scores - inner) * inverse * same[None]).astype(BF16).reshape(flat)
            found = dot(grad_scores, keys_phi)
            grad_phi[block, :] = gather_heads(found.reshape(GROUP, QUERY_ROWS, -1))
            grad_phi[far_keys, :] += dot(grad_scores, spread_q, CONTRACT_FIRST)

        if at == 0:
            for copy in got_shared:
                copy.wait()
        got_first.wait()
        for block in row_blocks(2 * rows, 128):
            high, low = two_parts(grad_phi[block, :] * phi[block, :])
            grad_parts[block, :small] = high
            grad_parts[block, small:] = low
        for part, held in enumerate((query, key)):
            for block in row_blocks(rows, 128):
                there = slice(part * rows + block.start, part * rows + block.stop)
                both = dot(grad_parts[there, :], back_table[at], CONTRACT_LAST)
                grad_rows = (both[:, :wide] - held[at, block, :] * both[:, wide:]) * scale
                turned = grad_rows * cosine[block, :]
                turned = turned + swap_halves(grad_rows * sine[block, :], half)
                grad_projected[block, part * wide : (part + 1) * wide] = turned.astype(BF16)
        grad_projected[:, 2 * wide :] = grad_value[...].astype(BF16)
        found = dot(normed_a[...], grad_projected[own, :], CONTRACT_FIRST)
        grad_weight[at, :, : 3 * wide] = found.astype(BF16)
        for index in range(count):
            place = pl.ds(pl.multiple_of(places[index], 16), size) if split else pl.ds(0, size)
            each = count // len(grad_targets)
            target = grad_targets[index // each]
            to = pl.ds(index % each * size, size)
            copies.append(
                pltpu.make_async_copy(
                    grad_weight.at[at, place, :],
                    target.at[to, pl.ds(at * deep, deep)],
                    leaving.at[at, index],
                )
            )
            copies[-1].start()
        back = dot(grad_projected[...], weights[at, :, : 3 * wide], CONTRACT_LAST)
        ending = at == len(groups) - 1
        if at == 0 and not first:
            got_total.wait()
        if at > 0 or not first:
            back = total[...] + back
        if ending and not last:
            total_out[...] = back
        else:
            total[...] = back
    if last:
        grad_gain[...] = jnp.zeros_like(grad_gain)

        def step(block):
            hat, inverse = normalised(state[block, :])
            back = norm_back(total[block, :], gain_1[...], hat, inverse)
            grad_state[block, :] = grad_middle[block, :] + back
            if own_block(block, rows):
                grad_gain[...] += jnp.sum(total[block, :] * hat, axis=0, keepdims=True)

        each_block(rows, 64, step)
    for copy in copies:
        copy.wait()


def begins_of(pieces):
    begins = [0]
    for piece in pieces:
        begins.append(begins[-1] + piece.shape[0])
    return begins


def hidden_chunks(count):
    return [slice(begin, min(begin + CHUNK, count)) for begin in range(0, count, CHUNK)]


def feed_forward(piece_count, carried_in, normed_in, *others):
    pieces = others[:piece_count]
    activated_out, slope_out, state_out, *others = others[piece_count:]
    held, carried, normed_c, hidden, activated, slope, arrived, leaving = others
    rows, width = carried.shape
    count = held.shape[0]
    begins = begins_of(pieces)
    copies = [
        pltpu.make_async_copy(
            piece, held.at[pl.ds(begins[index], piece.shape[0]), :], arrived.at[index]
        )
        for index, piece in enumerate(pieces)
    ]
    norm_copy = pltpu.make_async_copy(normed_in, normed_c, arrived.at[piece_count])
    carried_copy = pltpu.make_async_copy(carried_in, carried, arrived.at[piece_count + 1])
    norm_copy.start()
    for copy in copies:
        copy.start()
    carried_copy.start()
    norm_copy.wait()
    chunks = hidden_chunks(count)
    waited = 0
    outgoing = []

    def project(chunk):
        hidden[:, chunk] = dot(normed_c[...], held[chunk, :width], CONTRACT_LAST)

    def wait_until(row):
        nonlocal waited
        while waited < piece_count and begins[waited] < row:
            copies[waited].wait()
            waited += 1

    wait_until(chunks[0].stop)
    project(chunks[0])
    wait_until(count)
    for index, chunk in enumerate(chunks):
        if index + 1 < len(chunks):
            project(chunks[index + 1])
        for block in row_blocks(rows, 32):
            value, back = gelu_and_slope(hidden[block, chunk])
            activated[block, chunk] = value.astype(BF16)
            slope[block, chunk] = back.astype(BF16)
        for target, source in ((activated_out, activated), (slope_out, slope)):
            outgoing.append(
                pltpu.make_async_copy(
                    source.at[:, chunk], target.at[:, chunk], leaving.at[len(outgoing)]
                )
            )
            outgoing[-1].start()
    carried_copy.wait()
    carried[...] += dot(activated[...], held[:, width:])
    outgoing.append(pltpu.make_async_copy(carried, state_out, leaving.at[len(outgoing)]))
    outgoing[-1].start()
    for copy in outgoing:
        copy.wait()


def feed_back(first, last, segments, piece_count, places, gradient_in, middle, gain_2, normed_in, *others):
    kept, others = others[: 2 * len(segments)], others[2 * len(segments) :]
    if not first:
        total_in, *others = others
    pieces = others[:piece_count]
    grad_out, grad_middle, *others = others[piece_count:]
    if last:
        grad_gain, grad_attn, *others = others
    (
        held,
        gradient,
        normed_c,
        activated,
        slope,
        total,
        branch,
        grad_hidden,
        grad_weight,
        arrived,
        leaving,
    ) = others
    rows, width = gradient.shape
    own_rows = rows - 2 * MOST
    own = pl.ds(MOST, own_rows)
    count = held.shape[0]
    begins = begins_of(pieces)
    arrivals = Arrivals(arrived)
    left, right = pl.ds(0, width), pl.ds(width, width)

    def weight_half(half):
        return [
            arrivals.start(
                piece.at[:, half], held.at[pl.ds(begins[index], piece.shape[0]), half]
            )
            for index, piece in enumerate(pieces)
        ]

    def leave(half, offset):
        copies = []
        for index, piece in enumerate(pieces):
            size = piece.shape[0]
            copies.append(
                pltpu.make_async_copy(
                    grad_weight.at[pl.ds(begins[index], size), half],
                    grad_out.at[pl.ds(pl.multiple_of(places[index], 16), size), half],
                    leaving.at[offset + index],
                )
            )
            copies[-1].start()
        return copies

    got_gradient = arrivals.start(gradient_in, gradient)
    got_down = weight_half(right)
    got_act, got_slope, begin = [], [], 0
    for index, (column, size) in enumerate(segments):
        place = pl.ds(begin, size)
        act, back = kept[2 * index : 2 * index + 2]
        source = pl.ds(column, size)
        got_act.append(arrivals.start(act.at[own, source], activated.at[:, place]))
        got_slope.append(arrivals.start(back.at[:, source], slope.at[:, place]))
        begin += size
    got_norm = arrivals.start(normed_in.at[own, :], normed_c)
    got_up = weight_half(left)
    if not first:
        got_total = arrivals.start(total_in, total)
    got_gradient.wait()
    for block in row_blocks(rows, 64):
        branch[block, :] = gradient[block, :].astype(BF16)
    for copy in got_down + got_act:
        copy.wait()
    for chunk in row_blocks(count, count // 2):
        found = dot(activated[:, chunk], branch[own, :], CONTRACT_FIRST)
        grad_weight[chunk, width:] = found.astype(BF16)
    down_leaves = leave(right, 0)
    for copy in got_slope + [got_norm] + got_up:
        copy.wait()
    for chunk in hidden_chunks(count):
        grad_act = dot(branch[...], held[chunk, width:], CONTRACT_LAST)
        grad_hidden[:, chunk] = (grad_act * slope[:, chunk].astype(F32)).astype(BF16)
    for chunk in row_blocks(count, count // 2):
        found = dot(grad_hidden[MOST : MOST + own_rows, chunk], normed_c[...], CONTRACT_FIRST)
        grad_weight[chunk, :width] = found.astype(BF16)
    up_leaves = leave(left, piece_count)
    back = dot(grad_hidden[...], held[:, :width])
    if not first:
        got_total.wait()
        back = total[...] + back
    if not last:
        grad_middle[...] = back
    else:
        total[...] = back
        grad_gain[...] = jnp.zeros_like(grad_gain)

        def step(block):
            hat, inverse = normalised(middle[block, :])
            back = gradient[block, :] + norm_back(total[block, :], gain_2[...], hat, inverse)
            grad_middle[block, :] = back
            grad_attn[block, :] = back.astype(BF16)
            if own_block(block, rows):
                grad_gain[...] += jnp.sum(total[block, :] * hat, axis=0, keepdims=True)

        each_block(rows, 64, step)
    for copy in down_leaves + up_leaves:
        copy.wait()


def column_runs(parts, part, begin, width, group_width):
    stop = begin + width
    while begin < stop:
        group = begin // group_width
        end = min(stop, (group + 1) * group_width)
        place = group * parts * group_width + part * group_width + begin % group_width
        yield begin, end, place
        begin = end


def joining(parts, begin, group_width, source, joined):
    rows = joined.shape[0]
    count = source.shape[0]
    width = joined.shape[1] // parts // count
    across = source.shape[2] // width
    for part in range(parts):
        top = begin + part // across * rows
        left = part % across * width
        side = [source[at, top : top + rows, left : left + width] for at in range(count)]
        side = jnp.concatenate(side, axis=1)
        for first, end, place in column_runs(parts, part, 0, count * width, group_width):
            joined[:, place : place + end - first] = side[:, first:end]


def tabulating(begin, source, *others):
    layers = len(others) // 2
    groups, _, small = others[0].shape
    feats = small // GROUP
    own_heads = groups * GROUP // source.shape[0]
    wide = others[layers].shape[1] // 2
    deep = wide // GROUP
    thin = source.shape[1] - begin
    runs = deep // thin
    run_width = layers * own_heads * feats
    for target in others:
        target[...] = jnp.zeros_like(target)
    for layer in range(layers):
        tables, back_tables = others[layer], others[layers + layer]
        for index in range(groups * GROUP):
            group, place = index // GROUP, index % GROUP
            column = (layer * own_heads + index % own_heads) * feats
            across = slice(place * feats, (place + 1) * feats)
            again = slice(small + place * feats, small + (place + 1) * feats)
            for part in range(4):
                for run in range(runs):
                    top = part * wide + place * deep + run * thin
                    down = slice(top, top + thin)
                    if part < 2:
                        at = run * run_width + column
                        value = source[index // own_heads, begin : begin + thin, at : at + feats]
                    else:
                        value = jnp.full((thin, feats), -0.5, BF16)
                    tables[group, down, across] = value
                    if part < 2:
                        value = value if part < 1 else jnp.ones((thin, feats), BF16)
                        back_tables[group, down, across] = value
                        back_tables[group, down, again] = value


def parting(parts, group_width, pieces, *others):
    *sources, target = others
    count, rows, all_width = target.shape
    width = all_width // parts
    each = len(sources) // pieces
    starts = [0]
    for piece in range(pieces - 1):
        starts.append(starts[-1] + sources[piece * each].shape[1])
    for part in range(parts):
        for at in range(count):
            runs = []
            for begin, end, place in column_runs(parts, part, at * width, width, group_width):
                piece = max(at for at in range(pieces) if starts[at] <= place)
                run = slice(place - starts[piece], place - starts[piece] + end - begin)
                mine = sources[piece * each : (piece + 1) * each]
                total = mine[0][:, run].astype(F32)
                for source in mine[1:]:
                    total = total + source[:, run].astype(F32)
                runs.append(total)
            total = runs[0] if len(runs) == 1 else jnp.concatenate(runs, axis=1)
            target[at, :, part * width : (part + 1) * width] = total.astype(target.dtype)


def finishing(parts, *others):
    sources, targets = others[: -len(parts)], others[-len(parts) :]
    for layer, source in enumerate(sources):
        begin = 0
        for target, count in zip(targets, parts):
            for part in range(count):
                width = target.shape[-1]
                run = slice(begin, begin + width)
                total = source[0, :, run].astype(F32)
                for at in range(1, source.shape[0]):
                    total = total + source[at, :, run].astype(F32)
                if count > 1:
                    target[layer, part] = total
                else:
                    target[layer] = total
                begin += width


def adding_corner(near, far, to_x, to_y):
    half = to_x.shape[0]
    for target, place in ((to_x, slice(0, half)), (to_y, slice(half, 2 * half))):
        target[...] = (near[place, :].astype(F32) + far[place, :].astype(F32)).astype(BF16)


def adding_sides(near_x, far_x, near_y, far_y, from_x, from_y, to_x, to_y):
    half = from_x.shape[0]
    top, bottom = slice(0, half), slice(half, 2 * half)
    for near, far, place, more, target in (
        (near_x, far_x, top, None, to_x),
        (near_x, far_x, bottom, from_y, to_x),
        (near_y, far_y, top, from_x, to_y),
        (near_y, far_y, bottom, None, to_y),
    ):
        total = near[place, :].astype(F32) + far[place, :].astype(F32)
        if more is not None:
            total = total + more[...].astype(F32)
        target[place, :] = total.astype(BF16)


def whole(shape):
    return pl.BlockSpec(
        shape, lambda step, *_: (0,) * len(shape), pipeline_mode=pl.Buffered(buffer_count=1)
    )


def columns(rows, width):
    return pl.BlockSpec((rows, width), lambda step, *_: (0, step))


def leading(shape):
    return pl.BlockSpec(shape, lambda step, *_: (step,) + (0,) * (len(shape) - 1))


def struct(shape, dtype):
    return jax.ShapeDtypeStruct(shape, dtype)


ANYWHERE = pl.BlockSpec(memory_space=pltpu.HBM)


def kernel_call(kernel, steps, in_specs, out_specs, out_shape, scratch, flops, prefetch=0):
    return pl.pallas_call(
        kernel,
        grid_spec=pltpu.PrefetchScalarGridSpec(
            num_scalar_prefetch=prefetch,
            grid=(steps,),
            in_specs=in_specs,
            out_specs=out_specs,
            scratch_shapes=scratch,
        ),
        out_shape=out_shape,
        compiler_params=pltpu.CompilerParams(vmem_limit_bytes=VMEM_BYTES),
        cost_estimate=pl.CostEstimate(flops=flops, bytes_accessed=flops // 600, transcendentals=0),
    )


def run_attention_forward(state, gains, pieces, places, table, *, tables, ids, scale):
    rows, width = state.shape
    wide = tables[0].shape[1]
    groups, deep, small = table.shape
    blocks = rows // QUERY_ROWS
    return kernel_call(
        functools.partial(attention_forward, scale, len(pieces)),
        groups,
        [
            whole((rows, width)),
            whole((1, width)),
            whole((1, width)),
            leading((1, deep, small)),
            whole((rows, wide)),
            whole((rows, wide)),
            whole((rows, 1)),
            whole((blocks, 1, KEY_ROWS)),
            *[ANYWHERE for _ in pieces],
        ],
        [
            ANYWHERE,
            whole((rows, width)),
            columns(rows, wide),
            columns(rows, wide),
            columns(rows, wide),
            columns(rows, wide),
            whole((rows, width)),
            whole((rows, width)),
        ],
        [
            struct((width, 4 * width), BF16),
            struct((rows, width), BF16),
            struct((rows, width), F32),
            struct((rows, width), F32),
            struct((rows, width), BF16),
            struct((rows, width), BF16),
            struct((rows, width), F32),
            struct((rows, width), BF16),
        ],
        [
            pltpu.VMEM((groups, width, 4 * wide), BF16),
            pltpu.VMEM((rows, width), F32),
            pltpu.VMEM((rows, 3 * wide), F32),
            pltpu.VMEM((2 * rows, deep), BF16),
            pltpu.VMEM((2 * rows, small), BF16),
            pltpu.SemaphoreType.DMA((groups, len(pieces))),
            pltpu.SemaphoreType.DMA((groups,)),
        ],
        FORWARD_COST,
        1,
    )(places, state, gains[0][None], gains[1][None], table, *tables, *ids, *pieces)


def run_attention_backward(
    groups,
    carried,
    *,
    grad_middle,
    branch,
    state,
    gain,
    weights,
    places,
    table,
    back_table,
    tables,
    ids,
    kept,
    scale,
):
    rows, width = state.shape
    wide = tables[0].shape[1]
    all_groups, deep, small = table.shape
    first, last = groups[0] == 0, groups[-1] == all_groups - 1
    count = len(groups)
    normed_a, query, key, value, mixed = kept
    own_rows = rows - 2 * MOST
    blocks = rows // QUERY_ROWS
    copied = [branch, weights, mixed, query, key, value, normed_a, *tables]
    ending = [grad_middle, state, gain[None]] if last else []
    split = places.shape[0] > 1
    halves = 1 + split
    return kernel_call(
        functools.partial(attention_backward, first, last, scale, groups, split),
        1,
        [
            *[ANYWHERE] * (len(copied) + (not first)),
            *([whole((rows, width)), whole((rows, width)), whole((1, width))] if last else []),
            whole((count, deep, small)),
            whole((count,) + back_table.shape[1:]),
            whole((rows, 1)),
            whole((blocks, 1, KEY_ROWS)),
        ],
        [
            *([whole((rows, width)), whole((1, width))] if last else [whole((rows, width))]),
            *[ANYWHERE] * halves,
        ],
        [
            struct((rows, width), F32),
            *([struct((1, width), F32)] if last else []),
            *[struct((width // halves, count * 4 * wide), BF16)] * halves,
        ],
        [
            pltpu.VMEM((rows, width), BF16),
            pltpu.VMEM((count, width, 4 * wide), BF16),
            pltpu.VMEM((count, own_rows, wide), BF16),
            pltpu.VMEM((count, rows, wide), F32),
            pltpu.VMEM((count, rows, wide), F32),
            pltpu.VMEM((count, rows, wide), BF16),
            pltpu.VMEM((own_rows, width), BF16),
            pltpu.VMEM((rows, wide), F32),
            pltpu.VMEM((rows, wide), F32),
            pltpu.VMEM((rows, width), F32),
            pltpu.VMEM((count, width, 4 * wide), BF16),
            pltpu.VMEM((rows, wide), BF16),
            pltpu.VMEM((2 * rows, deep), BF16),
            pltpu.VMEM((2 * rows, small), F32),
            pltpu.VMEM((2 * rows, small), F32),
            pltpu.VMEM((rows, wide), F32),
            pltpu.VMEM((2 * rows, 2 * small), BF16),
            pltpu.VMEM((rows, 3 * wide), BF16),
            pltpu.SemaphoreType.DMA((5 + 6 * count,)),
            pltpu.SemaphoreType.DMA((count,) + places.shape),
        ],
        BACKWARD_COST // 3 * count,
        1,
    )(
        places,
        *copied,
        *([] if first else [carried]),
        *ending,
        table[groups[0] : groups[-1] + 1],
        back_table[groups[0] : groups[-1] + 1],
        *ids,
    )


def run_feed_forward(carried, normed_c, pieces):
    rows, width = carried.shape
    count = sum(piece.shape[0] for piece in pieces)
    return kernel_call(
        functools.partial(feed_forward, len(pieces)),
        1,
        [ANYWHERE] * (2 + len(pieces)),
        [ANYWHERE] * 3,
        [
            struct((rows, count), BF16),
            struct((rows, count), BF16),
            struct((rows, width), F32),
        ],
        [
            pltpu.VMEM((count, 2 * width), BF16),
            pltpu.VMEM((rows, width), F32),
            pltpu.VMEM((rows, width), BF16),
            pltpu.VMEM((rows, count), F32),
            pltpu.VMEM((rows, count), BF16),
            pltpu.VMEM((rows, count), BF16),
            pltpu.SemaphoreType.DMA((len(pieces) + 2,)),
            pltpu.SemaphoreType.DMA((2 * len(hidden_chunks(count)) + 1,)),
        ],
        FORWARD_COST // 3,
    )(carried, normed_c, *pieces)


def run_feed_back(gradient, middle, gain, normed_c, stretches, pieces, places, carried, last):
    rows, width = middle.shape
    count = sum(piece.shape[0] for piece in pieces)
    first = carried is None
    kept = [array for arrays, _, _ in stretches for array in arrays]
    segments = [(column, size) for _, column, size in stretches]
    arrivals = 2 + not_first(first) + 2 * len(pieces) + len(kept)
    return kernel_call(
        functools.partial(feed_back, first, last, segments, len(pieces)),
        1,
        [
            ANYWHERE,
            whole((rows, width)),
            whole((1, width)),
            *[ANYWHERE] * (1 + len(kept) + not_first(first) + len(pieces)),
        ],
        [
            ANYWHERE,
            whole((rows, width)),
            *([whole((1, width)), whole((rows, width))] if last else []),
        ],
        [
            struct((count, 2 * width), BF16),
            struct((rows, width), F32),
            *([struct((1, width), F32), struct((rows, width), BF16)] if last else []),
        ],
        [
            pltpu.VMEM((count, 2 * width), BF16),
            pltpu.VMEM((rows, width), F32),
            pltpu.VMEM((rows - 2 * MOST, width), BF16),
            pltpu.VMEM((rows - 2 * MOST, count), BF16),
            pltpu.VMEM((rows, count), BF16),
            pltpu.VMEM((rows, width), F32),
            pltpu.VMEM((rows, width), BF16),
            pltpu.VMEM((rows, count), BF16),
            pltpu.VMEM((count, 2 * width), BF16),
            pltpu.SemaphoreType.DMA((arrivals,)),
            pltpu.SemaphoreType.DMA((2 * len(pieces),)),
        ],
        FORWARD_COST // 2,
        1,
    )(
        places,
        gradient,
        middle,
        gain[None],
        normed_c,
        *kept,
        *([] if first else [carried]),
        *pieces,
    )


def not_first(first):
    return 0 if first else 1


HEAD_DEVICES = 4
CHUNK = 512
X, Y, CORE = 2, 4, 1
FORWARD_COST = 29_000_000_000
BACKWARD_COST = 40_000_000_000


def hop(values, bit):
    count = lax.axis_size("dp")
    return lax.ppermute(values, "dp", [(i, i ^ bit) for i in range(count)])


def exchange(values):
    return lax.all_to_all(values, "head", split_axis=0, concat_axis=0, tiled=True)


def together(*values):
    return lax.optimization_barrier(values)


def by_permutes():
    return lax.axis_size("dp") == 8 and lax.axis_size("head") == HEAD_DEVICES


def group_width(parts, width, wide):
    return wide if parts == 4 else width


def join_columns(source, parts, begin, rows, width, wide):
    count = source.shape[0]
    return kernel_call(
        functools.partial(joining, parts, begin, group_width(parts, count * width, wide)),
        1,
        [whole(source.shape)],
        whole((rows, parts * count * width)),
        struct((rows, parts * count * width), BF16),
        [],
        1_000_000,
    )(source)


def feature_tables(source, begin, shapes):
    return kernel_call(
        functools.partial(tabulating, begin),
        1,
        [whole(source.shape)],
        [whole(shape) for shape in shapes],
        [struct(shape, BF16) for shape in shapes],
        [],
        1_000_000,
    )(source)


def block_of(rows, columns_all, index):
    return pl.BlockSpec((rows, columns_all), lambda *_: (index, 0))


def part_columns(pieces, parts, wide):
    rows = pieces[0][-1].shape[0]
    columns_all = sum(piece[0].shape[1] for piece in pieces)
    shape = (HEAD_DEVICES, rows, columns_all // HEAD_DEVICES)
    return kernel_call(
        functools.partial(
            parting, parts, group_width(parts, columns_all // parts, wide), len(pieces)
        ),
        1,
        [block_of(rows, source.shape[1], 0) for piece in pieces for source in piece],
        whole(shape),
        struct(shape, BF16),
        [],
        1_000_000,
    )(*[source for piece in pieces for source in piece])


def finish(sources, parts):
    _, rows, width = sources[0].shape
    width = width // sum(parts)
    shapes = [
        (len(sources), count, rows, width) if count > 1 else (len(sources), rows, width)
        for count in parts
    ]
    return kernel_call(
        functools.partial(finishing, parts),
        1,
        [whole(source.shape) for source in sources],
        [whole(shape) for shape in shapes],
        [struct(shape, F32) for shape in shapes],
        [],
        1_000_000,
    )(*sources)


def next_chips(own):
    return hop(own, X), hop(own, Y), hop(own, CORE)


def halves_to_pass(over_x, over_y):
    half = over_x.shape[0] // 2
    return over_x[:half], over_y[half:]


def chip_across(passed):
    to_y, to_x = passed
    return hop(to_y, Y), hop(to_x, X)


def other_core(pieces):
    return tuple(hop(piece, CORE) for piece in pieces)


def piece_places(rows):
    own = lax.axis_index("dp")
    bits = [(0, 0), (X, 0), (Y, 0), (X | Y, 0), (X | Y, rows // 2)]
    return jnp.stack(
        [(own ^ (bit | core)) * rows + begin for core in (0, CORE) for bit, begin in bits]
    ).astype(jnp.int32)


def block_places(rows):
    own = lax.axis_index("dp")
    return jnp.stack(
        [(own ^ (bit | core)) * rows for core in (CORE, 0) for bit in (0, X, Y, X | Y)]
    ).astype(jnp.int32)


class Reduction:
    def __init__(self, far, slow):
        self.slow, self.stage, self.left = slow, 0, 1
        self.came = hop(far, CORE)

    def prepare(self):
        rows, width = self.near.shape[0] // 4, self.near.shape[1]
        half, shape = (rows // 2, width), (rows, width)
        if self.stage == 0:
            self.far = self.came
            kernel, operands = adding_corner, (self.near, self.far)
            specs, out = [block_of(rows, width, 3)] * 2, half
        else:
            kernel, operands = adding_sides, (self.near, self.far, self.near, self.far, *self.came)
            specs, out = [block_of(rows, width, at) for at in (1, 1, 2, 2)] + [whole(half)] * 2, shape
        self.sent = kernel_call(
            kernel, 1, specs, [whole(out)] * 2, [struct(out, BF16)] * 2, [], 1_000_000
        )(*operands)

    def send(self):
        to_x, to_y = self.sent
        self.came = hop(to_x, X), hop(to_y, Y)
        self.stage += 1
        self.left = self.slow[self.stage - 1]

    def arrays(self):
        return [self.near, self.far, *self.came]


class Sharing:
    def __init__(self, reductions, parts, wide, slow):
        self.reductions, self.parts, self.wide, self.slow = reductions, parts, wide, slow
        self.stage, self.left, self.came = 0, 0, ()

    def prepare(self):
        pieces = [reduction.arrays() for reduction in self.reductions]
        self.sent = part_columns(pieces, self.parts, self.wide)

    def send(self):
        self.came = exchange(self.sent)
        self.stage, self.left = 1, self.slow


class Traffic:
    def __init__(self):
        self.moving = []

    def slot(self, values):
        ready = []
        for item in self.moving:
            item.left -= 1
            if item.left <= 0:
                ready.append(item)
        values, came = together(values, [item.came for item in ready])
        for item, arrived in zip(ready, came):
            item.came = arrived
        sending = []
        for item in ready:
            if isinstance(item, Sharing):
                if item.stage == 0 and all(r.stage == 3 for r in item.reductions):
                    sending.append(item)
            elif item.stage < 2:
                sending.append(item)
            else:
                item.stage = 3
        for item in ready:
            if isinstance(item, Sharing) and item.stage == 0 and item not in sending:
                if all(r.stage == 3 for r in item.reductions):
                    sending.append(item)
        for item in sending:
            item.prepare()
        values, sent = together(values, [item.sent for item in sending])
        for item, prepared in zip(sending, sent):
            item.sent = prepared
            item.send()
        self.moving = [
            item
            for item in self.moving
            if item.stage < (1 if isinstance(item, Sharing) else 3) or item.left > 0
        ]
        return values


def grouped_columns(values, parts, wide):
    rows = values.shape[0]
    return values.reshape(rows, parts, -1, wide).swapaxes(1, 2).reshape(rows, -1)


def over_heads(part, parts, wide):
    rows = part.shape[0]
    if parts == 4:
        part = part.reshape(rows, -1, parts, wide).swapaxes(1, 2)
    part = part.reshape(rows, parts, -1)
    part = lax.psum_scatter(part, "head", scatter_dimension=2, tiled=True)
    return part.swapaxes(0, 1).astype(F32)


def shared_gain(values, stage):
    if stage < 3:
        return values + hop(values, (CORE, X, Y)[stage])
    bit = 1 << (stage - 3)
    return values + lax.ppermute(values, "head", [(i, i ^ bit) for i in range(HEAD_DEVICES)])


def with_halo(inputs, cotangent):
    count = lax.axis_size("head")
    both = jnp.concatenate([inputs, cotangent], axis=1)
    before = lax.ppermute(both[-MOST:], "head", [(i, i + 1) for i in range(count - 1)])
    after = lax.ppermute(both[:MOST], "head", [(i + 1, i) for i in range(count - 1)])
    joined = jnp.concatenate([before, both, after], axis=0).astype(F32)
    return joined[:, : inputs.shape[1]], joined[:, inputs.shape[1] :]


def window_ids(segment_ids, own_rows):
    padded = jnp.pad(segment_ids[0], (MOST, MOST), constant_values=-1)
    begin = lax.axis_index("head") * own_rows
    ids = lax.dynamic_slice(padded, (begin,), (own_rows + 2 * MOST,))
    place = jnp.arange(ids.shape[0])
    earlier = (ids[:, None] == ids[None, :]) & (place[None, :] < place[:, None])
    position = jnp.sum(earlier.astype(F32), axis=1)
    used = (ids >= ids[MOST]) & (ids <= ids[MOST + own_rows - 1])
    column = jnp.where(used, ids, -1)[:, None]
    row = jnp.where(used, ids, -2)
    starts = [
        min(max(b * QUERY_ROWS - MOST, 0), ids.shape[0] - KEY_ROWS)
        for b in range(ids.shape[0] // QUERY_ROWS)
    ]
    rows = jnp.stack([row[start : start + KEY_ROWS] for start in starts])[:, None, :]
    return position, (column, rows)


def rotary_tables(position, head_width):
    halves = head_width // 2
    frequency = jnp.exp(jnp.arange(halves, dtype=F32) * (-2.0 * math.log(10000.0) / head_width))
    angles = position[:, None] * frequency[None, :]
    cosine, sine = jnp.cos(angles), jnp.sin(angles)
    return (
        jnp.tile(jnp.concatenate([cosine, cosine], axis=1), (1, GROUP)),
        jnp.tile(jnp.concatenate([-sine, sine], axis=1), (1, GROUP)),
    )


def body(
    inputs,
    segment_ids,
    features,
    norm_gain,
    query_key_value,
    output_weight,
    up_weight,
    down_weight,
    cotangent,
):
    layer_count = norm_gain.shape[0]
    own_rows = inputs.shape[0]
    head_width = features.shape[3]
    feature_count = features.shape[2]
    scale = head_width ** (-0.25)
    own_place = slice(MOST, MOST + own_rows)

    in_rows, part_width = output_weight.shape[1:]
    groups = inputs.shape[1] // (GROUP * head_width)
    wide, small = GROUP * head_width, GROUP * feature_count
    table_shapes = [(groups, 4 * wide, small)] * layer_count + [
        (groups, 2 * wide, 2 * small)
    ] * layer_count
    chunks = []
    for layer in range(layer_count):
        chunks.append((4, *query_key_value[layer], output_weight[layer]))
        chunks.append((2, up_weight[layer], down_weight[layer]))
    stored = []
    if by_permutes():
        attention_places = piece_places(in_rows)
        grad_places = block_places(in_rows)
        feed_places = piece_places(up_weight.shape[1])[jnp.array([0, 1, 2, 5, 6, 7, 3, 4, 8, 9])]
        feature_rows = jnp.moveaxis(features, 3, 0).reshape(4, head_width // 4, -1)
        feature_rows = jnp.concatenate(list(feature_rows), axis=1)

        def join(index, came, begin=0):
            parts, *weights = chunks[index]
            return join_columns(came, parts, begin, *weights[-1].shape, wide)

        def gathered_columns(sent):
            return lax.all_gather(sent, "head", axis=0, tiled=False)

        sent = jnp.concatenate([jnp.concatenate(chunks[0][1:], axis=1), feature_rows])
        sent = jnp.broadcast_to(sent[None], (HEAD_DEVICES,) + sent.shape)
        sent, inputs, cotangent = together(sent, inputs, cotangent)
        came = exchange(sent)
        state, gradient = with_halo(inputs, cotangent)
        position, ids = window_ids(segment_ids, own_rows)
        tables = rotary_tables(position, head_width)
        both = []
        for layer in range(1, layer_count):
            q, k, v, o = chunks[2 * layer][1:]
            both.append(
                jnp.concatenate(
                    [
                        jnp.concatenate(pair, axis=1)
                        for pair in ((q, k), (v, o), chunks[2 * layer + 1][1:])
                    ]
                )
            )
        first_feed = jnp.concatenate(chunks[1][1:], axis=1)
        came, state, gradient, tables, ids, first_feed = together(
            came, state, gradient, tables, ids, first_feed
        )
        attend = functools.partial(run_attention_forward, tables=tables, ids=ids, scale=scale)
        own = join(0, came)
        came_feed = gathered_columns(first_feed)
        over_x, over_y, over_core = next_chips(own)
        made = feature_tables(came, in_rows, table_shapes)
        over_x, over_y, over_core, made, both = together(over_x, over_y, over_core, made, both)
        blocks, back_blocks = made[:layer_count], made[layer_count:]
        passed = halves_to_pass(over_x, over_y)
        across = chip_across(passed)
        own_feed = join(1, came_feed)
        for layer in range(layer_count):
            more = layer + 1 < layer_count
            near = (own, over_x, over_y) + tuple(across)
            far = (over_core,) + other_core(near[1:])
            attention_pieces = near + far
            own = own_feed
            state, own, sent = together(state, own, both[layer] if more else ())
            over_x, over_y, over_core = next_chips(own)
            came = gathered_columns(sent) if more else ()
            weights, *kept, middle, normed_c = attend(
                state,
                norm_gain[layer],
                attention_pieces,
                attention_places,
                blocks[layer],
            )

            middle, over_x, over_y, over_core = together(middle, over_x, over_y, over_core)
            sides = own, over_x, over_y
            passed = halves_to_pass(over_x, over_y)
            carried, passed = together(middle, passed)
            across = chip_across(passed)
            far_sides = (over_core,) + other_core(sides[1:])
            near_kept = run_feed_forward(carried, normed_c, sides)

            carried, across, far_sides = together(near_kept[2], across, far_sides)
            far_across = other_core(across)
            if more:
                carried, came = together(carried, came)
                carried, own = together(carried, join(2 * layer + 2, came))
                over_x, over_y, over_core = next_chips(own)
            last_pieces = across + far_across
            feed_pieces = sides, far_sides, across, far_across
            far_kept = run_feed_forward(carried, normed_c, far_sides)

            carried = far_kept[2]
            if more:
                carried, over_x, over_y, over_core = together(carried, over_x, over_y, over_core)
                passed = halves_to_pass(over_x, over_y)
                carried, passed = together(carried, passed)
                across = chip_across(passed)
            last_kept = run_feed_forward(carried, normed_c, last_pieces)
            hidden_kept = near_kept[:2], far_kept[:2], last_kept[:2]
            stored.append(
                (state, weights, kept, middle, normed_c, hidden_kept, feed_pieces)
            )
            state = last_kept[2]
            if more:
                state, across, came = together(state, across, came)
                own_feed = join(2 * layer + 3, came, 2 * in_rows)
    else:
        state, gradient = with_halo(inputs, cotangent)
        position, ids = window_ids(segment_ids, own_rows)
        tables = rotary_tables(position, head_width)
        attend = functools.partial(run_attention_forward, tables=tables, ids=ids, scale=scale)
        all_features = lax.all_gather(features, "head", axis=1, tiled=True)
        shaped = all_features.reshape(layer_count, -1, GROUP, feature_count, head_width)
        eye = jnp.eye(GROUP, dtype=BF16)
        block = jnp.einsum("lghmw,hk->lghwkm", shaped, eye).reshape(layer_count, groups, wide, small)
        ones = jnp.kron(eye, jnp.ones((head_width, feature_count), BF16))
        ones = jnp.broadcast_to(ones, block.shape)
        blocks = jnp.concatenate([block, block, ones * -0.5, ones * -0.5], axis=2)
        back_blocks = jnp.concatenate([block, ones], axis=2)
        back_blocks = jnp.concatenate([back_blocks, back_blocks], axis=3)
        owned = []
        for parts, *weights in chunks:
            rows = weights[-1].shape[0]
            joined = jnp.stack(weights)
            joined = lax.all_gather(joined, "head", axis=2, tiled=True)
            joined = lax.all_gather(joined, "dp", axis=1, tiled=True)
            joined = joined.swapaxes(0, 1).reshape(joined.shape[1], -1)
            owned.append(grouped_columns(joined, parts, wide) if parts == 4 else joined)
        middle_row = inputs.shape[1] // 2
        attention_places = jnp.array([0, middle_row], jnp.int32)
        size = up_weight.shape[1] * lax.axis_size("dp") // 8
        feed_places = jnp.array([0, 4 * size, 3 * size, 7 * size], jnp.int32)
        for layer in range(layer_count):
            own_attention, own_feed = owned[2 * layer], owned[2 * layer + 1]
            weights, *kept, middle, normed_c = attend(
                state,
                norm_gain[layer],
                (own_attention[:middle_row], own_attention[middle_row:]),
                attention_places,
                blocks[layer],
            )
            size = own_feed.shape[0] // 8
            feed_pieces = [
                (own_feed[begin * size : end * size],) for begin, end in ((0, 3), (4, 7), (3, 4), (7, 8))
            ]
            near_kept = run_feed_forward(middle, normed_c, feed_pieces[0])
            far_kept = run_feed_forward(near_kept[2], normed_c, feed_pieces[1])
            last_kept = run_feed_forward(far_kept[2], normed_c, feed_pieces[2] + feed_pieces[3])
            hidden_kept = near_kept[:2], far_kept[:2], last_kept[:2]
            stored.append(
                (state, weights, kept, middle, normed_c, hidden_kept, feed_pieces)
            )
            state = last_kept[2]
    outputs = state[own_place].astype(BF16)

    gains = [None] * layer_count
    shares = [None] * layer_count
    traffic = Traffic()
    summing = []
    for layer in reversed(range(layer_count)):
        before, weights, kept, middle, normed_c, hidden_kept, feed_pieces = stored[layer]
        near_kept, far_kept, corner_kept = hidden_kept
        side, corner = near_kept[0].shape[1], corner_kept[0].shape[1] // 2
        stretches = [
            (near_kept, 0, side),
            (far_kept, 0, side),
            (corner_kept, 0, corner),
            (corner_kept, corner, corner),
        ]
        feed = (middle, norm_gain[layer, 1], normed_c)
        attend_back = functools.partial(
            run_attention_backward,
            state=before,
            gain=norm_gain[layer, 0],
            weights=weights,
            table=blocks[layer],
            back_table=back_blocks[layer],
            tables=tables,
            ids=ids,
            kept=kept,
            scale=scale,
        )
        if layer > 0 or not by_permutes():
            pieces = [piece for part in feed_pieces for piece in part]
            feed_grad, grad_middle, gain_c, branch = run_feed_back(
                gradient, *feed, stretches, pieces, feed_places, None, True
            )
            feed_part = lax.psum_scatter(feed_grad, "dp", scatter_dimension=0, tiled=True)
            gradient, gain_a, *grad = attend_back(
                tuple(range(groups)),
                None,
                grad_middle=grad_middle,
                branch=branch,
                places=grad_places if by_permutes() else jnp.zeros((1,), jnp.int32),
            )
            if by_permutes():
                gains[layer] = jnp.concatenate([gain_a, gain_c])
                attention_sum = Reduction(grad[0], (1, 1))
                attention_sum.near, attention_sum.left = grad[1], 2
                traffic.moving.append(attention_sum)
                summing.append((layer, feed_part, attention_sum))
                continue
            [grad] = grad
            attention_part = lax.psum_scatter(grad, "dp", scatter_dimension=0, tiled=True)
            gains[layer] = jnp.concatenate([gain_a, gain_c])
            shares[layer] = over_heads(feed_part, 2, wide), over_heads(attention_part, 4, wide)
            continue
        relative = [
            jnp.array(begins_of(feed_pieces[at] + feed_pieces[2 + at])[:-1], jnp.int32) for at in (0, 1)
        ]
        gradient = traffic.slot(gradient)
        feed_far, carried = run_feed_back(
            gradient,
            *feed,
            [stretches[1], stretches[3]],
            feed_pieces[1] + feed_pieces[3],
            relative[1],
            None,
            False,
        )
        carried, feed_far = traffic.slot((carried, feed_far))
        feed_sum = Reduction(feed_far, (1, 1))
        traffic.moving.append(feed_sum)
        feed_near, grad_middle, gain_c, branch = run_feed_back(
            gradient,
            *feed,
            [stretches[0], stretches[2]],
            feed_pieces[0] + feed_pieces[2],
            relative[0],
            carried,
            True,
        )
        feed_sum.near = feed_near
        feed_share = Sharing([feed_sum], 2, wide, 2)
        traffic.moving.append(feed_share)
        carried, attention_sums = None, []
        for call_groups in (tuple(range(groups - 1)), (groups - 1,)):
            branch, grad_middle, carried = traffic.slot((branch, grad_middle, carried))
            if attention_sums:
                traffic.moving.append(attention_sums[-1])
                for later, feed_part, attention_sum in summing:
                    carried, feed_part = together(carried, feed_part)
                    share = Sharing([], 2, wide, 1)
                    share.sent = part_columns([[feed_part]], 2, wide)
                    parted = part_columns([attention_sum.arrays()], 4, wide)
                    carried, share.sent, parted = together(carried, share.sent, parted)
                    share.send()
                    traffic.moving.append(share)
                    parted = lax.psum_scatter(parted, "head", scatter_dimension=0, tiled=True)
                    shares[later] = share, parted
            carried, *gain_a, far, near = attend_back(
                call_groups, carried, grad_middle=grad_middle, branch=branch, places=grad_places
            )
            carried, far, near = together(carried, far, near)
            attention_sums.append(Reduction(far, (1, 1)))
            attention_sums[-1].near = near
        gradient = carried
        gains[layer] = jnp.concatenate([*gain_a, gain_c])
        traffic.moving.append(attention_sums[-1])
        attention_share = Sharing(attention_sums, 4, wide, 1)
        traffic.moving.append(attention_share)
        shares[layer] = feed_share, attention_share
    if by_permutes():
        gain_all = jnp.stack(gains)
        input_grad = gradient[own_place]
        gain_all = traffic.slot(gain_all)
        gain_all = shared_gain(gain_all, 0)
        gain_all = traffic.slot(gain_all)
        gain_all, outputs, input_grad = together(gain_all, outputs, input_grad)
        gain_all, parted = together(gain_all, [share[1] for share in shares[1:]])
        gain_all = shared_gain(shared_gain(gain_all, 1), 2)
        gain_all = traffic.slot(gain_all)
        up_grad, down_grad = finish([share[0].came for share in shares], (1, 1))
        gain_all = shared_gain(shared_gain(gain_all, 3), 4)
        gain_all, up_grad, down_grad = together(gain_all, up_grad, down_grad)
        while traffic.moving:
            gain_all = traffic.slot(gain_all)
        gain_total = gain_all
        qkv_grad, out_grad = finish([shares[0][1].came] + parted, (3, 1))
    else:
        gain_total = lax.psum(jnp.stack(gains), ("dp", "head"))
        input_grad = gradient[own_place]
        results = [(a[:3], a[3], f[0], f[1]) for f, a in shares]
        qkv_grad, out_grad, up_grad, down_grad = (
            jnp.stack(list(kind)) for kind in zip(*results)
        )
    return (
        outputs,
        input_grad,
        gain_total[:, 0],
        gain_total[:, 1],
        qkv_grad,
        out_grad,
        up_grad,
        down_grad,
    )


def solution(mesh):
    in_specs = (
        P(("dp", "head"), None),
        P("dp", None),
        P(None, "head", None, None),
        P(),
        P(None, None, "dp", "head"),
        P(None, "dp", "head"),
        P(None, "dp", "head"),
        P(None, "dp", "head"),
        P(("dp", "head"), None),
    )
    out_specs = (
        P(("dp", "head"), None),
        P(("dp", "head"), None),
        P(),
        P(),
        P(None, None, "dp", "head"),
        P(None, "dp", "head"),
        P(None, "dp", "head"),
        P(None, "dp", "head"),
    )
    return jax.shard_map(body, mesh=mesh, in_specs=in_specs, out_specs=out_specs, check_vma=False)
```

```python
import functools
import math

import jax
import jax.numpy as jnp
from jax import lax
from jax.experimental import pallas as pl
from jax.experimental.pallas import tpu as pltpu
from jax.sharding import PartitionSpec as P

MOST = 64
EPSILON = 1e-05
QUERY_ROWS = 128
KEY_ROWS = QUERY_ROWS + 2 * MOST
GROUP = 4
VMEM_BYTES = 60 * 2**20

BF16 = jnp.bfloat16
F32 = jnp.float32
CONTRACT_LAST = (((1,), (1,)), ((), ()))
CONTRACT_FIRST = (((0,), (0,)), ((), ()))
CONTRACT_MIDDLE = (((1,), (0,)), ((), ()))

TAIL_SCALE = 0.3275911 / math.sqrt(2.0)
TAIL_TERMS = (1.061405429, -1.453152027, 1.421413741, -0.284496736, 0.254829592)


def dot(left, right, dims=CONTRACT_MIDDLE):
    return lax.dot_general(left, right, dims, preferred_element_type=F32)


def gelu_and_slope(hidden):
    bell = jnp.exp(hidden * hidden * -0.5)
    below = 1.0 + jnp.abs(hidden) * TAIL_SCALE
    guess = pl.reciprocal(below, approx=True)
    inverse = guess * (2.0 - below * guess)
    tail = 0.5 * TAIL_TERMS[0]
    for term in TAIL_TERMS[1:]:
        tail = tail * inverse + 0.5 * term
    tail = tail * inverse * bell
    cumulative = jnp.where(hidden > 0.0, 1.0 - tail, tail)
    return hidden * cumulative, cumulative + hidden * (bell * (1.0 / math.sqrt(2.0 * math.pi)))


def normalised(values):
    centred = values - jnp.mean(values, axis=-1, keepdims=True)
    inverse = lax.rsqrt(jnp.mean(centred * centred, axis=-1, keepdims=True) + EPSILON)
    return centred * inverse, inverse


def norm_back(grad_out, gain, hat, inverse):
    scaled = grad_out * gain
    first_mean = jnp.mean(scaled, axis=-1, keepdims=True)
    second_mean = jnp.mean(scaled * hat, axis=-1, keepdims=True)
    return inverse * (scaled - first_mean - hat * second_mean)


def each_block(rows, size, step):
    for block in row_blocks(rows, size):
        step(block)


def own_block(block, rows):
    return MOST <= block.start and block.stop <= rows - MOST


def swap_halves(values, half):
    width = values.shape[-1]
    lane = lax.broadcasted_iota(jnp.int32, values.shape, len(values.shape) - 1)
    ahead = pltpu.roll(values, width - half, 1)
    behind = pltpu.roll(values, half, 1)
    return jnp.where(lane % (2 * half) < half, ahead, behind)


def two_parts(values):
    high = values.astype(BF16)
    return high, (values - high.astype(F32)).astype(BF16)


def row_blocks(rows, size):
    return [slice(begin, begin + size) for begin in range(0, rows, size)]


def spread_parts(rows, target, place):
    width = rows.shape[1]
    for index, part in enumerate((*two_parts(rows), *two_parts(rows * rows))):
        target[place, index * width : (index + 1) * width] = part


def phi_of(parts, table):
    return jnp.exp(dot(parts, table)) * (1.0 / math.sqrt(table.shape[1] // GROUP))


def head_masks(width, dtype):
    lane = lax.broadcasted_iota(jnp.int32, (1, width), 1) // (width // GROUP)
    return [jnp.where(lane == head, 1.0, 0.0).astype(dtype) for head in range(GROUP)]


def spread_heads(values):
    return jnp.concatenate([values * mask for mask in head_masks(values.shape[1], BF16)], axis=0)


def gather_heads(values):
    masks = head_masks(values.shape[-1], F32)
    total = values[0] * masks[0]
    for head in range(1, GROUP):
        total = total + values[head] * masks[head]
    return total


def block_scores(phi_q, phi_k, ids_column, ids_row):
    scores = dot(phi_q, phi_k, CONTRACT_LAST)
    same = (ids_column == ids_row).astype(F32)
    scores = scores.reshape(GROUP, QUERY_ROWS, KEY_ROWS) * same[None]
    totals = jnp.sum(scores, axis=-1, keepdims=True)
    inverse = jnp.where(totals > 0.0, 1.0 / totals, 0.0)
    return scores * inverse, inverse, same


def query_blocks(rows):
    for index, block in enumerate(row_blocks(rows, QUERY_ROWS)):
        begin = min(max(block.start - MOST, 0), rows - KEY_ROWS)
        yield index, block, slice(begin, begin + KEY_ROWS)


def attention_forward(
    scale,
    piece_count,
    places,
    state,
    gain_1,
    gain_2,
    table,
    cosine,
    sine,
    ids_column,
    ids_row,
    *others,
):
    pieces = others[:piece_count]
    weights_out, normed_a, query, key, value, mixed, middle, normed_c, *others = others[piece_count:]
    weights, total, projected, parts, phi, arrived, leaving = others
    group = pl.program_id(0)
    groups = weights.shape[0]
    rows = state.shape[0]
    wide = query.shape[1]
    deep = weights.shape[2]
    half = cosine.shape[1] // GROUP // 2

    def columns_of(at):
        return pl.ds(at * deep, deep)

    def arriving_at(at):
        for index, piece in enumerate(pieces):
            place = pl.ds(pl.multiple_of(places[index], 16), piece.shape[0])
            yield pltpu.make_async_copy(
                piece.at[:, columns_of(at)], weights.at[at, place, :], arrived.at[at, index]
            )

    def leaving_at(at):
        return pltpu.make_async_copy(
            weights.at[at], weights_out.at[:, columns_of(at)], leaving.at[at]
        )

    @pl.when(group == 0)
    def _():
        for at in range(groups):
            for copy in arriving_at(at):
                copy.start()

        def step(block):
            hat, _ = normalised(state[block, :])
            normed_a[block, :] = (hat * gain_1[...]).astype(BF16)
            total[block, :] = state[block, :]

        each_block(rows, 64, step)

    for at in range(groups):

        @pl.when(group == at)
        def _(at=at):
            for copy in arriving_at(at):
                copy.wait()
            leaving_at(at).start()

    projected[...] = dot(normed_a[...], weights[group, :, : 3 * wide])
    for block in row_blocks(rows, 64):
        for part, held in enumerate((query, key)):
            values = projected[block, part * wide : (part + 1) * wide]
            turned = values * cosine[block, :] + swap_halves(values, half) * sine[block, :]
            turned = turned * scale
            held[block, :] = turned
            spread_parts(turned, parts, slice(part * rows + block.start, part * rows + block.stop))
        value[block, :] = projected[block, 2 * wide :].astype(BF16)
    phi[...] = phi_of(parts[...], table[0]).astype(BF16)

    for index, block, keys in query_blocks(rows):
        scores, _, _ = block_scores(
            spread_heads(phi[block, :]),
            phi[rows + keys.start : rows + keys.stop, :],
            ids_column[block, :],
            ids_row[index],
        )
        scores = scores.reshape(GROUP * QUERY_ROWS, KEY_ROWS).astype(BF16)
        found = dot(scores, value[keys, :])
        mixed[block, :] = gather_heads(found.reshape(GROUP, QUERY_ROWS, -1)).astype(BF16)

    total[...] += dot(mixed[...], weights[group, :, 3 * wide :], CONTRACT_LAST)

    @pl.when(group == groups - 1)
    def _():
        def step(block):
            middle[block, :] = total[block, :]
            hat, _ = normalised(total[block, :])
            normed_c[block, :] = (hat * gain_2[...]).astype(BF16)

        each_block(rows, 64, step)
        for at in range(groups):
            leaving_at(at).wait()


class Arrivals:
    def __init__(self, semaphores):
        self.semaphores, self.copies = semaphores, []

    def start(self, source, target):
        copy = pltpu.make_async_copy(source, target, self.semaphores.at[len(self.copies)])
        copy.start()
        self.copies.append(copy)
        return copy


def attention_backward(first, last, scale, groups, split, places, branch_in, weights_in, mixed_in, query_in, key_in, value_in, *others):
    normed_in, cosine_in, sine_in, *others = others
    if not first:
        total_in, *others = others
    if last:
        grad_middle, state, gain_1, *others = others
    table, back_table, ids_column, ids_row, *others = others
    if last:
        grad_state, grad_gain, *others = others
    else:
        total_out, *others = others
    grad_targets, others = others[: 1 + split], others[1 + split :]
    (
        branch,
        weights,
        mixed,
        query,
        key,
        value,
        normed_a,
        cosine,
        sine,
        total,
        grad_weight,
        grad_mixed,
        parts,
        phi,
        grad_phi,
        grad_value,
        grad_parts,
        grad_projected,
        arrived,
        leaving,
    ) = others
    _, rows, wide = query.shape
    half = wide // GROUP // 2
    own_rows = rows - 2 * MOST
    own = pl.ds(MOST, own_rows)
    small = phi.shape[1]
    deep = weights.shape[2]
    arrivals = Arrivals(arrived)
    got_branch = arrivals.start(branch_in, branch)
    got = []
    for at, group in enumerate(groups):
        columns_in = pl.ds(group * wide, wide)
        got.append(
            (
                arrivals.start(
                    weights_in.at[:, pl.ds(group * deep + 3 * wide, wide)],
                    weights.at[at, :, pl.ds(3 * wide, wide)],
                ),
                arrivals.start(query_in.at[:, columns_in], query.at[at]),
                arrivals.start(key_in.at[:, columns_in], key.at[at]),
                arrivals.start(mixed_in.at[own, columns_in], mixed.at[at]),
                arrivals.start(value_in.at[:, columns_in], value.at[at]),
                arrivals.start(
                    weights_in.at[:, pl.ds(group * deep, 3 * wide)],
                    weights.at[at, :, pl.ds(0, 3 * wide)],
                ),
            )
        )
        if at == 0:
            got_shared = [
                arrivals.start(cosine_in, cosine),
                arrivals.start(sine_in, sine),
                arrivals.start(normed_in.at[own, :], normed_a),
            ]
    if not first:
        got_total = arrivals.start(total_in, total)
    got_branch.wait()
    count = leaving.shape[1]
    size = grad_weight.shape[1] // count
    copies = []
    for at in range(len(groups)):
        got_last, *got_rows, got_first = got[at]
        got_last.wait()
        for copy in got_rows:
            copy.wait()
        grad_mixed[...] = dot(branch[...], weights[at, :, 3 * wide :]).astype(BF16)
        for block in row_blocks(rows, 64):
            for part, held in enumerate((query, key)):
                place = slice(part * rows + block.start, part * rows + block.stop)
                spread_parts(held[at, block, :], parts, place)
        phi[...] = phi_of(parts[...], table[at])
        grad_phi[rows:, :] = jnp.zeros((rows, small), F32)
        grad_value[...] = jnp.zeros_like(grad_value)
        found = dot(branch[own, :], mixed[at], CONTRACT_FIRST)
        grad_weight[at, :, 3 * wide :] = found.astype(BF16)

        for index, block, keys in query_blocks(rows):
            far_keys = slice(rows + keys.start, rows + keys.stop)
            spread_q = spread_heads(phi[block, :].astype(BF16))
            spread_grad = spread_heads(grad_mixed[block, :])
            keys_phi = phi[far_keys, :].astype(BF16)
            scores, inverse, same = block_scores(
                spread_q, keys_phi, ids_column[block, :], ids_row[index]
            )
            flat = (GROUP * QUERY_ROWS, KEY_ROWS)
            grad_scores = dot(spread_grad, value[at, keys, :], CONTRACT_LAST)
            grad_value[keys, :] += dot(
                scores.reshape(flat).astype(BF16), spread_grad, CONTRACT_FIRST
            )
            grad_scores = grad_scores.reshape(scores.shape)
            inner = jnp.sum(grad_scores * scores, axis=-1, keepdims=True)
            grad_scores = ((grad_scores - inner) * inverse * same[None]).astype(BF16).reshape(flat)
            found = dot(grad_scores, keys_phi)
            grad_phi[block, :] = gather_heads(found.reshape(GROUP, QUERY_ROWS, -1))
            grad_phi[far_keys, :] += dot(grad_scores, spread_q, CONTRACT_FIRST)

        if at == 0:
            for copy in got_shared:
                copy.wait()
        got_first.wait()
        for block in row_blocks(2 * rows, 128):
            high, low = two_parts(grad_phi[block, :] * phi[block, :])
            grad_parts[block, :small] = high
            grad_parts[block, small:] = low
        for part, held in enumerate((query, key)):
            for block in row_blocks(rows, 128):
                there = slice(part * rows + block.start, part * rows + block.stop)
                both = dot(grad_parts[there, :], back_table[at], CONTRACT_LAST)
                grad_rows = (both[:, :wide] - held[at, block, :] * both[:, wide:]) * scale
                turned = grad_rows * cosine[block, :]
                turned = turned + swap_halves(grad_rows * sine[block, :], half)
                grad_projected[block, part * wide : (part + 1) * wide] = turned.astype(BF16)
        grad_projected[:, 2 * wide :] = grad_value[...].astype(BF16)
        found = dot(normed_a[...], grad_projected[own, :], CONTRACT_FIRST)
        grad_weight[at, :, : 3 * wide] = found.astype(BF16)
        for index in range(count):
            place = pl.ds(pl.multiple_of(places[index], 16), size) if split else pl.ds(0, size)
            each = count // len(grad_targets)
            target = grad_targets[index // each]
            to = pl.ds(index % each * size, size)
            copies.append(
                pltpu.make_async_copy(
                    grad_weight.at[at, place, :],
                    target.at[to, pl.ds(at * deep, deep)],
                    leaving.at[at, index],
                )
            )
            copies[-1].start()
        back = dot(grad_projected[...], weights[at, :, : 3 * wide], CONTRACT_LAST)
        ending = at == len(groups) - 1
        if at == 0 and not first:
            got_total.wait()
        if at > 0 or not first:
            back = total[...] + back
        if ending and not last:
            total_out[...] = back
        else:
            total[...] = back
    if last:
        grad_gain[...] = jnp.zeros_like(grad_gain)

        def step(block):
            hat, inverse = normalised(state[block, :])
            back = norm_back(total[block, :], gain_1[...], hat, inverse)
            grad_state[block, :] = grad_middle[block, :] + back
            if own_block(block, rows):
                grad_gain[...] += jnp.sum(total[block, :] * hat, axis=0, keepdims=True)

        each_block(rows, 64, step)
    for copy in copies:
        copy.wait()


def adding(stages, *others):
    takes = [2 if stage == 0 else 6 for stage in stages]
    targets = others[sum(takes) :]
    begin = 0
    for index, (stage, count) in enumerate(zip(stages, takes)):
        kernel = adding_corner if stage == 0 else adding_sides
        kernel(*others[begin : begin + count], *targets[2 * index : 2 * index + 2])
        begin += count


def begins_of(pieces):
    begins = [0]
    for piece in pieces:
        begins.append(begins[-1] + piece.shape[0])
    return begins


def hidden_chunks(count):
    return [slice(begin, min(begin + CHUNK, count)) for begin in range(0, count, CHUNK)]


def feed_forward(piece_count, carried_in, normed_in, *others):
    pieces = others[:piece_count]
    activated_out, slope_out, state_out, *others = others[piece_count:]
    held, carried, normed_c, hidden, activated, slope, arrived, leaving = others
    rows, width = carried.shape
    count = held.shape[0]
    begins = begins_of(pieces)
    copies = [
        pltpu.make_async_copy(
            piece, held.at[pl.ds(begins[index], piece.shape[0]), :], arrived.at[index]
        )
        for index, piece in enumerate(pieces)
    ]
    norm_copy = pltpu.make_async_copy(normed_in, normed_c, arrived.at[piece_count])
    carried_copy = pltpu.make_async_copy(carried_in, carried, arrived.at[piece_count + 1])
    norm_copy.start()
    for copy in copies:
        copy.start()
    carried_copy.start()
    norm_copy.wait()
    chunks = hidden_chunks(count)
    waited = 0
    outgoing = []

    def project(chunk):
        hidden[:, chunk] = dot(normed_c[...], held[chunk, :width], CONTRACT_LAST)

    def wait_until(row):
        nonlocal waited
        while waited < piece_count and begins[waited] < row:
            copies[waited].wait()
            waited += 1

    wait_until(chunks[0].stop)
    project(chunks[0])
    wait_until(count)
    for index, chunk in enumerate(chunks):
        if index + 1 < len(chunks):
            project(chunks[index + 1])
        for block in row_blocks(rows, 32):
            value, back = gelu_and_slope(hidden[block, chunk])
            activated[block, chunk] = value.astype(BF16)
            slope[block, chunk] = back.astype(BF16)
        for target, source in ((activated_out, activated), (slope_out, slope)):
            outgoing.append(
                pltpu.make_async_copy(
                    source.at[:, chunk], target.at[:, chunk], leaving.at[len(outgoing)]
                )
            )
            outgoing[-1].start()
    carried_copy.wait()
    carried[...] += dot(activated[...], held[:, width:])
    outgoing.append(pltpu.make_async_copy(carried, state_out, leaving.at[len(outgoing)]))
    outgoing[-1].start()
    for copy in outgoing:
        copy.wait()


def feed_back(first, last, segments, piece_count, places, gradient_in, middle, gain_2, normed_in, *others):
    kept, others = others[: 2 * len(segments)], others[2 * len(segments) :]
    if not first:
        total_in, *others = others
    pieces = others[:piece_count]
    grad_out, grad_middle, *others = others[piece_count:]
    if last:
        grad_gain, grad_attn, *others = others
    (
        held,
        gradient,
        normed_c,
        activated,
        slope,
        total,
        branch,
        grad_hidden,
        grad_weight,
        arrived,
        leaving,
    ) = others
    rows, width = gradient.shape
    own_rows = rows - 2 * MOST
    own = pl.ds(MOST, own_rows)
    count = held.shape[0]
    begins = begins_of(pieces)
    arrivals = Arrivals(arrived)
    left, right = pl.ds(0, width), pl.ds(width, width)

    def weight_half(half):
        return [
            arrivals.start(
                piece.at[:, half], held.at[pl.ds(begins[index], piece.shape[0]), half]
            )
            for index, piece in enumerate(pieces)
        ]

    def leave(half, offset):
        copies = []
        for index, piece in enumerate(pieces):
            size = piece.shape[0]
            copies.append(
                pltpu.make_async_copy(
                    grad_weight.at[pl.ds(begins[index], size), half],
                    grad_out.at[pl.ds(pl.multiple_of(places[index], 16), size), half],
                    leaving.at[offset + index],
                )
            )
            copies[-1].start()
        return copies

    def stretch(which, rows_taken, target):
        copies, begin = [], 0
        for index, (column, size) in enumerate(segments):
            source = kept[2 * index + which].at[rows_taken, pl.ds(column, size)]
            copies.append(arrivals.start(source, target.at[:, pl.ds(begin, size)]))
            begin += size
        return copies

    got_gradient = arrivals.start(gradient_in, gradient)
    got_act = stretch(0, own, activated)
    got_down = weight_half(right)
    got_slope = stretch(1, pl.ds(0, rows), slope)
    got_norm = arrivals.start(normed_in.at[own, :], normed_c)
    got_up = weight_half(left)
    if not first:
        got_total = arrivals.start(total_in, total)
    got_gradient.wait()
    for block in row_blocks(rows, 64):
        branch[block, :] = gradient[block, :].astype(BF16)
    for copy in got_act:
        copy.wait()
    for chunk in row_blocks(count, count // 2):
        found = dot(activated[:, chunk], branch[own, :], CONTRACT_FIRST)
        grad_weight[chunk, width:] = found.astype(BF16)
    down_leaves = leave(right, 0)
    for copy in got_down + got_slope:
        copy.wait()
    for chunk in hidden_chunks(count):
        grad_act = dot(branch[...], held[chunk, width:], CONTRACT_LAST)
        grad_hidden[:, chunk] = (grad_act * slope[:, chunk].astype(F32)).astype(BF16)
    for copy in [got_norm] + got_up:
        copy.wait()
    for chunk in row_blocks(count, count // 2):
        found = dot(grad_hidden[MOST : MOST + own_rows, chunk], normed_c[...], CONTRACT_FIRST)
        grad_weight[chunk, :width] = found.astype(BF16)
    up_leaves = leave(left, piece_count)
    back = dot(grad_hidden[...], held[:, :width])
    if not first:
        got_total.wait()
        back = total[...] + back
    if not last:
        grad_middle[...] = back
    else:
        total[...] = back
        grad_gain[...] = jnp.zeros_like(grad_gain)

        def step(block):
            hat, inverse = normalised(middle[block, :])
            back = gradient[block, :] + norm_back(total[block, :], gain_2[...], hat, inverse)
            grad_middle[block, :] = back
            grad_attn[block, :] = back.astype(BF16)
            if own_block(block, rows):
                grad_gain[...] += jnp.sum(total[block, :] * hat, axis=0, keepdims=True)

        each_block(rows, 64, step)
    for copy in down_leaves + up_leaves:
        copy.wait()


def column_runs(parts, part, begin, width, group_width):
    stop = begin + width
    while begin < stop:
        group = begin // group_width
        end = min(stop, (group + 1) * group_width)
        place = group * parts * group_width + part * group_width + begin % group_width
        yield begin, end, place
        begin = end


def joining(parts, begin, group_width, source, joined):
    rows = joined.shape[0]
    count = source.shape[0]
    width = joined.shape[1] // parts // count
    across = source.shape[2] // width
    for part in range(parts):
        top = begin + part // across * rows
        left = part % across * width
        side = [source[at, top : top + rows, left : left + width] for at in range(count)]
        side = jnp.concatenate(side, axis=1)
        for first, end, place in column_runs(parts, part, 0, count * width, group_width):
            joined[:, place : place + end - first] = side[:, first:end]


def tabulating(begin, source, *others):
    layers = len(others) // 2
    groups, _, small = others[0].shape
    feats = small // GROUP
    own_heads = groups * GROUP // source.shape[0]
    wide = others[layers].shape[1] // 2
    deep = wide // GROUP
    thin = source.shape[1] - begin
    runs = deep // thin
    run_width = layers * own_heads * feats
    for target in others:
        target[...] = jnp.zeros_like(target)
    for layer in range(layers):
        tables, back_tables = others[layer], others[layers + layer]
        for index in range(groups * GROUP):
            group, place = index // GROUP, index % GROUP
            column = (layer * own_heads + index % own_heads) * feats
            across = slice(place * feats, (place + 1) * feats)
            again = slice(small + place * feats, small + (place + 1) * feats)
            for part in range(4):
                for run in range(runs):
                    top = part * wide + place * deep + run * thin
                    down = slice(top, top + thin)
                    if part < 2:
                        at = run * run_width + column
                        value = source[index // own_heads, begin : begin + thin, at : at + feats]
                    else:
                        value = jnp.full((thin, feats), -0.5, BF16)
                    tables[group, down, across] = value
                    if part < 2:
                        value = value if part < 1 else jnp.ones((thin, feats), BF16)
                        back_tables[group, down, across] = value
                        back_tables[group, down, again] = value


def parting(parts, group_width, pieces, gains, *others):
    if gains:
        gain, *others = others
    *sources, target = others
    count, rows, all_width = target.shape
    if gains:
        rows -= GAIN_ROWS
        left, done = gain[...], 0
        for _ in range(3):
            part = left.astype(BF16)
            left = left - part.astype(F32)
            for at in range(count):
                target[at, rows + done : rows + done + gains, :] = part
            done += gains
        target[:, rows + done :, :] = jnp.zeros((count, GAIN_ROWS - done, all_width), BF16)
    width = all_width // parts
    each = len(sources) // pieces
    starts = [0]
    for piece in range(pieces - 1):
        starts.append(starts[-1] + sources[piece * each].shape[1])
    for part in range(parts):
        for at in range(count):
            runs = []
            for begin, end, place in column_runs(parts, part, at * width, width, group_width):
                piece = max(at for at in range(pieces) if starts[at] <= place)
                run = slice(place - starts[piece], place - starts[piece] + end - begin)
                mine = sources[piece * each : (piece + 1) * each]
                total = mine[0][:, run].astype(F32)
                for source in mine[1:]:
                    total = total + source[:, run].astype(F32)
                runs.append(total)
            total = runs[0] if len(runs) == 1 else jnp.concatenate(runs, axis=1)
            target[at, :rows, part * width : (part + 1) * width] = total.astype(target.dtype)


def finishing(parts, gains, turned, *others):
    if gains:
        *others, gain_out = others
        total = 0.0
        first = others[0]
        rows = first.shape[1] - GAIN_ROWS
        for at in range(first.shape[0]):
            for part in range(3):
                begin = rows + part * gains
                total = total + first[at, begin : begin + gains, :].astype(F32)
        gain_out[...] = total
    sources, targets = others[: -len(parts)], others[-len(parts) :]
    rows = targets[0].shape[-1 if turned else -2]
    for layer, source in enumerate(sources):
        begin = 0
        for target, count in zip(targets, parts):
            for part in range(count):
                width = target.shape[-2 if turned else -1]
                run = slice(begin, begin + width)
                total = source[0, :rows, run].astype(F32)
                for at in range(1, source.shape[0]):
                    total = total + source[at, :rows, run].astype(F32)
                if turned:
                    target[layer] = total.T
                elif count > 1:
                    target[layer, part] = total
                else:
                    target[layer] = total
                begin += width


def turning(cosine_in, sine_in, ids_in, cosine, sine, ids_column):
    half = cosine_in.shape[0]
    down = cosine_in[...].T
    across = sine_in[...].T
    for head in range(cosine.shape[1] // (2 * half)):
        for part in range(2):
            place = slice((2 * head + part) * half, (2 * head + part + 1) * half)
            cosine[:, place] = down
            sine[:, place] = across if part else -across
    ids_column[...] = ids_in[...].T[:, :1].astype(jnp.int32)


def adding_corner(near, far, to_x, to_y):
    half = to_x.shape[0]
    for target, place in ((to_x, slice(0, half)), (to_y, slice(half, 2 * half))):
        target[...] = (near[place, :].astype(F32) + far[place, :].astype(F32)).astype(BF16)


def adding_sides(near_x, far_x, near_y, far_y, from_x, from_y, to_x, to_y):
    half = from_x.shape[0]
    top, bottom = slice(0, half), slice(half, 2 * half)
    for near, far, place, more, target in (
        (near_x, far_x, top, None, to_x),
        (near_x, far_x, bottom, from_y, to_x),
        (near_y, far_y, top, from_x, to_y),
        (near_y, far_y, bottom, None, to_y),
    ):
        total = near[place, :].astype(F32) + far[place, :].astype(F32)
        if more is not None:
            total = total + more[...].astype(F32)
        target[place, :] = total.astype(BF16)


def whole(shape):
    return pl.BlockSpec(
        shape, lambda step, *_: (0,) * len(shape), pipeline_mode=pl.Buffered(buffer_count=1)
    )


def columns(rows, width):
    return pl.BlockSpec((rows, width), lambda step, *_: (0, step))


def leading(shape):
    return pl.BlockSpec(shape, lambda step, *_: (step,) + (0,) * (len(shape) - 1))


def struct(shape, dtype):
    return jax.ShapeDtypeStruct(shape, dtype)


ANYWHERE = pl.BlockSpec(memory_space=pltpu.HBM)


def kernel_call(kernel, steps, in_specs, out_specs, out_shape, scratch, flops, prefetch=0):
    return pl.pallas_call(
        kernel,
        grid_spec=pltpu.PrefetchScalarGridSpec(
            num_scalar_prefetch=prefetch,
            grid=(steps,),
            in_specs=in_specs,
            out_specs=out_specs,
            scratch_shapes=scratch,
        ),
        out_shape=out_shape,
        compiler_params=pltpu.CompilerParams(vmem_limit_bytes=VMEM_BYTES),
        cost_estimate=pl.CostEstimate(flops=flops, bytes_accessed=flops // 600, transcendentals=0),
    )


def run_attention_forward(state, gains, pieces, places, table, *, tables, ids, scale):
    rows, width = state.shape
    wide = tables[0].shape[1]
    groups, deep, small = table.shape
    blocks = rows // QUERY_ROWS
    return kernel_call(
        functools.partial(attention_forward, scale, len(pieces)),
        groups,
        [
            whole((rows, width)),
            whole((1, width)),
            whole((1, width)),
            leading((1, deep, small)),
            whole((rows, wide)),
            whole((rows, wide)),
            whole((rows, 1)),
            whole((blocks, 1, KEY_ROWS)),
            *[ANYWHERE for _ in pieces],
        ],
        [
            ANYWHERE,
            whole((rows, width)),
            columns(rows, wide),
            columns(rows, wide),
            columns(rows, wide),
            columns(rows, wide),
            whole((rows, width)),
            whole((rows, width)),
        ],
        [
            struct((width, 4 * width), BF16),
            struct((rows, width), BF16),
            struct((rows, width), F32),
            struct((rows, width), F32),
            struct((rows, width), BF16),
            struct((rows, width), BF16),
            struct((rows, width), F32),
            struct((rows, width), BF16),
        ],
        [
            pltpu.VMEM((groups, width, 4 * wide), BF16),
            pltpu.VMEM((rows, width), F32),
            pltpu.VMEM((rows, 3 * wide), F32),
            pltpu.VMEM((2 * rows, deep), BF16),
            pltpu.VMEM((2 * rows, small), BF16),
            pltpu.SemaphoreType.DMA((groups, len(pieces))),
            pltpu.SemaphoreType.DMA((groups,)),
        ],
        FORWARD_COST,
        1,
    )(places, state, gains[0], gains[1], table, *tables, *ids, *pieces)


def run_attention_backward(
    groups,
    carried,
    *,
    grad_middle,
    branch,
    state,
    gain,
    weights,
    places,
    table,
    back_table,
    tables,
    ids,
    kept,
    scale,
):
    rows, width = state.shape
    wide = tables[0].shape[1]
    all_groups, deep, small = table.shape
    first, last = groups[0] == 0, groups[-1] == all_groups - 1
    count = len(groups)
    normed_a, query, key, value, mixed = kept
    own_rows = rows - 2 * MOST
    blocks = rows // QUERY_ROWS
    copied = [branch, weights, mixed, query, key, value, normed_a, *tables]
    ending = [grad_middle, state, gain] if last else []
    split = places.shape[0] > 1
    halves = 1 + split
    return kernel_call(
        functools.partial(attention_backward, first, last, scale, groups, split),
        1,
        [
            *[ANYWHERE] * (len(copied) + (not first)),
            *([whole((rows, width)), whole((rows, width)), whole((1, width))] if last else []),
            pl.BlockSpec((count, deep, small), lambda *_: (groups[0] // count, 0, 0)),
            pl.BlockSpec((count,) + back_table.shape[1:], lambda *_: (groups[0] // count, 0, 0)),
            whole((rows, 1)),
            whole((blocks, 1, KEY_ROWS)),
        ],
        [
            *([whole((rows, width)), whole((1, width))] if last else [whole((rows, width))]),
            *[ANYWHERE] * halves,
        ],
        [
            struct((rows, width), F32),
            *([struct((1, width), F32)] if last else []),
            *[struct((width // halves, count * 4 * wide), BF16)] * halves,
        ],
        [
            pltpu.VMEM((rows, width), BF16),
            pltpu.VMEM((count, width, 4 * wide), BF16),
            pltpu.VMEM((count, own_rows, wide), BF16),
            pltpu.VMEM((count, rows, wide), F32),
            pltpu.VMEM((count, rows, wide), F32),
            pltpu.VMEM((count, rows, wide), BF16),
            pltpu.VMEM((own_rows, width), BF16),
            pltpu.VMEM((rows, wide), F32),
            pltpu.VMEM((rows, wide), F32),
            pltpu.VMEM((rows, width), F32),
            pltpu.VMEM((count, width, 4 * wide), BF16),
            pltpu.VMEM((rows, wide), BF16),
            pltpu.VMEM((2 * rows, deep), BF16),
            pltpu.VMEM((2 * rows, small), F32),
            pltpu.VMEM((2 * rows, small), F32),
            pltpu.VMEM((rows, wide), F32),
            pltpu.VMEM((2 * rows, 2 * small), BF16),
            pltpu.VMEM((rows, 3 * wide), BF16),
            pltpu.SemaphoreType.DMA((5 + 6 * count,)),
            pltpu.SemaphoreType.DMA((count,) + places.shape),
        ],
        BACKWARD_COST // 3 * count,
        1,
    )(
        places,
        *copied,
        *([] if first else [carried]),
        *ending,
        table,
        back_table,
        *ids,
    )


def run_feed_forward(carried, normed_c, pieces):
    rows, width = carried.shape
    count = sum(piece.shape[0] for piece in pieces)
    return kernel_call(
        functools.partial(feed_forward, len(pieces)),
        1,
        [ANYWHERE] * (2 + len(pieces)),
        [ANYWHERE] * 3,
        [
            struct((rows, count), BF16),
            struct((rows, count), BF16),
            struct((rows, width), F32),
        ],
        [
            pltpu.VMEM((count, 2 * width), BF16),
            pltpu.VMEM((rows, width), F32),
            pltpu.VMEM((rows, width), BF16),
            pltpu.VMEM((rows, count), F32),
            pltpu.VMEM((rows, count), BF16),
            pltpu.VMEM((rows, count), BF16),
            pltpu.SemaphoreType.DMA((len(pieces) + 2,)),
            pltpu.SemaphoreType.DMA((2 * len(hidden_chunks(count)) + 1,)),
        ],
        FORWARD_COST // 3,
    )(carried, normed_c, *pieces)


def kept_stretches(near_kept, far_kept, corner_kept):
    side, corner = near_kept[0].shape[1], corner_kept[0].shape[1] // 2
    return [
        (near_kept[:2], 0, side),
        (far_kept[:2], 0, side),
        (corner_kept[:2], 0, corner),
        (corner_kept[:2], corner, corner),
    ]


def run_feed_back(gradient, middle, gain, normed_c, stretches, pieces, places, carried, last):
    rows, width = middle.shape
    count = sum(piece.shape[0] for piece in pieces)
    first = carried is None
    kept = [array for arrays, _, _ in stretches for array in arrays]
    segments = [(column, size) for _, column, size in stretches]
    arrivals = 2 + not_first(first) + 2 * len(pieces) + len(kept)
    return kernel_call(
        functools.partial(feed_back, first, last, segments, len(pieces)),
        1,
        [
            ANYWHERE,
            whole((rows, width)),
            whole((1, width)),
            *[ANYWHERE] * (1 + len(kept) + not_first(first) + len(pieces)),
        ],
        [
            ANYWHERE,
            whole((rows, width)),
            *([whole((1, width)), whole((rows, width))] if last else []),
        ],
        [
            struct((count, 2 * width), BF16),
            struct((rows, width), F32),
            *([struct((1, width), F32), struct((rows, width), BF16)] if last else []),
        ],
        [
            pltpu.VMEM((count, 2 * width), BF16),
            pltpu.VMEM((rows, width), F32),
            pltpu.VMEM((rows - 2 * MOST, width), BF16),
            pltpu.VMEM((rows - 2 * MOST, count), BF16),
            pltpu.VMEM((rows, count), BF16),
            pltpu.VMEM((rows, width), F32),
            pltpu.VMEM((rows, width), BF16),
            pltpu.VMEM((rows, count), BF16),
            pltpu.VMEM((count, 2 * width), BF16),
            pltpu.SemaphoreType.DMA((arrivals,)),
            pltpu.SemaphoreType.DMA((2 * len(pieces),)),
        ],
        FORWARD_COST // 2,
        1,
    )(
        places,
        gradient,
        middle,
        gain,
        normed_c,
        *kept,
        *([] if first else [carried]),
        *pieces,
    )


def not_first(first):
    return 0 if first else 1


HEAD_DEVICES = 4
CHUNK = 512
GAIN_ROWS = 16
X, Y, CORE = 2, 4, 1
FORWARD_COST = 29_000_000_000
BACKWARD_COST = 40_000_000_000


def hop(values, bit):
    count = lax.axis_size("dp")
    return lax.ppermute(values, "dp", [(i, i ^ bit) for i in range(count)])


def exchange(values):
    return lax.all_to_all(values, "head", split_axis=0, concat_axis=0, tiled=True)


def together(*values):
    return lax.optimization_barrier(values)


def by_permutes():
    return lax.axis_size("dp") == 8 and lax.axis_size("head") == HEAD_DEVICES


def group_width(parts, width, wide):
    return wide if parts == 4 else width


def join_columns(source, parts, begin, rows, width, wide):
    count = source.shape[0]
    return kernel_call(
        functools.partial(joining, parts, begin, group_width(parts, count * width, wide)),
        1,
        [whole(source.shape)],
        whole((rows, parts * count * width)),
        struct((rows, parts * count * width), BF16),
        [],
        1_000_000,
    )(source)


def feature_tables(source, begin, shapes):
    return kernel_call(
        functools.partial(tabulating, begin),
        1,
        [whole(source.shape)],
        [whole(shape) for shape in shapes],
        [struct(shape, BF16) for shape in shapes],
        [],
        1_000_000,
    )(source)


def block_of(rows, columns_all, index):
    return pl.BlockSpec((rows, columns_all), lambda *_: (index, 0))


def part_columns(pieces, parts, wide, gain=None):
    rows = pieces[0][-1].shape[0]
    columns_all = sum(piece[0].shape[1] for piece in pieces)
    gains = 0 if gain is None else gain.shape[0]
    shape = (
        HEAD_DEVICES,
        rows + (GAIN_ROWS if gains else 0),
        columns_all // HEAD_DEVICES,
    )
    return kernel_call(
        functools.partial(
            parting, parts, group_width(parts, columns_all // parts, wide), len(pieces), gains
        ),
        1,
        [
            *([whole(gain.shape)] if gains else []),
            *[block_of(rows, source.shape[1], 0) for piece in pieces for source in piece],
        ],
        whole(shape),
        struct(shape, BF16),
        [],
        1_000_000,
    )(*([gain] if gains else []), *[source for piece in pieces for source in piece])


def finish(sources, parts, rows, gains=0, turned=False):
    all_width = sources[0].shape[2]
    width = all_width // sum(parts)
    shapes = [
        (len(sources), count, rows, width) if count > 1 else (len(sources), rows, width)
        for count in parts
    ]
    if turned:
        shapes = [(len(sources), width, rows) for _ in parts]
    if gains:
        shapes.append((gains, all_width))
    return kernel_call(
        functools.partial(finishing, parts, gains, turned),
        1,
        [whole(source.shape) for source in sources],
        [whole(shape) for shape in shapes],
        [struct(shape, F32) for shape in shapes],
        [],
        1_000_000,
    )(*sources)


def next_chips(own):
    return hop(own, X), hop(own, Y), hop(own, CORE)


def halves_to_pass(over_x, over_y):
    half = over_x.shape[0] // 2
    return over_x[:half], over_y[half:]


def chip_across(passed):
    to_y, to_x = passed
    return hop(to_y, Y), hop(to_x, X)


def other_core(pieces):
    return tuple(hop(piece, CORE) for piece in pieces)


def piece_places(rows, order=range(10)):
    own = lax.axis_index("dp")
    bits = [(0, 0), (X, 0), (Y, 0), (X | Y, 0), (X | Y, rows // 2)]
    places = [(own ^ (bit | core)) * rows + begin for core in (0, CORE) for bit, begin in bits]
    return jnp.stack([places[at] for at in order]).astype(jnp.int32)


def block_places(rows):
    own = lax.axis_index("dp")
    return jnp.stack(
        [(own ^ (bit | core)) * rows for core in (CORE, 0) for bit in (0, X, Y, X | Y)]
    ).astype(jnp.int32)


class Reduction:
    def __init__(self, far, slow):
        self.slow, self.stage, self.left = slow, 0, 1
        self.came = hop(far, CORE)

    def operands(self):
        rows = self.near.shape[0] // 4
        half = rows // 2
        if self.stage == 0:
            self.far = self.came
            return [(self.near, rows, 3), (self.far, rows, 3)], half
        sides = [(array, rows, at) for at in (1, 2) for array in (self.near, self.far)]
        return sides + [(array, half, 0) for array in self.came], rows

    def send(self):
        to_x, to_y = self.sent
        self.came = hop(to_x, X), hop(to_y, Y)
        self.stage += 1
        self.left = self.slow[self.stage - 1]

    def arrays(self):
        return [self.near, self.far, *self.came]


def prepare(reductions):
    arrays, in_specs, out_specs, shapes = [], [], [], []
    for reduction in reductions:
        operands, out_rows = reduction.operands()
        width = reduction.near.shape[1]
        for array, rows, at in operands:
            arrays.append(array)
            in_specs.append(block_of(rows, width, at))
        out_specs += [whole((out_rows, width))] * 2
        shapes += [struct((out_rows, width), BF16)] * 2
    sent = kernel_call(
        functools.partial(adding, [reduction.stage for reduction in reductions]),
        1,
        in_specs,
        out_specs,
        shapes,
        [],
        1_000_000,
    )(*arrays)
    for index, reduction in enumerate(reductions):
        reduction.sent = sent[2 * index : 2 * index + 2]


class Sharing:
    def __init__(self, reductions, parts, wide, slow):
        self.reductions, self.parts, self.wide, self.slow = reductions, parts, wide, slow
        self.stage, self.left, self.came, self.gain = 0, 0, (), None

    def prepare(self):
        pieces = [reduction.arrays() for reduction in self.reductions]
        self.sent = part_columns(pieces, self.parts, self.wide, self.gain)

    def send(self):
        self.came = exchange(self.sent)
        self.stage, self.left = 1, self.slow


class Traffic:
    def __init__(self):
        self.moving = []

    def slot(self, values):
        ready = []
        for item in self.moving:
            item.left -= 1
            if item.left <= 0:
                ready.append(item)
        values, came = together(values, [item.came for item in ready])
        for item, arrived in zip(ready, came):
            item.came = arrived
        sending = []
        for item in ready:
            if isinstance(item, Sharing):
                if item.stage == 0 and all(r.stage == 3 for r in item.reductions):
                    sending.append(item)
            elif item.stage < 2:
                sending.append(item)
            else:
                item.stage = 3
        for item in ready:
            if isinstance(item, Sharing) and item.stage == 0 and item not in sending:
                if all(r.stage == 3 for r in item.reductions):
                    sending.append(item)
        reductions = [item for item in sending if isinstance(item, Reduction)]
        if reductions:
            prepare(reductions)
        for item in sending:
            if isinstance(item, Sharing):
                item.prepare()
        values, sent = together(values, [item.sent for item in sending])
        for item, prepared in zip(sending, sent):
            item.sent = prepared
            item.send()
        self.moving = [
            item
            for item in self.moving
            if item.stage < (1 if isinstance(item, Sharing) else 3) or item.left > 0
        ]
        return values


def grouped_columns(values, parts, wide):
    rows = values.shape[0]
    return values.reshape(rows, parts, -1, wide).swapaxes(1, 2).reshape(rows, -1)


def over_heads(part, parts, wide):
    rows = part.shape[0]
    if parts == 4:
        part = part.reshape(rows, -1, parts, wide).swapaxes(1, 2)
    part = part.reshape(rows, parts, -1)
    part = lax.psum_scatter(part, "head", scatter_dimension=2, tiled=True)
    return part.swapaxes(0, 1).astype(F32)


def shared_gain(values, bit):
    return values + hop(values, bit)


def with_halo(inputs, cotangent):
    count = lax.axis_size("head")
    both = jnp.concatenate([inputs, cotangent], axis=1)
    before = lax.ppermute(both[-MOST:], "head", [(i, i + 1) for i in range(count - 1)])
    after = lax.ppermute(both[:MOST], "head", [(i + 1, i) for i in range(count - 1)])
    joined = jnp.concatenate([before, both, after], axis=0).astype(F32)
    return joined[:, : inputs.shape[1]], joined[:, inputs.shape[1] :]


def window_ids(segment_ids, own_rows):
    padded = jnp.pad(segment_ids[0], (MOST, MOST), constant_values=-1)
    begin = lax.axis_index("head") * own_rows
    ids = lax.dynamic_slice(padded, (begin,), (own_rows + 2 * MOST,))
    place = jnp.arange(ids.shape[0])
    earlier = (ids[:, None] == ids[None, :]) & (place[None, :] < place[:, None])
    position = jnp.sum(earlier.astype(F32), axis=1)
    used = (ids >= ids[MOST]) & (ids <= ids[MOST + own_rows - 1])
    column = jnp.where(used, ids, -1)
    row = jnp.where(used, ids, -2)
    starts = [
        min(max(b * QUERY_ROWS - MOST, 0), ids.shape[0] - KEY_ROWS)
        for b in range(ids.shape[0] // QUERY_ROWS)
    ]
    rows = jnp.stack([row[start : start + KEY_ROWS] for start in starts])[:, None, :]
    return position, (column, rows)


def rotary_tables(position, ids, head_width):
    halves = head_width // 2
    frequency = jnp.exp(jnp.arange(halves, dtype=F32) * (-2.0 * math.log(10000.0) / head_width))
    angles = frequency[:, None] * position[None, :]
    column, rows = ids
    count = position.shape[0]
    wide = (count, GROUP * head_width)
    spread = jnp.broadcast_to(column.astype(F32)[None], (8, count))
    cosine, sine, column = kernel_call(
        turning,
        1,
        [whole(angles.shape)] * 2 + [whole(spread.shape)],
        [whole(wide), whole(wide), whole((count, 1))],
        [struct(wide, F32), struct(wide, F32), struct((count, 1), jnp.int32)],
        [],
        1_000_000,
    )(jnp.cos(angles), jnp.sin(angles), spread)
    return (cosine, sine), (column, rows)


def body(
    inputs,
    segment_ids,
    features,
    norm_gain,
    query_key_value,
    output_weight,
    up_weight,
    down_weight,
    cotangent,
):
    layer_count = norm_gain.shape[0]
    own_rows = inputs.shape[0]
    head_width = features.shape[3]
    feature_count = features.shape[2]
    scale = head_width ** (-0.25)
    own_place = slice(MOST, MOST + own_rows)

    in_rows, part_width = output_weight.shape[1:]
    groups = inputs.shape[1] // (GROUP * head_width)
    wide, small = GROUP * head_width, GROUP * feature_count
    table_shapes = [(groups, 4 * wide, small)] * layer_count + [
        (groups, 2 * wide, 2 * small)
    ] * layer_count
    chunks = []
    for layer in range(layer_count):
        chunks.append((4, *query_key_value[layer], output_weight[layer]))
        chunks.append((2, up_weight[layer], down_weight[layer]))
    stored = []
    if by_permutes():
        attention_places = piece_places(in_rows)
        grad_places = block_places(in_rows)
        gain_rows = [[norm_gain[layer, at][None] for at in range(2)] for layer in range(layer_count)]
        feed_places = piece_places(up_weight.shape[1], (0, 1, 2, 5, 6, 7, 3, 4, 8, 9))
        feature_rows = jnp.moveaxis(features, 3, 0).reshape(4, head_width // 4, -1)
        feature_rows = jnp.concatenate(list(feature_rows), axis=1)

        def join(index, came, begin=0):
            parts, *weights = chunks[index]
            return join_columns(came, parts, begin, *weights[-1].shape, wide)

        def gathered_columns(sent):
            return lax.all_gather(sent, "head", axis=0, tiled=False)

        sent = jnp.concatenate([jnp.concatenate(chunks[0][1:], axis=1), feature_rows])
        sent = jnp.broadcast_to(sent[None], (HEAD_DEVICES,) + sent.shape)
        sent, inputs, cotangent = together(sent, inputs, cotangent)
        came = exchange(sent)
        state, gradient = with_halo(inputs, cotangent)
        position, ids = window_ids(segment_ids, own_rows)
        tables, ids = rotary_tables(position, ids, head_width)
        both = []
        for layer in range(1, layer_count):
            q, k, v, o = chunks[2 * layer][1:]
            both.append(
                jnp.concatenate(
                    [
                        jnp.concatenate(pair, axis=1)
                        for pair in ((q, k), (v, o), chunks[2 * layer + 1][1:])
                    ]
                )
            )
        first_feed = jnp.concatenate(chunks[1][1:], axis=1)
        came, state, gradient, tables, ids, first_feed, gain_rows, attention_places = together(
            came, state, gradient, tables, ids, first_feed, gain_rows, attention_places
        )
        attend = functools.partial(run_attention_forward, tables=tables, ids=ids, scale=scale)
        own = join(0, came)
        came_feed = gathered_columns(first_feed)
        over_x, over_y, over_core = next_chips(own)
        made = feature_tables(came, in_rows, table_shapes)
        over_x, over_y, over_core, made, both = together(over_x, over_y, over_core, made, both)
        blocks, back_blocks = made[:layer_count], made[layer_count:]
        passed = halves_to_pass(over_x, over_y)
        across = chip_across(passed)
        own_feed = join(1, came_feed)
        for layer in range(layer_count):
            more = layer + 1 < layer_count
            near = (own, over_x, over_y) + tuple(across)
            far = (over_core,) + other_core(near[1:])
            attention_pieces = near + far
            own = own_feed
            state, own, sent = together(state, own, both[layer] if more else ())
            over_x, over_y, over_core = next_chips(own)
            came = gathered_columns(sent) if more else ()
            weights, *kept, middle, normed_c = attend(
                state,
                gain_rows[layer],
                attention_pieces,
                attention_places,
                blocks[layer],
            )

            middle, over_x, over_y, over_core = together(middle, over_x, over_y, over_core)
            sides = own, over_x, over_y
            passed = halves_to_pass(over_x, over_y)
            carried, passed = together(middle, passed)
            across = chip_across(passed)
            far_sides = (over_core,) + other_core(sides[1:])
            near_kept = run_feed_forward(carried, normed_c, sides)

            carried, across, far_sides = together(near_kept[2], across, far_sides)
            far_across = other_core(across)
            if more:
                carried, came = together(carried, came)
                carried, own = together(carried, join(2 * layer + 2, came))
                over_x, over_y, over_core = next_chips(own)
            last_pieces = across + far_across
            feed_pieces = sides, far_sides, across, far_across
            if not more:
                rest = run_feed_forward(carried, normed_c, far_sides + last_pieces)
                side = near_kept[0].shape[1]
                stretches = [(near_kept[:2], 0, side), (rest[:2], 0, rest[0].shape[1])]
                stored.append((state, weights, kept, middle, normed_c, stretches, feed_pieces))
                state = rest[2]
                break
            far_kept = run_feed_forward(carried, normed_c, far_sides)

            carried = far_kept[2]
            if more:
                carried, over_x, over_y, over_core = together(carried, over_x, over_y, over_core)
                passed = halves_to_pass(over_x, over_y)
                carried, passed = together(carried, passed)
                across = chip_across(passed)
            last_kept = run_feed_forward(carried, normed_c, last_pieces)
            stretches = kept_stretches(near_kept, far_kept, last_kept)
            stored.append((state, weights, kept, middle, normed_c, stretches, feed_pieces))
            state = last_kept[2]
            if more:
                state, across, came = together(state, across, came)
                own_feed = join(2 * layer + 3, came, 2 * in_rows)
    else:
        gain_rows = [[norm_gain[layer, at][None] for at in range(2)] for layer in range(layer_count)]
        state, gradient = with_halo(inputs, cotangent)
        position, ids = window_ids(segment_ids, own_rows)
        tables, ids = rotary_tables(position, ids, head_width)
        attend = functools.partial(run_attention_forward, tables=tables, ids=ids, scale=scale)
        all_features = lax.all_gather(features, "head", axis=1, tiled=True)
        shaped = all_features.reshape(layer_count, -1, GROUP, feature_count, head_width)
        eye = jnp.eye(GROUP, dtype=BF16)
        block = jnp.einsum("lghmw,hk->lghwkm", shaped, eye).reshape(layer_count, groups, wide, small)
        ones = jnp.kron(eye, jnp.ones((head_width, feature_count), BF16))
        ones = jnp.broadcast_to(ones, block.shape)
        blocks = jnp.concatenate([block, block, ones * -0.5, ones * -0.5], axis=2)
        back_blocks = jnp.concatenate([block, ones], axis=2)
        back_blocks = jnp.concatenate([back_blocks, back_blocks], axis=3)
        owned = []
        for parts, *weights in chunks:
            rows = weights[-1].shape[0]
            joined = jnp.stack(weights)
            joined = lax.all_gather(joined, "head", axis=2, tiled=True)
            joined = lax.all_gather(joined, "dp", axis=1, tiled=True)
            joined = joined.swapaxes(0, 1).reshape(joined.shape[1], -1)
            owned.append(grouped_columns(joined, parts, wide) if parts == 4 else joined)
        middle_row = inputs.shape[1] // 2
        attention_places = jnp.array([0, middle_row], jnp.int32)
        size = up_weight.shape[1] * lax.axis_size("dp") // 8
        feed_places = jnp.array([0, 4 * size, 3 * size, 7 * size], jnp.int32)
        for layer in range(layer_count):
            own_attention, own_feed = owned[2 * layer], owned[2 * layer + 1]
            weights, *kept, middle, normed_c = attend(
                state,
                gain_rows[layer],
                (own_attention[:middle_row], own_attention[middle_row:]),
                attention_places,
                blocks[layer],
            )
            size = own_feed.shape[0] // 8
            feed_pieces = [
                (own_feed[begin * size : end * size],) for begin, end in ((0, 3), (4, 7), (3, 4), (7, 8))
            ]
            near_kept = run_feed_forward(middle, normed_c, feed_pieces[0])
            far_kept = run_feed_forward(near_kept[2], normed_c, feed_pieces[1])
            last_kept = run_feed_forward(far_kept[2], normed_c, feed_pieces[2] + feed_pieces[3])
            stretches = kept_stretches(near_kept, far_kept, last_kept)
            stored.append((state, weights, kept, middle, normed_c, stretches, feed_pieces))
            state = last_kept[2]
    outputs = state[own_place].astype(BF16)

    gains = [None] * layer_count
    shares = [None] * layer_count
    traffic = Traffic()
    summing = []
    for layer in reversed(range(layer_count)):
        before, weights, kept, middle, normed_c, stretches, feed_pieces = stored[layer]
        feed = (middle, gain_rows[layer][1], normed_c)
        attend_back = functools.partial(
            run_attention_backward,
            state=before,
            gain=gain_rows[layer][0],
            weights=weights,
            table=blocks[layer],
            back_table=back_blocks[layer],
            tables=tables,
            ids=ids,
            kept=kept,
            scale=scale,
        )
        if layer > 0 or not by_permutes():
            pieces = [piece for part in feed_pieces for piece in part]
            feed_grad, grad_middle, gain_c, branch = run_feed_back(
                gradient, *feed, stretches, pieces, feed_places, None, True
            )
            feed_part = lax.psum_scatter(feed_grad, "dp", scatter_dimension=0, tiled=True)
            gradient, gain_a, *grad = attend_back(
                tuple(range(groups)),
                None,
                grad_middle=grad_middle,
                branch=branch,
                places=grad_places if by_permutes() else jnp.zeros((1,), jnp.int32),
            )
            if by_permutes():
                gains[layer] = jnp.concatenate([gain_a, gain_c])
                attention_sum = Reduction(grad[0], (1, 1))
                attention_sum.near, attention_sum.left = grad[1], 2
                traffic.moving.append(attention_sum)
                summing.append((layer, feed_part, attention_sum))
                continue
            [grad] = grad
            attention_part = lax.psum_scatter(grad, "dp", scatter_dimension=0, tiled=True)
            gains[layer] = jnp.concatenate([gain_a, gain_c])
            shares[layer] = over_heads(feed_part, 2, wide), over_heads(attention_part, 4, wide)
            continue
        relative = [
            jnp.array(begins_of(feed_pieces[at] + feed_pieces[2 + at])[:-1], jnp.int32) for at in (0, 1)
        ]
        gradient = traffic.slot(gradient)
        feed_far, carried = run_feed_back(
            gradient,
            *feed,
            [stretches[1], stretches[3]],
            feed_pieces[1] + feed_pieces[3],
            relative[1],
            None,
            False,
        )
        carried, feed_far = traffic.slot((carried, feed_far))
        feed_sum = Reduction(feed_far, (1, 1))
        traffic.moving.append(feed_sum)
        feed_near, grad_middle, gain_c, branch = run_feed_back(
            gradient,
            *feed,
            [stretches[0], stretches[2]],
            feed_pieces[0] + feed_pieces[2],
            relative[0],
            carried,
            True,
        )
        feed_sum.near = feed_near
        feed_share = Sharing([feed_sum], 2, wide, 2)
        traffic.moving.append(feed_share)
        carried, attention_sums = None, []
        for call_groups in (tuple(range(groups - 1)), (groups - 1,)):
            if attention_sums:
                for index, (later, feed_part, attention_sum) in enumerate(summing):
                    carried, feed_part = together(carried, feed_part)
                    parted = part_columns([[feed_part]], 2, wide)
                    carried, parted = together(carried, parted)
                    parted = lax.psum_scatter(parted, "head", scatter_dimension=0, tiled=True)
                    summing[index] = later, parted, attention_sum
            branch, grad_middle, carried = traffic.slot((branch, grad_middle, carried))
            if attention_sums:
                traffic.moving.append(attention_sums[-1])
                for later, parted, attention_sum in summing:
                    attention_part = part_columns([attention_sum.arrays()], 4, wide)
                    carried, attention_part = together(carried, attention_part)
                    shares[later] = parted, attention_part
            carried, *gain_a, far, near = attend_back(
                call_groups, carried, grad_middle=grad_middle, branch=branch, places=grad_places
            )
            carried, far, near = together(carried, far, near)
            attention_sums.append(Reduction(far, (1, 1)))
            attention_sums[-1].near = near
        gradient = carried
        gains[layer] = jnp.concatenate([*gain_a, gain_c])
        traffic.moving.append(attention_sums[-1])
        attention_share = Sharing(attention_sums, 4, wide, 1)
        traffic.moving.append(attention_share)
        shares[layer] = feed_share, attention_share
    if by_permutes():
        gain_all = jnp.concatenate(gains)
        input_grad = gradient[own_place]
        gain_all = traffic.slot(gain_all)
        gain_all = shared_gain(shared_gain(gain_all, CORE), X)
        gain_all = traffic.slot(gain_all)
        gain_all, outputs, input_grad = together(gain_all, outputs, input_grad)
        gain_all = shared_gain(gain_all, Y)
        gain_all, parted, attention_parts = together(
            gain_all, [share[0] for share in shares[1:]], [share[1] for share in shares[1:]]
        )
        attention_parts = [
            lax.psum_scatter(part, "head", scatter_dimension=0, tiled=True)
            for part in attention_parts
        ]
        attention_share.gain = gain_all
        parted = traffic.slot(parted)
        turned = finish([shares[0][0].came] + parted, (1, 1), up_weight.shape[1], turned=True)
        up_grad, down_grad = traffic.slot(turned)
        up_grad, down_grad = up_grad.swapaxes(1, 2), down_grad.swapaxes(1, 2)
        assert not traffic.moving
        qkv_grad, out_grad, gain_total = finish(
            [shares[0][1].came] + attention_parts, (3, 1), in_rows, 2 * layer_count
        )
        gain_total = gain_total.reshape(layer_count, 2, -1)
    else:
        gain_total = lax.psum(jnp.stack(gains), ("dp", "head"))
        input_grad = gradient[own_place]
        results = [(a[:3], a[3], f[0], f[1]) for f, a in shares]
        qkv_grad, out_grad, up_grad, down_grad = (
            jnp.stack(list(kind)) for kind in zip(*results)
        )
    return (
        outputs,
        input_grad,
        gain_total[:, 0],
        gain_total[:, 1],
        qkv_grad,
        out_grad,
        up_grad,
        down_grad,
    )


def solution(mesh):
    in_specs = (
        P(("dp", "head"), None),
        P("dp", None),
        P(None, "head", None, None),
        P(),
        P(None, None, "dp", "head"),
        P(None, "dp", "head"),
        P(None, "dp", "head"),
        P(None, "dp", "head"),
        P(("dp", "head"), None),
    )
    out_specs = (
        P(("dp", "head"), None),
        P(("dp", "head"), None),
        P(),
        P(),
        P(None, None, "dp", "head"),
        P(None, "dp", "head"),
        P(None, "dp", "head"),
        P(None, "dp", "head"),
    )
    return jax.shard_map(body, mesh=mesh, in_specs=in_specs, out_specs=out_specs, check_vma=False)
```

```python
import functools
import math

import jax
import jax.numpy as jnp
from jax import lax
from jax.experimental import pallas as pl
from jax.experimental.pallas import tpu as pltpu
from jax.sharding import PartitionSpec as P

MOST = 64
EPSILON = 1e-05
QUERY_ROWS = 128
KEY_ROWS = QUERY_ROWS + 2 * MOST
GROUP = 4
VMEM_BYTES = 60 * 2**20

BF16 = jnp.bfloat16
F32 = jnp.float32
CONTRACT_LAST = (((1,), (1,)), ((), ()))
CONTRACT_FIRST = (((0,), (0,)), ((), ()))
CONTRACT_MIDDLE = (((1,), (0,)), ((), ()))

TAIL_SCALE = 0.3275911 / math.sqrt(2.0)
TAIL_TERMS = (1.061405429, -1.453152027, 1.421413741, -0.284496736, 0.254829592)


def dot(left, right, dims=CONTRACT_MIDDLE):
    return lax.dot_general(left, right, dims, preferred_element_type=F32)


def gelu_and_slope(hidden):
    bell = jnp.exp(hidden * hidden * -0.5)
    below = 1.0 + jnp.abs(hidden) * TAIL_SCALE
    guess = pl.reciprocal(below, approx=True)
    inverse = guess * (2.0 - below * guess)
    tail = 0.5 * TAIL_TERMS[0]
    for term in TAIL_TERMS[1:]:
        tail = tail * inverse + 0.5 * term
    tail = tail * inverse * bell
    cumulative = jnp.where(hidden > 0.0, 1.0 - tail, tail)
    return hidden * cumulative, cumulative + hidden * (bell * (1.0 / math.sqrt(2.0 * math.pi)))


def normalised(values):
    centred = values - jnp.mean(values, axis=-1, keepdims=True)
    inverse = lax.rsqrt(jnp.mean(centred * centred, axis=-1, keepdims=True) + EPSILON)
    return centred * inverse, inverse


def norm_back(grad_out, gain, hat, inverse):
    scaled = grad_out * gain
    first_mean = jnp.mean(scaled, axis=-1, keepdims=True)
    second_mean = jnp.mean(scaled * hat, axis=-1, keepdims=True)
    return inverse * (scaled - first_mean - hat * second_mean)


def each_block(rows, size, step):
    for block in row_blocks(rows, size):
        step(block)


def own_block(block, rows):
    return MOST <= block.start and block.stop <= rows - MOST


def swap_halves(values, half):
    width = values.shape[-1]
    lane = lax.broadcasted_iota(jnp.int32, values.shape, len(values.shape) - 1)
    ahead = pltpu.roll(values, width - half, 1)
    behind = pltpu.roll(values, half, 1)
    return jnp.where(lane % (2 * half) < half, ahead, behind)


def two_parts(values):
    high = values.astype(BF16)
    return high, (values - high.astype(F32)).astype(BF16)


def row_blocks(rows, size):
    return [slice(begin, begin + size) for begin in range(0, rows, size)]


def spread_parts(rows, target, place):
    width = rows.shape[1]
    for index, part in enumerate((*two_parts(rows), *two_parts(rows * rows))):
        target[place, index * width : (index + 1) * width] = part


def phi_of(parts, table):
    return jnp.exp(dot(parts, table)) * (1.0 / math.sqrt(table.shape[1] // GROUP))


def head_masks(width, dtype):
    lane = lax.broadcasted_iota(jnp.int32, (1, width), 1) // (width // GROUP)
    return [jnp.where(lane == head, 1.0, 0.0).astype(dtype) for head in range(GROUP)]


def spread_heads(values):
    return jnp.concatenate([values * mask for mask in head_masks(values.shape[1], BF16)], axis=0)


def gather_heads(values):
    masks = head_masks(values.shape[-1], F32)
    total = values[0] * masks[0]
    for head in range(1, GROUP):
        total = total + values[head] * masks[head]
    return total


def block_scores(phi_q, phi_k, ids_column, ids_row):
    scores = dot(phi_q, phi_k, CONTRACT_LAST)
    same = (ids_column == ids_row).astype(F32)
    scores = scores.reshape(GROUP, QUERY_ROWS, KEY_ROWS) * same[None]
    totals = jnp.sum(scores, axis=-1, keepdims=True)
    inverse = jnp.where(totals > 0.0, 1.0 / totals, 0.0)
    return scores * inverse, inverse, same


def query_blocks(rows):
    for index, block in enumerate(row_blocks(rows, QUERY_ROWS)):
        begin = min(max(block.start - MOST, 0), rows - KEY_ROWS)
        yield index, block, slice(begin, begin + KEY_ROWS)


def attention_forward(
    scale,
    piece_count,
    places,
    state,
    gain_1,
    gain_2,
    table,
    cosine,
    sine,
    ids_column,
    ids_row,
    *others,
):
    pieces = others[:piece_count]
    weights_out, normed_a, query, key, value, mixed, middle, normed_c, *others = others[piece_count:]
    weights, total, projected, parts, phi, arrived, leaving = others
    group = pl.program_id(0)
    groups = weights.shape[0]
    rows = state.shape[0]
    wide = query.shape[1]
    deep = weights.shape[2]
    half = cosine.shape[1] // GROUP // 2

    def columns_of(at):
        return pl.ds(at * deep, deep)

    def arriving_at(at):
        for index, piece in enumerate(pieces):
            place = pl.ds(pl.multiple_of(places[index], 16), piece.shape[0])
            yield pltpu.make_async_copy(
                piece.at[:, columns_of(at)], weights.at[at, place, :], arrived.at[at, index]
            )

    def leaving_at(at):
        return pltpu.make_async_copy(
            weights.at[at], weights_out.at[:, columns_of(at)], leaving.at[at]
        )

    @pl.when(group == 0)
    def _():
        for at in range(groups):
            for copy in arriving_at(at):
                copy.start()

        def step(block):
            hat, _ = normalised(state[block, :])
            normed_a[block, :] = (hat * gain_1[...]).astype(BF16)
            total[block, :] = state[block, :]

        each_block(rows, 64, step)

    for at in range(groups):

        @pl.when(group == at)
        def _(at=at):
            for copy in arriving_at(at):
                copy.wait()
            leaving_at(at).start()

    projected[...] = dot(normed_a[...], weights[group, :, : 3 * wide])
    for block in row_blocks(rows, 64):
        for part, held in enumerate((query, key)):
            values = projected[block, part * wide : (part + 1) * wide]
            turned = values * cosine[block, :] + swap_halves(values, half) * sine[block, :]
            turned = turned * scale
            held[block, :] = turned
            spread_parts(turned, parts, slice(part * rows + block.start, part * rows + block.stop))
        value[block, :] = projected[block, 2 * wide :].astype(BF16)
    phi[...] = phi_of(parts[...], table[0]).astype(BF16)

    for index, block, keys in query_blocks(rows):
        scores, _, _ = block_scores(
            spread_heads(phi[block, :]),
            phi[rows + keys.start : rows + keys.stop, :],
            ids_column[block, :],
            ids_row[index],
        )
        scores = scores.reshape(GROUP * QUERY_ROWS, KEY_ROWS).astype(BF16)
        found = dot(scores, value[keys, :])
        mixed[block, :] = gather_heads(found.reshape(GROUP, QUERY_ROWS, -1)).astype(BF16)

    total[...] += dot(mixed[...], weights[group, :, 3 * wide :], CONTRACT_LAST)

    @pl.when(group == groups - 1)
    def _():
        def step(block):
            middle[block, :] = total[block, :]
            hat, _ = normalised(total[block, :])
            normed_c[block, :] = (hat * gain_2[...]).astype(BF16)

        each_block(rows, 64, step)
        for at in range(groups):
            leaving_at(at).wait()


class Arrivals:
    def __init__(self, semaphores):
        self.semaphores, self.copies = semaphores, []

    def start(self, source, target):
        copy = pltpu.make_async_copy(source, target, self.semaphores.at[len(self.copies)])
        copy.start()
        self.copies.append(copy)
        return copy


def attention_backward(first, last, scale, groups, split, places, branch_in, weights_in, mixed_in, query_in, key_in, value_in, *others):
    normed_in, cosine_in, sine_in, *others = others
    if not first:
        total_in, *others = others
    if last:
        grad_middle, state, gain_1, *others = others
    table, back_table, ids_column, ids_row, *others = others
    if last:
        grad_state, grad_gain, *others = others
    else:
        total_out, *others = others
    grad_targets, others = others[: 1 + split], others[1 + split :]
    (
        branch,
        weights,
        mixed,
        query,
        key,
        value,
        normed_a,
        cosine,
        sine,
        total,
        grad_weight,
        grad_mixed,
        parts,
        phi,
        grad_phi,
        grad_value,
        grad_parts,
        grad_projected,
        arrived,
        leaving,
    ) = others
    _, rows, wide = query.shape
    half = wide // GROUP // 2
    own_rows = rows - 2 * MOST
    own = pl.ds(MOST, own_rows)
    small = phi.shape[1]
    deep = weights.shape[2]
    arrivals = Arrivals(arrived)
    got_branch = arrivals.start(branch_in, branch)
    got = []
    for at, group in enumerate(groups):
        columns_in = pl.ds(group * wide, wide)
        got.append(
            (
                arrivals.start(
                    weights_in.at[:, pl.ds(group * deep + 3 * wide, wide)],
                    weights.at[at, :, pl.ds(3 * wide, wide)],
                ),
                arrivals.start(query_in.at[:, columns_in], query.at[at]),
                arrivals.start(key_in.at[:, columns_in], key.at[at]),
                arrivals.start(mixed_in.at[own, columns_in], mixed.at[at]),
                arrivals.start(value_in.at[:, columns_in], value.at[at]),
                arrivals.start(
                    weights_in.at[:, pl.ds(group * deep, 3 * wide)],
                    weights.at[at, :, pl.ds(0, 3 * wide)],
                ),
            )
        )
        if at == 0:
            got_shared = [
                arrivals.start(cosine_in, cosine),
                arrivals.start(sine_in, sine),
                arrivals.start(normed_in.at[own, :], normed_a),
            ]
    if not first:
        got_total = arrivals.start(total_in, total)
    got_branch.wait()
    count = leaving.shape[1]
    size = grad_weight.shape[1] // count
    copies = []
    for at in range(len(groups)):
        got_last, *got_rows, got_first = got[at]
        got_last.wait()
        for copy in got_rows:
            copy.wait()
        grad_mixed[...] = dot(branch[...], weights[at, :, 3 * wide :]).astype(BF16)
        for block in row_blocks(rows, 64):
            for part, held in enumerate((query, key)):
                place = slice(part * rows + block.start, part * rows + block.stop)
                spread_parts(held[at, block, :], parts, place)
        phi[...] = phi_of(parts[...], table[at])
        grad_phi[rows:, :] = jnp.zeros((rows, small), F32)
        grad_value[...] = jnp.zeros_like(grad_value)
        found = dot(branch[own, :], mixed[at], CONTRACT_FIRST)
        grad_weight[at, :, 3 * wide :] = found.astype(BF16)

        for index, block, keys in query_blocks(rows):
            far_keys = slice(rows + keys.start, rows + keys.stop)
            spread_q = spread_heads(phi[block, :].astype(BF16))
            spread_grad = spread_heads(grad_mixed[block, :])
            keys_phi = phi[far_keys, :].astype(BF16)
            scores, inverse, same = block_scores(
                spread_q, keys_phi, ids_column[block, :], ids_row[index]
            )
            flat = (GROUP * QUERY_ROWS, KEY_ROWS)
            grad_scores = dot(spread_grad, value[at, keys, :], CONTRACT_LAST)
            grad_value[keys, :] += dot(
                scores.reshape(flat).astype(BF16), spread_grad, CONTRACT_FIRST
            )
            grad_scores = grad_scores.reshape(scores.shape)
            inner = jnp.sum(grad_scores * scores, axis=-1, keepdims=True)
            grad_scores = ((grad_scores - inner) * inverse * same[None]).astype(BF16).reshape(flat)
            found = dot(grad_scores, keys_phi)
            grad_phi[block, :] = gather_heads(found.reshape(GROUP, QUERY_ROWS, -1))
            grad_phi[far_keys, :] += dot(grad_scores, spread_q, CONTRACT_FIRST)

        if at == 0:
            for copy in got_shared:
                copy.wait()
        got_first.wait()
        for block in row_blocks(2 * rows, 128):
            high, low = two_parts(grad_phi[block, :] * phi[block, :])
            grad_parts[block, :small] = high
            grad_parts[block, small:] = low
        for part, held in enumerate((query, key)):
            for block in row_blocks(rows, 128):
                there = slice(part * rows + block.start, part * rows + block.stop)
                both = dot(grad_parts[there, :], back_table[at], CONTRACT_LAST)
                grad_rows = (both[:, :wide] - held[at, block, :] * both[:, wide:]) * scale
                turned = grad_rows * cosine[block, :]
                turned = turned + swap_halves(grad_rows * sine[block, :], half)
                grad_projected[block, part * wide : (part + 1) * wide] = turned.astype(BF16)
        grad_projected[:, 2 * wide :] = grad_value[...].astype(BF16)
        found = dot(normed_a[...], grad_projected[own, :], CONTRACT_FIRST)
        grad_weight[at, :, : 3 * wide] = found.astype(BF16)
        for index in range(count):
            place = pl.ds(pl.multiple_of(places[index], 16), size) if split else pl.ds(0, size)
            each = count // len(grad_targets)
            target = grad_targets[index // each]
            to = pl.ds(index % each * size, size)
            copies.append(
                pltpu.make_async_copy(
                    grad_weight.at[at, place, :],
                    target.at[to, pl.ds(at * deep, deep)],
                    leaving.at[at, index],
                )
            )
            copies[-1].start()
        back = dot(grad_projected[...], weights[at, :, : 3 * wide], CONTRACT_LAST)
        ending = at == len(groups) - 1
        if at == 0 and not first:
            got_total.wait()
        if at > 0 or not first:
            back = total[...] + back
        if ending and not last:
            total_out[...] = back
        else:
            total[...] = back
    if last:
        grad_gain[...] = jnp.zeros_like(grad_gain)

        def step(block):
            hat, inverse = normalised(state[block, :])
            back = norm_back(total[block, :], gain_1[...], hat, inverse)
            grad_state[block, :] = grad_middle[block, :] + back
            if own_block(block, rows):
                grad_gain[...] += jnp.sum(total[block, :] * hat, axis=0, keepdims=True)

        each_block(rows, 64, step)
    for copy in copies:
        copy.wait()


def adding(stages, *others):
    takes = [2 if stage == 0 else 6 for stage in stages]
    targets = others[sum(takes) :]
    begin = 0
    for index, (stage, count) in enumerate(zip(stages, takes)):
        kernel = adding_corner if stage == 0 else adding_sides
        kernel(*others[begin : begin + count], *targets[2 * index : 2 * index + 2])
        begin += count


def begins_of(pieces):
    begins = [0]
    for piece in pieces:
        begins.append(begins[-1] + piece.shape[0])
    return begins


def hidden_chunks(count):
    return [slice(begin, min(begin + CHUNK, count)) for begin in range(0, count, CHUNK)]


def feed_forward(piece_count, carried_in, normed_in, *others):
    pieces = others[:piece_count]
    activated_out, slope_out, state_out, *others = others[piece_count:]
    held, carried, normed_c, hidden, activated, slope, arrived, leaving = others
    rows, width = carried.shape
    count = held.shape[0]
    begins = begins_of(pieces)
    copies = [
        pltpu.make_async_copy(
            piece, held.at[pl.ds(begins[index], piece.shape[0]), :], arrived.at[index]
        )
        for index, piece in enumerate(pieces)
    ]
    norm_copy = pltpu.make_async_copy(normed_in, normed_c, arrived.at[piece_count])
    carried_copy = pltpu.make_async_copy(carried_in, carried, arrived.at[piece_count + 1])
    norm_copy.start()
    for copy in copies:
        copy.start()
    carried_copy.start()
    norm_copy.wait()
    chunks = hidden_chunks(count)
    waited = 0
    outgoing = []

    def project(chunk):
        hidden[:, chunk] = dot(normed_c[...], held[chunk, :width], CONTRACT_LAST)

    def wait_until(row):
        nonlocal waited
        while waited < piece_count and begins[waited] < row:
            copies[waited].wait()
            waited += 1

    wait_until(chunks[0].stop)
    project(chunks[0])
    wait_until(count)
    for index, chunk in enumerate(chunks):
        if index + 1 < len(chunks):
            project(chunks[index + 1])
        for block in row_blocks(rows, 32):
            value, back = gelu_and_slope(hidden[block, chunk])
            activated[block, chunk] = value.astype(BF16)
            slope[block, chunk] = back.astype(BF16)
        for target, source in ((activated_out, activated), (slope_out, slope)):
            outgoing.append(
                pltpu.make_async_copy(
                    source.at[:, chunk], target.at[:, chunk], leaving.at[len(outgoing)]
                )
            )
            outgoing[-1].start()
    carried_copy.wait()
    carried[...] += dot(activated[...], held[:, width:])
    outgoing.append(pltpu.make_async_copy(carried, state_out, leaving.at[len(outgoing)]))
    outgoing[-1].start()
    for copy in outgoing:
        copy.wait()


def feed_back(first, last, segments, piece_count, places, gradient_in, middle, gain_2, normed_in, *others):
    kept, others = others[: 2 * len(segments)], others[2 * len(segments) :]
    if not first:
        total_in, *others = others
    pieces = others[:piece_count]
    grad_out, grad_middle, *others = others[piece_count:]
    if last:
        grad_gain, grad_attn, *others = others
    (
        held,
        gradient,
        normed_c,
        activated,
        slope,
        total,
        branch,
        grad_hidden,
        grad_weight,
        arrived,
        leaving,
    ) = others
    rows, width = gradient.shape
    own_rows = rows - 2 * MOST
    own = pl.ds(MOST, own_rows)
    count = held.shape[0]
    begins = begins_of(pieces)
    arrivals = Arrivals(arrived)
    left, right = pl.ds(0, width), pl.ds(width, width)

    def weight_half(half):
        return [
            arrivals.start(
                piece.at[:, half], held.at[pl.ds(begins[index], piece.shape[0]), half]
            )
            for index, piece in enumerate(pieces)
        ]

    def leave(half, offset):
        copies = []
        for index, piece in enumerate(pieces):
            size = piece.shape[0]
            copies.append(
                pltpu.make_async_copy(
                    grad_weight.at[pl.ds(begins[index], size), half],
                    grad_out.at[pl.ds(pl.multiple_of(places[index], 16), size), half],
                    leaving.at[offset + index],
                )
            )
            copies[-1].start()
        return copies

    def stretch(which, rows_taken, target):
        copies, begin = [], 0
        for index, (column, size) in enumerate(segments):
            source = kept[2 * index + which].at[rows_taken, pl.ds(column, size)]
            copies.append(arrivals.start(source, target.at[:, pl.ds(begin, size)]))
            begin += size
        return copies

    got_gradient = arrivals.start(gradient_in, gradient)
    got_act = stretch(0, own, activated)
    got_down = weight_half(right)
    got_slope = stretch(1, pl.ds(0, rows), slope)
    got_norm = arrivals.start(normed_in.at[own, :], normed_c)
    got_up = weight_half(left)
    if not first:
        got_total = arrivals.start(total_in, total)
    got_gradient.wait()
    for block in row_blocks(rows, 64):
        branch[block, :] = gradient[block, :].astype(BF16)
    for copy in got_act:
        copy.wait()
    for chunk in row_blocks(count, count // 2):
        found = dot(activated[:, chunk], branch[own, :], CONTRACT_FIRST)
        grad_weight[chunk, width:] = found.astype(BF16)
    down_leaves = leave(right, 0)
    for copy in got_down + got_slope:
        copy.wait()
    for chunk in hidden_chunks(count):
        grad_act = dot(branch[...], held[chunk, width:], CONTRACT_LAST)
        grad_hidden[:, chunk] = (grad_act * slope[:, chunk].astype(F32)).astype(BF16)
    for copy in [got_norm] + got_up:
        copy.wait()
    for chunk in row_blocks(count, count // 2):
        found = dot(grad_hidden[MOST : MOST + own_rows, chunk], normed_c[...], CONTRACT_FIRST)
        grad_weight[chunk, :width] = found.astype(BF16)
    up_leaves = leave(left, piece_count)
    back = dot(grad_hidden[...], held[:, :width])
    if not first:
        got_total.wait()
        back = total[...] + back
    if not last:
        grad_middle[...] = back
    else:
        total[...] = back
        grad_gain[...] = jnp.zeros_like(grad_gain)

        def step(block):
            hat, inverse = normalised(middle[block, :])
            back = gradient[block, :] + norm_back(total[block, :], gain_2[...], hat, inverse)
            grad_middle[block, :] = back
            grad_attn[block, :] = back.astype(BF16)
            if own_block(block, rows):
                grad_gain[...] += jnp.sum(total[block, :] * hat, axis=0, keepdims=True)

        each_block(rows, 64, step)
    for copy in down_leaves + up_leaves:
        copy.wait()


def column_runs(parts, part, begin, width, group_width):
    stop = begin + width
    while begin < stop:
        group = begin // group_width
        end = min(stop, (group + 1) * group_width)
        place = group * parts * group_width + part * group_width + begin % group_width
        yield begin, end, place
        begin = end


def joining(parts, begin, group_width, source_in, joined, source, arrived):
    copy = pltpu.make_async_copy(source_in, source, arrived)
    copy.start()
    copy.wait()
    rows = joined.shape[0]
    count = source.shape[0]
    width = joined.shape[1] // parts // count
    across = source.shape[2] // width
    for part in range(parts):
        top = begin + part // across * rows
        left = part % across * width
        side = [source[at, top : top + rows, left : left + width] for at in range(count)]
        side = jnp.concatenate(side, axis=1)
        for first, end, place in column_runs(parts, part, 0, count * width, group_width):
            joined[:, place : place + end - first] = side[:, first:end]


def tabulating(begin, source, *others):
    layers = len(others) // 2
    groups, _, small = others[0].shape
    feats = small // GROUP
    own_heads = groups * GROUP // source.shape[0]
    wide = others[layers].shape[1] // 2
    deep = wide // GROUP
    thin = source.shape[1] - begin
    runs = deep // thin
    run_width = layers * own_heads * feats
    for target in others:
        target[...] = jnp.zeros_like(target)
    for layer in range(layers):
        tables, back_tables = others[layer], others[layers + layer]
        for index in range(groups * GROUP):
            group, place = index // GROUP, index % GROUP
            column = (layer * own_heads + index % own_heads) * feats
            across = slice(place * feats, (place + 1) * feats)
            again = slice(small + place * feats, small + (place + 1) * feats)
            for part in range(4):
                for run in range(runs):
                    top = part * wide + place * deep + run * thin
                    down = slice(top, top + thin)
                    if part < 2:
                        at = run * run_width + column
                        value = source[index // own_heads, begin : begin + thin, at : at + feats]
                    else:
                        value = jnp.full((thin, feats), -0.5, BF16)
                    tables[group, down, across] = value
                    if part < 2:
                        value = value if part < 1 else jnp.ones((thin, feats), BF16)
                        back_tables[group, down, across] = value
                        back_tables[group, down, again] = value


def parting(parts, group_width, pieces, gains, *others):
    if gains:
        gain, *others = others
    *sources, target = others
    count, rows, all_width = target.shape
    if gains:
        rows -= GAIN_ROWS
        left, done = gain[...], 0
        for _ in range(3):
            part = left.astype(BF16)
            left = left - part.astype(F32)
            for at in range(count):
                target[at, rows + done : rows + done + gains, :] = part
            done += gains
        target[:, rows + done :, :] = jnp.zeros((count, GAIN_ROWS - done, all_width), BF16)
    width = all_width // parts
    each = len(sources) // pieces
    starts = [0]
    for piece in range(pieces - 1):
        starts.append(starts[-1] + sources[piece * each].shape[1])
    for part in range(parts):
        for at in range(count):
            runs = []
            for begin, end, place in column_runs(parts, part, at * width, width, group_width):
                piece = max(at for at in range(pieces) if starts[at] <= place)
                run = slice(place - starts[piece], place - starts[piece] + end - begin)
                mine = sources[piece * each : (piece + 1) * each]
                total = mine[0][:, run].astype(F32)
                for source in mine[1:]:
                    total = total + source[:, run].astype(F32)
                runs.append(total)
            total = runs[0] if len(runs) == 1 else jnp.concatenate(runs, axis=1)
            target[at, :rows, part * width : (part + 1) * width] = total.astype(target.dtype)


def finishing(parts, gains, turned, *others):
    if gains:
        *others, gain_out = others
        total = 0.0
        first = others[0]
        rows = first.shape[1] - GAIN_ROWS
        for at in range(first.shape[0]):
            for part in range(3):
                begin = rows + part * gains
                total = total + first[at, begin : begin + gains, :].astype(F32)
        gain_out[...] = total
    sources, targets = others[: -len(parts)], others[-len(parts) :]
    rows = targets[0].shape[-1 if turned else -2]
    for layer, source in enumerate(sources):
        begin = 0
        for target, count in zip(targets, parts):
            for part in range(count):
                width = target.shape[-2 if turned else -1]
                run = slice(begin, begin + width)
                total = source[0, :rows, run].astype(F32)
                for at in range(1, source.shape[0]):
                    total = total + source[at, :rows, run].astype(F32)
                if turned:
                    target[layer] = total.T
                elif count > 1:
                    target[layer, part] = total
                else:
                    target[layer] = total
                begin += width


def turning(cosine_in, sine_in, ids_in, cosine, sine, ids_column):
    half = cosine_in.shape[0]
    down = cosine_in[...].T
    across = sine_in[...].T
    for head in range(cosine.shape[1] // (2 * half)):
        for part in range(2):
            place = slice((2 * head + part) * half, (2 * head + part + 1) * half)
            cosine[:, place] = down
            sine[:, place] = across if part else -across
    ids_column[...] = ids_in[...].T[:, :1].astype(jnp.int32)


def adding_corner(near, far, to_x, to_y):
    half = to_x.shape[0]
    for target, place in ((to_x, slice(0, half)), (to_y, slice(half, 2 * half))):
        target[...] = (near[place, :].astype(F32) + far[place, :].astype(F32)).astype(BF16)


def adding_sides(near_x, far_x, near_y, far_y, from_x, from_y, to_x, to_y):
    half = from_x.shape[0]
    top, bottom = slice(0, half), slice(half, 2 * half)
    for near, far, place, more, target in (
        (near_x, far_x, top, None, to_x),
        (near_x, far_x, bottom, from_y, to_x),
        (near_y, far_y, top, from_x, to_y),
        (near_y, far_y, bottom, None, to_y),
    ):
        total = near[place, :].astype(F32) + far[place, :].astype(F32)
        if more is not None:
            total = total + more[...].astype(F32)
        target[place, :] = total.astype(BF16)


def whole(shape):
    return pl.BlockSpec(
        shape, lambda step, *_: (0,) * len(shape), pipeline_mode=pl.Buffered(buffer_count=1)
    )


def columns(rows, width):
    return pl.BlockSpec((rows, width), lambda step, *_: (0, step))


def leading(shape):
    return pl.BlockSpec(shape, lambda step, *_: (step,) + (0,) * (len(shape) - 1))


def struct(shape, dtype):
    return jax.ShapeDtypeStruct(shape, dtype)


ANYWHERE = pl.BlockSpec(memory_space=pltpu.HBM)


def kernel_call(kernel, steps, in_specs, out_specs, out_shape, scratch, flops, prefetch=0):
    return pl.pallas_call(
        kernel,
        grid_spec=pltpu.PrefetchScalarGridSpec(
            num_scalar_prefetch=prefetch,
            grid=(steps,),
            in_specs=in_specs,
            out_specs=out_specs,
            scratch_shapes=scratch,
        ),
        out_shape=out_shape,
        compiler_params=pltpu.CompilerParams(vmem_limit_bytes=VMEM_BYTES),
        cost_estimate=pl.CostEstimate(flops=flops, bytes_accessed=flops // 600, transcendentals=0),
    )


def run_attention_forward(state, gains, pieces, places, table, *, tables, ids, scale):
    rows, width = state.shape
    wide = tables[0].shape[1]
    groups, deep, small = table.shape
    blocks = rows // QUERY_ROWS
    return kernel_call(
        functools.partial(attention_forward, scale, len(pieces)),
        groups,
        [
            whole((rows, width)),
            whole((1, width)),
            whole((1, width)),
            leading((1, deep, small)),
            whole((rows, wide)),
            whole((rows, wide)),
            whole((rows, 1)),
            whole((blocks, 1, KEY_ROWS)),
            *[ANYWHERE for _ in pieces],
        ],
        [
            ANYWHERE,
            whole((rows, width)),
            columns(rows, wide),
            columns(rows, wide),
            columns(rows, wide),
            columns(rows, wide),
            whole((rows, width)),
            whole((rows, width)),
        ],
        [
            struct((width, 4 * width), BF16),
            struct((rows, width), BF16),
            struct((rows, width), F32),
            struct((rows, width), F32),
            struct((rows, width), BF16),
            struct((rows, width), BF16),
            struct((rows, width), F32),
            struct((rows, width), BF16),
        ],
        [
            pltpu.VMEM((groups, width, 4 * wide), BF16),
            pltpu.VMEM((rows, width), F32),
            pltpu.VMEM((rows, 3 * wide), F32),
            pltpu.VMEM((2 * rows, deep), BF16),
            pltpu.VMEM((2 * rows, small), BF16),
            pltpu.SemaphoreType.DMA((groups, len(pieces))),
            pltpu.SemaphoreType.DMA((groups,)),
        ],
        FORWARD_COST,
        1,
    )(places, state, gains[0], gains[1], table, *tables, *ids, *pieces)


def run_attention_backward(
    groups,
    carried,
    *,
    grad_middle,
    branch,
    state,
    gain,
    weights,
    places,
    table,
    back_table,
    tables,
    ids,
    kept,
    scale,
):
    rows, width = state.shape
    wide = tables[0].shape[1]
    all_groups, deep, small = table.shape
    first, last = groups[0] == 0, groups[-1] == all_groups - 1
    count = len(groups)
    normed_a, query, key, value, mixed = kept
    own_rows = rows - 2 * MOST
    blocks = rows // QUERY_ROWS
    copied = [branch, weights, mixed, query, key, value, normed_a, *tables]
    ending = [grad_middle, state, gain] if last else []
    split = places.shape[0] > 1
    halves = 1 + split
    return kernel_call(
        functools.partial(attention_backward, first, last, scale, groups, split),
        1,
        [
            *[ANYWHERE] * (len(copied) + (not first)),
            *([whole((rows, width)), whole((rows, width)), whole((1, width))] if last else []),
            pl.BlockSpec((count, deep, small), lambda *_: (groups[0] // count, 0, 0)),
            pl.BlockSpec((count,) + back_table.shape[1:], lambda *_: (groups[0] // count, 0, 0)),
            whole((rows, 1)),
            whole((blocks, 1, KEY_ROWS)),
        ],
        [
            *([whole((rows, width)), whole((1, width))] if last else [whole((rows, width))]),
            *[ANYWHERE] * halves,
        ],
        [
            struct((rows, width), F32),
            *([struct((1, width), F32)] if last else []),
            *[struct((width // halves, count * 4 * wide), BF16)] * halves,
        ],
        [
            pltpu.VMEM((rows, width), BF16),
            pltpu.VMEM((count, width, 4 * wide), BF16),
            pltpu.VMEM((count, own_rows, wide), BF16),
            pltpu.VMEM((count, rows, wide), F32),
            pltpu.VMEM((count, rows, wide), F32),
            pltpu.VMEM((count, rows, wide), BF16),
            pltpu.VMEM((own_rows, width), BF16),
            pltpu.VMEM((rows, wide), F32),
            pltpu.VMEM((rows, wide), F32),
            pltpu.VMEM((rows, width), F32),
            pltpu.VMEM((count, width, 4 * wide), BF16),
            pltpu.VMEM((rows, wide), BF16),
            pltpu.VMEM((2 * rows, deep), BF16),
            pltpu.VMEM((2 * rows, small), F32),
            pltpu.VMEM((2 * rows, small), F32),
            pltpu.VMEM((rows, wide), F32),
            pltpu.VMEM((2 * rows, 2 * small), BF16),
            pltpu.VMEM((rows, 3 * wide), BF16),
            pltpu.SemaphoreType.DMA((5 + 6 * count,)),
            pltpu.SemaphoreType.DMA((count,) + places.shape),
        ],
        BACKWARD_COST // 3 * count,
        1,
    )(
        places,
        *copied,
        *([] if first else [carried]),
        *ending,
        table,
        back_table,
        *ids,
    )


def run_feed_forward(carried, normed_c, pieces):
    rows, width = carried.shape
    count = sum(piece.shape[0] for piece in pieces)
    return kernel_call(
        functools.partial(feed_forward, len(pieces)),
        1,
        [ANYWHERE] * (2 + len(pieces)),
        [ANYWHERE] * 3,
        [
            struct((rows, count), BF16),
            struct((rows, count), BF16),
            struct((rows, width), F32),
        ],
        [
            pltpu.VMEM((count, 2 * width), BF16),
            pltpu.VMEM((rows, width), F32),
            pltpu.VMEM((rows, width), BF16),
            pltpu.VMEM((rows, count), F32),
            pltpu.VMEM((rows, count), BF16),
            pltpu.VMEM((rows, count), BF16),
            pltpu.SemaphoreType.DMA((len(pieces) + 2,)),
            pltpu.SemaphoreType.DMA((2 * len(hidden_chunks(count)) + 1,)),
        ],
        FORWARD_COST // 3,
    )(carried, normed_c, *pieces)


def kept_stretches(near_kept, far_kept, corner_kept):
    side, corner = near_kept[0].shape[1], corner_kept[0].shape[1] // 2
    return [
        (near_kept[:2], 0, side),
        (far_kept[:2], 0, side),
        (corner_kept[:2], 0, corner),
        (corner_kept[:2], corner, corner),
    ]


def run_feed_back(gradient, middle, gain, normed_c, stretches, pieces, places, carried, last):
    rows, width = middle.shape
    count = sum(piece.shape[0] for piece in pieces)
    first = carried is None
    kept = [array for arrays, _, _ in stretches for array in arrays]
    segments = [(column, size) for _, column, size in stretches]
    arrivals = 2 + not_first(first) + 2 * len(pieces) + len(kept)
    return kernel_call(
        functools.partial(feed_back, first, last, segments, len(pieces)),
        1,
        [
            ANYWHERE,
            whole((rows, width)),
            whole((1, width)),
            *[ANYWHERE] * (1 + len(kept) + not_first(first) + len(pieces)),
        ],
        [
            ANYWHERE,
            whole((rows, width)),
            *([whole((1, width)), whole((rows, width))] if last else []),
        ],
        [
            struct((count, 2 * width), BF16),
            struct((rows, width), F32),
            *([struct((1, width), F32), struct((rows, width), BF16)] if last else []),
        ],
        [
            pltpu.VMEM((count, 2 * width), BF16),
            pltpu.VMEM((rows, width), F32),
            pltpu.VMEM((rows - 2 * MOST, width), BF16),
            pltpu.VMEM((rows - 2 * MOST, count), BF16),
            pltpu.VMEM((rows, count), BF16),
            pltpu.VMEM((rows, width), F32),
            pltpu.VMEM((rows, width), BF16),
            pltpu.VMEM((rows, count), BF16),
            pltpu.VMEM((count, 2 * width), BF16),
            pltpu.SemaphoreType.DMA((arrivals,)),
            pltpu.SemaphoreType.DMA((2 * len(pieces),)),
        ],
        FORWARD_COST // 2,
        1,
    )(
        places,
        gradient,
        middle,
        gain,
        normed_c,
        *kept,
        *([] if first else [carried]),
        *pieces,
    )


def not_first(first):
    return 0 if first else 1


HEAD_DEVICES = 4
CHUNK = 512
GAIN_ROWS = 16
X, Y, CORE = 2, 4, 1
FORWARD_COST = 29_000_000_000
BACKWARD_COST = 40_000_000_000


def hop(values, bit):
    count = lax.axis_size("dp")
    return lax.ppermute(values, "dp", [(i, i ^ bit) for i in range(count)])


def exchange(values):
    return lax.all_to_all(values, "head", split_axis=0, concat_axis=0, tiled=True)


def together(*values):
    return lax.optimization_barrier(values)


def by_permutes():
    return lax.axis_size("dp") == 8 and lax.axis_size("head") == HEAD_DEVICES


def group_width(parts, width, wide):
    return wide if parts == 4 else width


def join_columns(source, parts, begin, rows, width, wide):
    count = source.shape[0]
    return kernel_call(
        functools.partial(joining, parts, begin, group_width(parts, count * width, wide)),
        1,
        [ANYWHERE],
        whole((rows, parts * count * width)),
        struct((rows, parts * count * width), BF16),
        [pltpu.VMEM(source.shape, BF16), pltpu.SemaphoreType.DMA],
        1_000_000,
    )(source)


def feature_tables(source, begin, shapes):
    return kernel_call(
        functools.partial(tabulating, begin),
        1,
        [whole(source.shape)],
        [whole(shape) for shape in shapes],
        [struct(shape, BF16) for shape in shapes],
        [],
        1_000_000,
    )(source)


def block_of(rows, columns_all, index):
    return pl.BlockSpec((rows, columns_all), lambda *_: (index, 0))


def part_columns(pieces, parts, wide, gain=None):
    rows = pieces[0][-1].shape[0]
    columns_all = sum(piece[0].shape[1] for piece in pieces)
    gains = 0 if gain is None else gain.shape[0]
    shape = (
        HEAD_DEVICES,
        rows + (GAIN_ROWS if gains else 0),
        columns_all // HEAD_DEVICES,
    )
    return kernel_call(
        functools.partial(
            parting, parts, group_width(parts, columns_all // parts, wide), len(pieces), gains
        ),
        1,
        [
            *([whole(gain.shape)] if gains else []),
            *[block_of(rows, source.shape[1], 0) for piece in pieces for source in piece],
        ],
        whole(shape),
        struct(shape, BF16),
        [],
        1_000_000,
    )(*([gain] if gains else []), *[source for piece in pieces for source in piece])


def finish(sources, parts, rows, gains=0, turned=False):
    all_width = sources[0].shape[2]
    width = all_width // sum(parts)
    shapes = [
        (len(sources), count, rows, width) if count > 1 else (len(sources), rows, width)
        for count in parts
    ]
    if turned:
        shapes = [(len(sources), width, rows) for _ in parts]
    if gains:
        shapes.append((gains, all_width))
    return kernel_call(
        functools.partial(finishing, parts, gains, turned),
        1,
        [whole(source.shape) for source in sources],
        [whole(shape) for shape in shapes],
        [struct(shape, F32) for shape in shapes],
        [],
        1_000_000,
    )(*sources)


def next_chips(own):
    return hop(own, X), hop(own, Y), hop(own, CORE)


def halves_to_pass(over_x, over_y):
    half = over_x.shape[0] // 2
    return over_x[:half], over_y[half:]


def chip_across(passed):
    to_y, to_x = passed
    return hop(to_y, Y), hop(to_x, X)


def other_core(pieces):
    return tuple(hop(piece, CORE) for piece in pieces)


def piece_places(rows, order=range(10)):
    own = lax.axis_index("dp")
    bits = [(0, 0), (X, 0), (Y, 0), (X | Y, 0), (X | Y, rows // 2)]
    places = [(own ^ (bit | core)) * rows + begin for core in (0, CORE) for bit, begin in bits]
    return jnp.stack([places[at] for at in order]).astype(jnp.int32)


def block_places(rows):
    own = lax.axis_index("dp")
    return jnp.stack(
        [(own ^ (bit | core)) * rows for core in (CORE, 0) for bit in (0, X, Y, X | Y)]
    ).astype(jnp.int32)


class Reduction:
    def __init__(self, far, slow):
        self.slow, self.stage, self.left = slow, 0, 1
        self.came = hop(far, CORE)

    def operands(self):
        rows = self.near.shape[0] // 4
        half = rows // 2
        if self.stage == 0:
            self.far = self.came
            return [(self.near, rows, 3), (self.far, rows, 3)], half
        sides = [(array, rows, at) for at in (1, 2) for array in (self.near, self.far)]
        return sides + [(array, half, 0) for array in self.came], rows

    def send(self):
        to_x, to_y = self.sent
        self.came = hop(to_x, X), hop(to_y, Y)
        self.stage += 1
        self.left = self.slow[self.stage - 1]

    def arrays(self):
        return [self.near, self.far, *self.came]


def prepare(reductions):
    arrays, in_specs, out_specs, shapes = [], [], [], []
    for reduction in reductions:
        operands, out_rows = reduction.operands()
        width = reduction.near.shape[1]
        for array, rows, at in operands:
            arrays.append(array)
            in_specs.append(block_of(rows, width, at))
        out_specs += [whole((out_rows, width))] * 2
        shapes += [struct((out_rows, width), BF16)] * 2
    sent = kernel_call(
        functools.partial(adding, [reduction.stage for reduction in reductions]),
        1,
        in_specs,
        out_specs,
        shapes,
        [],
        1_000_000,
    )(*arrays)
    for index, reduction in enumerate(reductions):
        reduction.sent = sent[2 * index : 2 * index + 2]


class Sharing:
    def __init__(self, reductions, parts, wide, slow):
        self.reductions, self.parts, self.wide, self.slow = reductions, parts, wide, slow
        self.stage, self.left, self.came, self.gain = 0, 0, (), None

    def prepare(self):
        pieces = [reduction.arrays() for reduction in self.reductions]
        self.sent = part_columns(pieces, self.parts, self.wide, self.gain)

    def send(self):
        self.came = exchange(self.sent)
        self.stage, self.left = 1, self.slow


class Traffic:
    def __init__(self):
        self.moving = []

    def slot(self, values):
        ready = []
        for item in self.moving:
            item.left -= 1
            if item.left <= 0:
                ready.append(item)
        values, came = together(values, [item.came for item in ready])
        for item, arrived in zip(ready, came):
            item.came = arrived
        sending = []
        for item in ready:
            if isinstance(item, Sharing):
                if item.stage == 0 and all(r.stage == 3 for r in item.reductions):
                    sending.append(item)
            elif item.stage < 2:
                sending.append(item)
            else:
                item.stage = 3
        for item in ready:
            if isinstance(item, Sharing) and item.stage == 0 and item not in sending:
                if all(r.stage == 3 for r in item.reductions):
                    sending.append(item)
        reductions = [item for item in sending if isinstance(item, Reduction)]
        if reductions:
            prepare(reductions)
        for item in sending:
            if isinstance(item, Sharing):
                item.prepare()
        values, sent = together(values, [item.sent for item in sending])
        for item, prepared in zip(sending, sent):
            item.sent = prepared
            item.send()
        self.moving = [
            item
            for item in self.moving
            if item.stage < (1 if isinstance(item, Sharing) else 3) or item.left > 0
        ]
        return values


def grouped_columns(values, parts, wide):
    rows = values.shape[0]
    return values.reshape(rows, parts, -1, wide).swapaxes(1, 2).reshape(rows, -1)


def over_heads(part, parts, wide):
    rows = part.shape[0]
    if parts == 4:
        part = part.reshape(rows, -1, parts, wide).swapaxes(1, 2)
    part = part.reshape(rows, parts, -1)
    part = lax.psum_scatter(part, "head", scatter_dimension=2, tiled=True)
    return part.swapaxes(0, 1).astype(F32)


def shared_gain(values, bit):
    return values + hop(values, bit)


def with_halo(inputs, cotangent):
    count = lax.axis_size("head")
    both = jnp.concatenate([inputs, cotangent], axis=1)
    before = lax.ppermute(both[-MOST:], "head", [(i, i + 1) for i in range(count - 1)])
    after = lax.ppermute(both[:MOST], "head", [(i + 1, i) for i in range(count - 1)])
    joined = jnp.concatenate([before, both, after], axis=0).astype(F32)
    return joined[:, : inputs.shape[1]], joined[:, inputs.shape[1] :]


def window_ids(segment_ids, own_rows):
    padded = jnp.pad(segment_ids[0], (MOST, MOST), constant_values=-1)
    begin = lax.axis_index("head") * own_rows
    ids = lax.dynamic_slice(padded, (begin,), (own_rows + 2 * MOST,))
    place = jnp.arange(ids.shape[0])
    earlier = (ids[:, None] == ids[None, :]) & (place[None, :] < place[:, None])
    position = jnp.sum(earlier.astype(F32), axis=1)
    used = (ids >= ids[MOST]) & (ids <= ids[MOST + own_rows - 1])
    column = jnp.where(used, ids, -1)
    row = jnp.where(used, ids, -2)
    starts = [
        min(max(b * QUERY_ROWS - MOST, 0), ids.shape[0] - KEY_ROWS)
        for b in range(ids.shape[0] // QUERY_ROWS)
    ]
    rows = jnp.stack([row[start : start + KEY_ROWS] for start in starts])[:, None, :]
    return position, (column, rows)


def rotary_tables(position, ids, head_width):
    halves = head_width // 2
    frequency = jnp.exp(jnp.arange(halves, dtype=F32) * (-2.0 * math.log(10000.0) / head_width))
    angles = frequency[:, None] * position[None, :]
    column, rows = ids
    count = position.shape[0]
    wide = (count, GROUP * head_width)
    spread = jnp.broadcast_to(column.astype(F32)[None], (8, count))
    cosine, sine, column = kernel_call(
        turning,
        1,
        [whole(angles.shape)] * 2 + [whole(spread.shape)],
        [whole(wide), whole(wide), whole((count, 1))],
        [struct(wide, F32), struct(wide, F32), struct((count, 1), jnp.int32)],
        [],
        1_000_000,
    )(jnp.cos(angles), jnp.sin(angles), spread)
    return (cosine, sine), (column, rows)


def body(
    inputs,
    segment_ids,
    features,
    norm_gain,
    query_key_value,
    output_weight,
    up_weight,
    down_weight,
    cotangent,
):
    layer_count = norm_gain.shape[0]
    own_rows = inputs.shape[0]
    head_width = features.shape[3]
    feature_count = features.shape[2]
    scale = head_width ** (-0.25)
    own_place = slice(MOST, MOST + own_rows)

    in_rows, part_width = output_weight.shape[1:]
    groups = inputs.shape[1] // (GROUP * head_width)
    wide, small = GROUP * head_width, GROUP * feature_count
    table_shapes = [(groups, 4 * wide, small)] * layer_count + [
        (groups, 2 * wide, 2 * small)
    ] * layer_count
    chunks = []
    for layer in range(layer_count):
        chunks.append((4, *query_key_value[layer], output_weight[layer]))
        chunks.append((2, up_weight[layer], down_weight[layer]))
    stored = []
    if by_permutes():
        attention_places = piece_places(in_rows)
        grad_places = block_places(in_rows)
        gain_rows = [[norm_gain[layer, at][None] for at in range(2)] for layer in range(layer_count)]
        feed_places = piece_places(up_weight.shape[1], (0, 1, 2, 5, 6, 7, 3, 4, 8, 9))
        feature_rows = jnp.moveaxis(features, 3, 0).reshape(4, head_width // 4, -1)
        feature_rows = jnp.concatenate(list(feature_rows), axis=1)

        def join(index, came, begin=0):
            parts, *weights = chunks[index]
            return join_columns(came, parts, begin, *weights[-1].shape, wide)

        def gathered_columns(sent):
            return lax.all_gather(sent, "head", axis=0, tiled=False)

        sent = jnp.concatenate([jnp.concatenate(chunks[0][1:], axis=1), feature_rows])
        sent = jnp.broadcast_to(sent[None], (HEAD_DEVICES,) + sent.shape)
        sent, inputs, cotangent = together(sent, inputs, cotangent)
        came = exchange(sent)
        state, gradient = with_halo(inputs, cotangent)
        position, ids = window_ids(segment_ids, own_rows)
        tables, ids = rotary_tables(position, ids, head_width)
        both = []
        for layer in range(1, layer_count):
            q, k, v, o = chunks[2 * layer][1:]
            both.append(
                jnp.concatenate(
                    [
                        jnp.concatenate(pair, axis=1)
                        for pair in ((q, k), (v, o), chunks[2 * layer + 1][1:])
                    ]
                )
            )
        first_feed = jnp.concatenate(chunks[1][1:], axis=1)
        came, state, gradient, tables, ids, first_feed, gain_rows, attention_places = together(
            came, state, gradient, tables, ids, first_feed, gain_rows, attention_places
        )
        attend = functools.partial(run_attention_forward, tables=tables, ids=ids, scale=scale)
        own = join(0, came)
        came_feed = gathered_columns(first_feed)
        over_x, over_y, over_core = next_chips(own)
        made = feature_tables(came, in_rows, table_shapes)
        over_x, over_y, over_core, made, both = together(over_x, over_y, over_core, made, both)
        blocks, back_blocks = made[:layer_count], made[layer_count:]
        passed = halves_to_pass(over_x, over_y)
        across = chip_across(passed)
        own_feed = join(1, came_feed)
        for layer in range(layer_count):
            more = layer + 1 < layer_count
            near = (own, over_x, over_y) + tuple(across)
            far = (over_core,) + other_core(near[1:])
            attention_pieces = near + far
            own = own_feed
            state, own, sent = together(state, own, both[layer] if more else ())
            over_x, over_y, over_core = next_chips(own)
            came = gathered_columns(sent) if more else ()
            weights, *kept, middle, normed_c = attend(
                state,
                gain_rows[layer],
                attention_pieces,
                attention_places,
                blocks[layer],
            )

            middle, over_x, over_y, over_core = together(middle, over_x, over_y, over_core)
            sides = own, over_x, over_y
            passed = halves_to_pass(over_x, over_y)
            carried, passed = together(middle, passed)
            across = chip_across(passed)
            far_sides = (over_core,) + other_core(sides[1:])
            near_kept = run_feed_forward(carried, normed_c, sides)

            carried, across, far_sides = together(near_kept[2], across, far_sides)
            far_across = other_core(across)
            if more:
                carried, came = together(carried, came)
                carried, own = together(carried, join(2 * layer + 2, came))
                over_x, over_y, over_core = next_chips(own)
            last_pieces = across + far_across
            feed_pieces = sides, far_sides, across, far_across
            if not more:
                rest = run_feed_forward(carried, normed_c, far_sides + last_pieces)
                side = near_kept[0].shape[1]
                stretches = [(near_kept[:2], 0, side), (rest[:2], 0, rest[0].shape[1])]
                stored.append((state, weights, kept, middle, normed_c, stretches, feed_pieces))
                state = rest[2]
                break
            far_kept = run_feed_forward(carried, normed_c, far_sides)

            carried = far_kept[2]
            if more:
                carried, over_x, over_y, over_core = together(carried, over_x, over_y, over_core)
                passed = halves_to_pass(over_x, over_y)
                carried, passed = together(carried, passed)
                across = chip_across(passed)
            last_kept = run_feed_forward(carried, normed_c, last_pieces)
            stretches = kept_stretches(near_kept, far_kept, last_kept)
            stored.append((state, weights, kept, middle, normed_c, stretches, feed_pieces))
            state = last_kept[2]
            if more:
                state, across, came = together(state, across, came)
                own_feed = join(2 * layer + 3, came, 2 * in_rows)
    else:
        gain_rows = [[norm_gain[layer, at][None] for at in range(2)] for layer in range(layer_count)]
        state, gradient = with_halo(inputs, cotangent)
        position, ids = window_ids(segment_ids, own_rows)
        tables, ids = rotary_tables(position, ids, head_width)
        attend = functools.partial(run_attention_forward, tables=tables, ids=ids, scale=scale)
        all_features = lax.all_gather(features, "head", axis=1, tiled=True)
        shaped = all_features.reshape(layer_count, -1, GROUP, feature_count, head_width)
        eye = jnp.eye(GROUP, dtype=BF16)
        block = jnp.einsum("lghmw,hk->lghwkm", shaped, eye).reshape(layer_count, groups, wide, small)
        ones = jnp.kron(eye, jnp.ones((head_width, feature_count), BF16))
        ones = jnp.broadcast_to(ones, block.shape)
        blocks = jnp.concatenate([block, block, ones * -0.5, ones * -0.5], axis=2)
        back_blocks = jnp.concatenate([block, ones], axis=2)
        back_blocks = jnp.concatenate([back_blocks, back_blocks], axis=3)
        owned = []
        for parts, *weights in chunks:
            rows = weights[-1].shape[0]
            joined = jnp.stack(weights)
            joined = lax.all_gather(joined, "head", axis=2, tiled=True)
            joined = lax.all_gather(joined, "dp", axis=1, tiled=True)
            joined = joined.swapaxes(0, 1).reshape(joined.shape[1], -1)
            owned.append(grouped_columns(joined, parts, wide) if parts == 4 else joined)
        middle_row = inputs.shape[1] // 2
        attention_places = jnp.array([0, middle_row], jnp.int32)
        size = up_weight.shape[1] * lax.axis_size("dp") // 8
        feed_places = jnp.array([0, 4 * size, 3 * size, 7 * size], jnp.int32)
        for layer in range(layer_count):
            own_attention, own_feed = owned[2 * layer], owned[2 * layer + 1]
            weights, *kept, middle, normed_c = attend(
                state,
                gain_rows[layer],
                (own_attention[:middle_row], own_attention[middle_row:]),
                attention_places,
                blocks[layer],
            )
            size = own_feed.shape[0] // 8
            feed_pieces = [
                (own_feed[begin * size : end * size],) for begin, end in ((0, 3), (4, 7), (3, 4), (7, 8))
            ]
            near_kept = run_feed_forward(middle, normed_c, feed_pieces[0])
            far_kept = run_feed_forward(near_kept[2], normed_c, feed_pieces[1])
            last_kept = run_feed_forward(far_kept[2], normed_c, feed_pieces[2] + feed_pieces[3])
            stretches = kept_stretches(near_kept, far_kept, last_kept)
            stored.append((state, weights, kept, middle, normed_c, stretches, feed_pieces))
            state = last_kept[2]
    outputs = state[own_place].astype(BF16)

    gains = [None] * layer_count
    shares = [None] * layer_count
    traffic = Traffic()
    summing = []
    for layer in reversed(range(layer_count)):
        before, weights, kept, middle, normed_c, stretches, feed_pieces = stored[layer]
        feed = (middle, gain_rows[layer][1], normed_c)
        attend_back = functools.partial(
            run_attention_backward,
            state=before,
            gain=gain_rows[layer][0],
            weights=weights,
            table=blocks[layer],
            back_table=back_blocks[layer],
            tables=tables,
            ids=ids,
            kept=kept,
            scale=scale,
        )
        if layer > 0 or not by_permutes():
            pieces = [piece for part in feed_pieces for piece in part]
            feed_grad, grad_middle, gain_c, branch = run_feed_back(
                gradient, *feed, stretches, pieces, feed_places, None, True
            )
            feed_part = lax.psum_scatter(feed_grad, "dp", scatter_dimension=0, tiled=True)
            gradient, gain_a, *grad = attend_back(
                tuple(range(groups)),
                None,
                grad_middle=grad_middle,
                branch=branch,
                places=grad_places if by_permutes() else jnp.zeros((1,), jnp.int32),
            )
            if by_permutes():
                gains[layer] = jnp.concatenate([gain_a, gain_c])
                attention_sum = Reduction(grad[0], (1, 1))
                attention_sum.near, attention_sum.left = grad[1], 2
                traffic.moving.append(attention_sum)
                summing.append((layer, feed_part, attention_sum))
                continue
            [grad] = grad
            attention_part = lax.psum_scatter(grad, "dp", scatter_dimension=0, tiled=True)
            gains[layer] = jnp.concatenate([gain_a, gain_c])
            shares[layer] = over_heads(feed_part, 2, wide), over_heads(attention_part, 4, wide)
            continue
        relative = [
            jnp.array(begins_of(feed_pieces[at] + feed_pieces[2 + at])[:-1], jnp.int32) for at in (0, 1)
        ]
        gradient = traffic.slot(gradient)
        feed_far, carried = run_feed_back(
            gradient,
            *feed,
            [stretches[1], stretches[3]],
            feed_pieces[1] + feed_pieces[3],
            relative[1],
            None,
            False,
        )
        carried, feed_far = traffic.slot((carried, feed_far))
        feed_sum = Reduction(feed_far, (1, 1))
        traffic.moving.append(feed_sum)
        feed_near, grad_middle, gain_c, branch = run_feed_back(
            gradient,
            *feed,
            [stretches[0], stretches[2]],
            feed_pieces[0] + feed_pieces[2],
            relative[0],
            carried,
            True,
        )
        feed_sum.near = feed_near
        feed_share = Sharing([feed_sum], 2, wide, 2)
        traffic.moving.append(feed_share)
        carried, attention_sums = None, []
        for call_groups in (tuple(range(groups - 1)), (groups - 1,)):
            if attention_sums:
                for index, (later, feed_part, attention_sum) in enumerate(summing):
                    carried, feed_part = together(carried, feed_part)
                    parted = part_columns([[feed_part]], 2, wide)
                    share = Sharing([], 2, wide, 2)
                    carried, share.sent = together(carried, parted)
                    share.send()
                    traffic.moving.append(share)
                    summing[index] = later, share, attention_sum
            branch, grad_middle, carried = traffic.slot((branch, grad_middle, carried))
            if attention_sums:
                traffic.moving.append(attention_sums[-1])
            carried, *gain_a, far, near = attend_back(
                call_groups, carried, grad_middle=grad_middle, branch=branch, places=grad_places
            )
            carried, far, near = together(carried, far, near)
            attention_sums.append(Reduction(far, (1, 1)))
            attention_sums[-1].near = near
        gradient = carried
        gains[layer] = jnp.concatenate([*gain_a, gain_c])
        traffic.moving.append(attention_sums[-1])
        attention_share = Sharing(attention_sums, 4, wide, 1)
        traffic.moving.append(attention_share)
        shares[layer] = feed_share, attention_share
    if by_permutes():
        gain_all = jnp.concatenate(gains)
        input_grad = gradient[own_place]
        gain_all = traffic.slot(gain_all)
        attention_parts = []
        for later, share, attention_sum in reversed(summing):
            parted = part_columns([attention_sum.arrays()], 4, wide)
            gain_all, parted = together(gain_all, parted)
            parted = lax.psum_scatter(parted, "head", scatter_dimension=0, tiled=True)
            attention_parts.append(parted)
            shares[later] = share, parted
        gain_all = shared_gain(shared_gain(gain_all, CORE), X)
        gain_all = traffic.slot(gain_all)
        gain_all, outputs, input_grad = together(gain_all, outputs, input_grad)
        gain_all = shared_gain(gain_all, Y)
        attention_share.gain = gain_all
        attention_parts = traffic.slot(attention_parts)
        feed_shares = [share[0].came for share in shares]
        turned = finish(feed_shares, (1, 1), up_weight.shape[1], turned=True)
        up_grad, down_grad = traffic.slot(turned)
        up_grad, down_grad = up_grad.swapaxes(1, 2), down_grad.swapaxes(1, 2)
        assert not traffic.moving
        qkv_grad, out_grad, gain_total = finish(
            [shares[0][1].came] + attention_parts, (3, 1), in_rows, 2 * layer_count
        )
        gain_total = gain_total.reshape(layer_count, 2, -1)
    else:
        gain_total = lax.psum(jnp.stack(gains), ("dp", "head"))
        input_grad = gradient[own_place]
        results = [(a[:3], a[3], f[0], f[1]) for f, a in shares]
        qkv_grad, out_grad, up_grad, down_grad = (
            jnp.stack(list(kind)) for kind in zip(*results)
        )
    return (
        outputs,
        input_grad,
        gain_total[:, 0],
        gain_total[:, 1],
        qkv_grad,
        out_grad,
        up_grad,
        down_grad,
    )


def solution(mesh):
    in_specs = (
        P(("dp", "head"), None),
        P("dp", None),
        P(None, "head", None, None),
        P(),
        P(None, None, "dp", "head"),
        P(None, "dp", "head"),
        P(None, "dp", "head"),
        P(None, "dp", "head"),
        P(("dp", "head"), None),
    )
    out_specs = (
        P(("dp", "head"), None),
        P(("dp", "head"), None),
        P(),
        P(),
        P(None, None, "dp", "head"),
        P(None, "dp", "head"),
        P(None, "dp", "head"),
        P(None, "dp", "head"),
    )
    return jax.shard_map(body, mesh=mesh, in_specs=in_specs, out_specs=out_specs, check_vma=False)
```

```python
import functools
import math

import jax
import jax.numpy as jnp
from jax import lax
from jax.experimental import pallas as pl
from jax.experimental.pallas import tpu as pltpu
from jax.sharding import PartitionSpec as P

MOST = 64
EPSILON = 1e-05
QUERY_ROWS = 128
KEY_ROWS = QUERY_ROWS + 2 * MOST
GROUP = 4
VMEM_BYTES = 60 * 2**20

BF16 = jnp.bfloat16
F32 = jnp.float32
CONTRACT_LAST = (((1,), (1,)), ((), ()))
CONTRACT_FIRST = (((0,), (0,)), ((), ()))
CONTRACT_MIDDLE = (((1,), (0,)), ((), ()))

TAIL_SCALE = 0.3275911 / math.sqrt(2.0)
TAIL_TERMS = (1.061405429, -1.453152027, 1.421413741, -0.284496736, 0.254829592)


def dot(left, right, dims=CONTRACT_MIDDLE):
    return lax.dot_general(left, right, dims, preferred_element_type=F32)


def gelu_and_slope(hidden):
    bell = jnp.exp(hidden * hidden * -0.5)
    below = 1.0 + jnp.abs(hidden) * TAIL_SCALE
    guess = pl.reciprocal(below, approx=True)
    inverse = guess * (2.0 - below * guess)
    tail = 0.5 * TAIL_TERMS[0]
    for term in TAIL_TERMS[1:]:
        tail = tail * inverse + 0.5 * term
    tail = tail * inverse * bell
    cumulative = jnp.where(hidden > 0.0, 1.0 - tail, tail)
    return hidden * cumulative, cumulative + hidden * (bell * (1.0 / math.sqrt(2.0 * math.pi)))


def normalised(values):
    centred = values - jnp.mean(values, axis=-1, keepdims=True)
    inverse = lax.rsqrt(jnp.mean(centred * centred, axis=-1, keepdims=True) + EPSILON)
    return centred * inverse, inverse


def norm_back(grad_out, gain, hat, inverse):
    scaled = grad_out * gain
    first_mean = jnp.mean(scaled, axis=-1, keepdims=True)
    second_mean = jnp.mean(scaled * hat, axis=-1, keepdims=True)
    return inverse * (scaled - first_mean - hat * second_mean)


def each_block(rows, size, step):
    for block in row_blocks(rows, size):
        step(block)


def own_block(block, rows):
    return MOST <= block.start and block.stop <= rows - MOST


def swap_halves(values, half):
    width = values.shape[-1]
    lane = lax.broadcasted_iota(jnp.int32, values.shape, len(values.shape) - 1)
    ahead = pltpu.roll(values, width - half, 1)
    behind = pltpu.roll(values, half, 1)
    return jnp.where(lane % (2 * half) < half, ahead, behind)


def two_parts(values):
    high = values.astype(BF16)
    return high, (values - high.astype(F32)).astype(BF16)


def row_blocks(rows, size):
    return [slice(begin, begin + size) for begin in range(0, rows, size)]


def spread_parts(rows, target, place):
    width = rows.shape[1]
    for index, part in enumerate((*two_parts(rows), *two_parts(rows * rows))):
        target[place, index * width : (index + 1) * width] = part


def phi_of(parts, table):
    return jnp.exp(dot(parts, table)) * (1.0 / math.sqrt(table.shape[1] // GROUP))


def head_masks(width, dtype):
    lane = lax.broadcasted_iota(jnp.int32, (1, width), 1) // (width // GROUP)
    return [jnp.where(lane == head, 1.0, 0.0).astype(dtype) for head in range(GROUP)]


def spread_heads(values):
    return jnp.concatenate([values * mask for mask in head_masks(values.shape[1], BF16)], axis=0)


def gather_heads(values):
    masks = head_masks(values.shape[-1], F32)
    total = values[0] * masks[0]
    for head in range(1, GROUP):
        total = total + values[head] * masks[head]
    return total


def block_scores(phi_q, phi_k, ids_column, ids_row):
    scores = dot(phi_q, phi_k, CONTRACT_LAST)
    same = (ids_column == ids_row).astype(F32)
    scores = scores.reshape(GROUP, QUERY_ROWS, KEY_ROWS) * same[None]
    totals = jnp.sum(scores, axis=-1, keepdims=True)
    inverse = jnp.where(totals > 0.0, 1.0 / totals, 0.0)
    return scores * inverse, inverse, same


def query_blocks(rows):
    for index, block in enumerate(row_blocks(rows, QUERY_ROWS)):
        begin = min(max(block.start - MOST, 0), rows - KEY_ROWS)
        yield index, block, slice(begin, begin + KEY_ROWS)


def attention_forward(
    scale,
    piece_count,
    places,
    state,
    gain_1,
    gain_2,
    table,
    cosine,
    sine,
    ids_column,
    ids_row,
    *others,
):
    pieces = others[:piece_count]
    weights_out, normed_a, query, key, value, mixed, middle, normed_c, *others = others[piece_count:]
    weights, total, projected, parts, phi, arrived, leaving = others
    group = pl.program_id(0)
    groups = weights.shape[0]
    rows = state.shape[0]
    wide = query.shape[1]
    deep = weights.shape[2]
    half = cosine.shape[1] // GROUP // 2

    def columns_of(at):
        return pl.ds(at * deep, deep)

    def arriving_at(at):
        for index, piece in enumerate(pieces):
            place = pl.ds(pl.multiple_of(places[index], 16), piece.shape[0])
            yield pltpu.make_async_copy(
                piece.at[:, columns_of(at)], weights.at[at, place, :], arrived.at[at, index]
            )

    def leaving_at(at):
        return pltpu.make_async_copy(
            weights.at[at], weights_out.at[:, columns_of(at)], leaving.at[at]
        )

    @pl.when(group == 0)
    def _():
        for at in range(groups):
            for copy in arriving_at(at):
                copy.start()

        def step(block):
            hat, _ = normalised(state[block, :])
            normed_a[block, :] = (hat * gain_1[...]).astype(BF16)
            total[block, :] = state[block, :]

        each_block(rows, 64, step)

    for at in range(groups):

        @pl.when(group == at)
        def _(at=at):
            for copy in arriving_at(at):
                copy.wait()
            leaving_at(at).start()

    projected[...] = dot(normed_a[...], weights[group, :, : 3 * wide])
    for block in row_blocks(rows, 64):
        for part, held in enumerate((query, key)):
            values = projected[block, part * wide : (part + 1) * wide]
            turned = values * cosine[block, :] + swap_halves(values, half) * sine[block, :]
            turned = turned * scale
            held[block, :] = turned
            spread_parts(turned, parts, slice(part * rows + block.start, part * rows + block.stop))
        value[block, :] = projected[block, 2 * wide :].astype(BF16)
    phi[...] = phi_of(parts[...], table[0]).astype(BF16)

    for index, block, keys in query_blocks(rows):
        scores, _, _ = block_scores(
            spread_heads(phi[block, :]),
            phi[rows + keys.start : rows + keys.stop, :],
            ids_column[block, :],
            ids_row[index],
        )
        scores = scores.reshape(GROUP * QUERY_ROWS, KEY_ROWS).astype(BF16)
        found = dot(scores, value[keys, :])
        mixed[block, :] = gather_heads(found.reshape(GROUP, QUERY_ROWS, -1)).astype(BF16)

    total[...] += dot(mixed[...], weights[group, :, 3 * wide :], CONTRACT_LAST)

    @pl.when(group == groups - 1)
    def _():
        def step(block):
            middle[block, :] = total[block, :]
            hat, _ = normalised(total[block, :])
            normed_c[block, :] = (hat * gain_2[...]).astype(BF16)

        each_block(rows, 64, step)
        for at in range(groups):
            leaving_at(at).wait()


class Arrivals:
    def __init__(self, semaphores):
        self.semaphores, self.copies = semaphores, []

    def start(self, source, target):
        copy = pltpu.make_async_copy(source, target, self.semaphores.at[len(self.copies)])
        copy.start()
        self.copies.append(copy)
        return copy


def attention_backward(first, last, scale, groups, split, places, branch_in, weights_in, mixed_in, query_in, key_in, value_in, *others):
    normed_in, cosine_in, sine_in, *others = others
    if not first:
        total_in, *others = others
    if last:
        grad_middle, state, gain_1, *others = others
    table, back_table, ids_column, ids_row, *others = others
    if last:
        grad_state, grad_gain, *others = others
    else:
        total_out, *others = others
    grad_targets, others = others[: 1 + split], others[1 + split :]
    (
        branch,
        weights,
        mixed,
        query,
        key,
        value,
        normed_a,
        cosine,
        sine,
        total,
        grad_weight,
        grad_mixed,
        parts,
        phi,
        grad_phi,
        grad_value,
        grad_parts,
        grad_projected,
        arrived,
        leaving,
    ) = others
    _, rows, wide = query.shape
    half = wide // GROUP // 2
    own_rows = rows - 2 * MOST
    own = pl.ds(MOST, own_rows)
    small = phi.shape[1]
    deep = weights.shape[2]
    arrivals = Arrivals(arrived)
    got_branch = arrivals.start(branch_in, branch)
    got = []
    for at, group in enumerate(groups):
        columns_in = pl.ds(group * wide, wide)
        got.append(
            (
                arrivals.start(
                    weights_in.at[:, pl.ds(group * deep + 3 * wide, wide)],
                    weights.at[at, :, pl.ds(3 * wide, wide)],
                ),
                arrivals.start(query_in.at[:, columns_in], query.at[at]),
                arrivals.start(key_in.at[:, columns_in], key.at[at]),
                arrivals.start(mixed_in.at[own, columns_in], mixed.at[at]),
                arrivals.start(value_in.at[:, columns_in], value.at[at]),
                arrivals.start(
                    weights_in.at[:, pl.ds(group * deep, 3 * wide)],
                    weights.at[at, :, pl.ds(0, 3 * wide)],
                ),
            )
        )
        if at == 0:
            got_shared = [
                arrivals.start(cosine_in, cosine),
                arrivals.start(sine_in, sine),
                arrivals.start(normed_in.at[own, :], normed_a),
            ]
    if not first:
        got_total = arrivals.start(total_in, total)
    got_branch.wait()
    count = leaving.shape[1]
    size = grad_weight.shape[1] // count
    copies = []
    for at in range(len(groups)):
        got_last, *got_rows, got_first = got[at]
        got_last.wait()
        for copy in got_rows:
            copy.wait()
        grad_mixed[...] = dot(branch[...], weights[at, :, 3 * wide :]).astype(BF16)
        for block in row_blocks(rows, 64):
            for part, held in enumerate((query, key)):
                place = slice(part * rows + block.start, part * rows + block.stop)
                spread_parts(held[at, block, :], parts, place)
        phi[...] = phi_of(parts[...], table[at])
        grad_phi[rows:, :] = jnp.zeros((rows, small), F32)
        grad_value[...] = jnp.zeros_like(grad_value)
        found = dot(branch[own, :], mixed[at], CONTRACT_FIRST)
        grad_weight[at, :, 3 * wide :] = found.astype(BF16)

        for index, block, keys in query_blocks(rows):
            far_keys = slice(rows + keys.start, rows + keys.stop)
            spread_q = spread_heads(phi[block, :].astype(BF16))
            spread_grad = spread_heads(grad_mixed[block, :])
            keys_phi = phi[far_keys, :].astype(BF16)
            scores, inverse, same = block_scores(
                spread_q, keys_phi, ids_column[block, :], ids_row[index]
            )
            flat = (GROUP * QUERY_ROWS, KEY_ROWS)
            grad_scores = dot(spread_grad, value[at, keys, :], CONTRACT_LAST)
            grad_value[keys, :] += dot(
                scores.reshape(flat).astype(BF16), spread_grad, CONTRACT_FIRST
            )
            grad_scores = grad_scores.reshape(scores.shape)
            inner = jnp.sum(grad_scores * scores, axis=-1, keepdims=True)
            grad_scores = ((grad_scores - inner) * inverse * same[None]).astype(BF16).reshape(flat)
            found = dot(grad_scores, keys_phi)
            grad_phi[block, :] = gather_heads(found.reshape(GROUP, QUERY_ROWS, -1))
            grad_phi[far_keys, :] += dot(grad_scores, spread_q, CONTRACT_FIRST)

        if at == 0:
            for copy in got_shared:
                copy.wait()
        got_first.wait()
        for block in row_blocks(2 * rows, 128):
            high, low = two_parts(grad_phi[block, :] * phi[block, :])
            grad_parts[block, :small] = high
            grad_parts[block, small:] = low
        for part, held in enumerate((query, key)):
            for block in row_blocks(rows, 128):
                there = slice(part * rows + block.start, part * rows + block.stop)
                both = dot(grad_parts[there, :], back_table[at], CONTRACT_LAST)
                grad_rows = (both[:, :wide] - held[at, block, :] * both[:, wide:]) * scale
                turned = grad_rows * cosine[block, :]
                turned = turned + swap_halves(grad_rows * sine[block, :], half)
                grad_projected[block, part * wide : (part + 1) * wide] = turned.astype(BF16)
        grad_projected[:, 2 * wide :] = grad_value[...].astype(BF16)
        found = dot(normed_a[...], grad_projected[own, :], CONTRACT_FIRST)
        grad_weight[at, :, : 3 * wide] = found.astype(BF16)
        for index in range(count):
            place = pl.ds(pl.multiple_of(places[index], 16), size) if split else pl.ds(0, size)
            each = count // len(grad_targets)
            target = grad_targets[index // each]
            to = pl.ds(index % each * size, size)
            copies.append(
                pltpu.make_async_copy(
                    grad_weight.at[at, place, :],
                    target.at[to, pl.ds(at * deep, deep)],
                    leaving.at[at, index],
                )
            )
            copies[-1].start()
        back = dot(grad_projected[...], weights[at, :, : 3 * wide], CONTRACT_LAST)
        ending = at == len(groups) - 1
        if at == 0 and not first:
            got_total.wait()
        if at > 0 or not first:
            back = total[...] + back
        if ending and not last:
            total_out[...] = back
        else:
            total[...] = back
    if last:
        grad_gain[...] = jnp.zeros_like(grad_gain)

        def step(block):
            hat, inverse = normalised(state[block, :])
            back = norm_back(total[block, :], gain_1[...], hat, inverse)
            grad_state[block, :] = grad_middle[block, :] + back
            if own_block(block, rows):
                grad_gain[...] += jnp.sum(total[block, :] * hat, axis=0, keepdims=True)

        each_block(rows, 64, step)
    for copy in copies:
        copy.wait()


def adding(stages, *others):
    takes = [2 if stage == 0 else 6 for stage in stages]
    targets = others[sum(takes) :]
    begin = 0
    for index, (stage, count) in enumerate(zip(stages, takes)):
        kernel = adding_corner if stage == 0 else adding_sides
        kernel(*others[begin : begin + count], *targets[2 * index : 2 * index + 2])
        begin += count


def begins_of(pieces):
    begins = [0]
    for piece in pieces:
        begins.append(begins[-1] + piece.shape[0])
    return begins


def hidden_chunks(count):
    return [slice(begin, min(begin + CHUNK, count)) for begin in range(0, count, CHUNK)]


def feed_forward(piece_count, carried_in, normed_in, *others):
    pieces = others[:piece_count]
    activated_out, slope_out, state_out, *others = others[piece_count:]
    held, carried, normed_c, hidden, activated, slope, arrived, leaving = others
    rows, width = carried.shape
    count = held.shape[0]
    begins = begins_of(pieces)
    copies = [
        pltpu.make_async_copy(
            piece, held.at[pl.ds(begins[index], piece.shape[0]), :], arrived.at[index]
        )
        for index, piece in enumerate(pieces)
    ]
    norm_copy = pltpu.make_async_copy(normed_in, normed_c, arrived.at[piece_count])
    carried_copy = pltpu.make_async_copy(carried_in, carried, arrived.at[piece_count + 1])
    norm_copy.start()
    for copy in copies:
        copy.start()
    carried_copy.start()
    norm_copy.wait()
    chunks = hidden_chunks(count)
    waited = 0
    outgoing = []

    def project(chunk):
        hidden[:, chunk] = dot(normed_c[...], held[chunk, :width], CONTRACT_LAST)

    def wait_until(row):
        nonlocal waited
        while waited < piece_count and begins[waited] < row:
            copies[waited].wait()
            waited += 1

    wait_until(chunks[0].stop)
    project(chunks[0])
    wait_until(count)
    for index, chunk in enumerate(chunks):
        if index + 1 < len(chunks):
            project(chunks[index + 1])
        for block in row_blocks(rows, 32):
            value, back = gelu_and_slope(hidden[block, chunk])
            activated[block, chunk] = value.astype(BF16)
            slope[block, chunk] = back.astype(BF16)
        for target, source in ((activated_out, activated), (slope_out, slope)):
            outgoing.append(
                pltpu.make_async_copy(
                    source.at[:, chunk], target.at[:, chunk], leaving.at[len(outgoing)]
                )
            )
            outgoing[-1].start()
    carried_copy.wait()
    carried[...] += dot(activated[...], held[:, width:])
    outgoing.append(pltpu.make_async_copy(carried, state_out, leaving.at[len(outgoing)]))
    outgoing[-1].start()
    for copy in outgoing:
        copy.wait()


def feed_back(first, last, segments, piece_count, places, gradient_in, middle, gain_2, normed_in, *others):
    kept, others = others[: 2 * len(segments)], others[2 * len(segments) :]
    if not first:
        total_in, *others = others
    pieces = others[:piece_count]
    grad_out, grad_middle, *others = others[piece_count:]
    if last:
        grad_gain, grad_attn, *others = others
    (
        held,
        gradient,
        normed_c,
        activated,
        slope,
        total,
        branch,
        grad_hidden,
        grad_weight,
        arrived,
        leaving,
    ) = others
    rows, width = gradient.shape
    own_rows = rows - 2 * MOST
    own = pl.ds(MOST, own_rows)
    count = held.shape[0]
    begins = begins_of(pieces)
    arrivals = Arrivals(arrived)
    left, right = pl.ds(0, width), pl.ds(width, width)

    def weight_half(half):
        return [
            arrivals.start(
                piece.at[:, half], held.at[pl.ds(begins[index], piece.shape[0]), half]
            )
            for index, piece in enumerate(pieces)
        ]

    def leave(half, offset):
        copies = []
        for index, piece in enumerate(pieces):
            size = piece.shape[0]
            copies.append(
                pltpu.make_async_copy(
                    grad_weight.at[pl.ds(begins[index], size), half],
                    grad_out.at[pl.ds(pl.multiple_of(places[index], 16), size), half],
                    leaving.at[offset + index],
                )
            )
            copies[-1].start()
        return copies

    def stretch(which, rows_taken, target):
        copies, begin = [], 0
        for index, (column, size) in enumerate(segments):
            source = kept[2 * index + which].at[rows_taken, pl.ds(column, size)]
            copies.append(arrivals.start(source, target.at[:, pl.ds(begin, size)]))
            begin += size
        return copies

    got_gradient = arrivals.start(gradient_in, gradient)
    got_act = stretch(0, own, activated)
    got_down = weight_half(right)
    got_slope = stretch(1, pl.ds(0, rows), slope)
    got_norm = arrivals.start(normed_in.at[own, :], normed_c)
    got_up = weight_half(left)
    if not first:
        got_total = arrivals.start(total_in, total)
    got_gradient.wait()
    for block in row_blocks(rows, 64):
        branch[block, :] = gradient[block, :].astype(BF16)
    for copy in got_act:
        copy.wait()
    for chunk in row_blocks(count, count // 2):
        found = dot(activated[:, chunk], branch[own, :], CONTRACT_FIRST)
        grad_weight[chunk, width:] = found.astype(BF16)
    down_leaves = leave(right, 0)
    for copy in got_down + got_slope:
        copy.wait()
    for chunk in hidden_chunks(count):
        grad_act = dot(branch[...], held[chunk, width:], CONTRACT_LAST)
        grad_hidden[:, chunk] = (grad_act * slope[:, chunk].astype(F32)).astype(BF16)
    for copy in [got_norm] + got_up:
        copy.wait()
    for chunk in row_blocks(count, count // 2):
        found = dot(grad_hidden[MOST : MOST + own_rows, chunk], normed_c[...], CONTRACT_FIRST)
        grad_weight[chunk, :width] = found.astype(BF16)
    up_leaves = leave(left, piece_count)
    back = dot(grad_hidden[...], held[:, :width])
    if not first:
        got_total.wait()
        back = total[...] + back
    if not last:
        grad_middle[...] = back
    else:
        total[...] = back
        grad_gain[...] = jnp.zeros_like(grad_gain)

        def step(block):
            hat, inverse = normalised(middle[block, :])
            back = gradient[block, :] + norm_back(total[block, :], gain_2[...], hat, inverse)
            grad_middle[block, :] = back
            grad_attn[block, :] = back.astype(BF16)
            if own_block(block, rows):
                grad_gain[...] += jnp.sum(total[block, :] * hat, axis=0, keepdims=True)

        each_block(rows, 64, step)
    for copy in down_leaves + up_leaves:
        copy.wait()


def column_runs(parts, part, begin, width, group_width):
    stop = begin + width
    while begin < stop:
        group = begin // group_width
        end = min(stop, (group + 1) * group_width)
        place = group * parts * group_width + part * group_width + begin % group_width
        yield begin, end, place
        begin = end


def joining(parts, begin, group_width, source_in, joined, source, arrived):
    copy = pltpu.make_async_copy(source_in, source, arrived)
    copy.start()
    copy.wait()
    rows = joined.shape[0]
    count = source.shape[0]
    width = joined.shape[1] // parts // count
    across = source.shape[2] // width
    for part in range(parts):
        top = begin + part // across * rows
        left = part % across * width
        side = [source[at, top : top + rows, left : left + width] for at in range(count)]
        side = jnp.concatenate(side, axis=1)
        for first, end, place in column_runs(parts, part, 0, count * width, group_width):
            joined[:, place : place + end - first] = side[:, first:end]


def tabulating(begin, source, *others):
    layers = len(others) // 2
    groups, _, small = others[0].shape
    feats = small // GROUP
    own_heads = groups * GROUP // source.shape[0]
    wide = others[layers].shape[1] // 2
    deep = wide // GROUP
    thin = source.shape[1] - begin
    runs = deep // thin
    run_width = layers * own_heads * feats
    for target in others:
        target[...] = jnp.zeros_like(target)
    for layer in range(layers):
        tables, back_tables = others[layer], others[layers + layer]
        for index in range(groups * GROUP):
            group, place = index // GROUP, index % GROUP
            column = (layer * own_heads + index % own_heads) * feats
            across = slice(place * feats, (place + 1) * feats)
            again = slice(small + place * feats, small + (place + 1) * feats)
            for part in range(4):
                for run in range(runs):
                    top = part * wide + place * deep + run * thin
                    down = slice(top, top + thin)
                    if part < 2:
                        at = run * run_width + column
                        value = source[index // own_heads, begin : begin + thin, at : at + feats]
                    else:
                        value = jnp.full((thin, feats), -0.5, BF16)
                    tables[group, down, across] = value
                    if part < 2:
                        value = value if part < 1 else jnp.ones((thin, feats), BF16)
                        back_tables[group, down, across] = value
                        back_tables[group, down, again] = value


def parting(parts, group_width, pieces, gains, *others):
    if gains:
        gain, *others = others
    *sources, target = others
    count, rows, all_width = target.shape
    if gains:
        rows -= GAIN_ROWS
        left, done = gain[...], 0
        for _ in range(3):
            part = left.astype(BF16)
            left = left - part.astype(F32)
            for at in range(count):
                target[at, rows + done : rows + done + gains, :] = part
            done += gains
        target[:, rows + done :, :] = jnp.zeros((count, GAIN_ROWS - done, all_width), BF16)
    width = all_width // parts
    each = len(sources) // pieces
    starts = [0]
    for piece in range(pieces - 1):
        starts.append(starts[-1] + sources[piece * each].shape[1])
    for part in range(parts):
        for at in range(count):
            runs = []
            for begin, end, place in column_runs(parts, part, at * width, width, group_width):
                piece = max(at for at in range(pieces) if starts[at] <= place)
                run = slice(place - starts[piece], place - starts[piece] + end - begin)
                mine = sources[piece * each : (piece + 1) * each]
                total = mine[0][:, run].astype(F32)
                for source in mine[1:]:
                    total = total + source[:, run].astype(F32)
                runs.append(total)
            total = runs[0] if len(runs) == 1 else jnp.concatenate(runs, axis=1)
            target[at, :rows, part * width : (part + 1) * width] = total.astype(target.dtype)


def finishing(parts, gains, turned, *others):
    if gains:
        *others, gain_out = others
        total = 0.0
        first = others[0]
        rows = first.shape[1] - GAIN_ROWS
        for at in range(first.shape[0]):
            for part in range(3):
                begin = rows + part * gains
                total = total + first[at, begin : begin + gains, :].astype(F32)
        gain_out[...] = total
    sources, targets = others[: -len(parts)], others[-len(parts) :]
    rows = targets[0].shape[-1 if turned else -2]
    for layer, source in enumerate(sources):
        begin = 0
        for target, count in zip(targets, parts):
            for part in range(count):
                width = target.shape[-2 if turned else -1]
                run = slice(begin, begin + width)
                total = source[0, :rows, run].astype(F32)
                for at in range(1, source.shape[0]):
                    total = total + source[at, :rows, run].astype(F32)
                if turned:
                    target[layer] = total.T
                elif count > 1:
                    target[layer, part] = total
                else:
                    target[layer] = total
                begin += width


def turning(cosine_in, sine_in, ids_in, cosine, sine, ids_column):
    half = cosine_in.shape[0]
    down = cosine_in[...].T
    across = sine_in[...].T
    for head in range(cosine.shape[1] // (2 * half)):
        for part in range(2):
            place = slice((2 * head + part) * half, (2 * head + part + 1) * half)
            cosine[:, place] = down
            sine[:, place] = across if part else -across
    ids_column[...] = ids_in[...].T[:, :1].astype(jnp.int32)


def adding_corner(near, far, to_x, to_y):
    half = to_x.shape[0]
    for target, place in ((to_x, slice(0, half)), (to_y, slice(half, 2 * half))):
        target[...] = (near[place, :].astype(F32) + far[place, :].astype(F32)).astype(BF16)


def adding_sides(near_x, far_x, near_y, far_y, from_x, from_y, to_x, to_y):
    half = from_x.shape[0]
    top, bottom = slice(0, half), slice(half, 2 * half)
    for near, far, place, more, target in (
        (near_x, far_x, top, None, to_x),
        (near_x, far_x, bottom, from_y, to_x),
        (near_y, far_y, top, from_x, to_y),
        (near_y, far_y, bottom, None, to_y),
    ):
        total = near[place, :].astype(F32) + far[place, :].astype(F32)
        if more is not None:
            total = total + more[...].astype(F32)
        target[place, :] = total.astype(BF16)


def whole(shape):
    return pl.BlockSpec(
        shape, lambda step, *_: (0,) * len(shape), pipeline_mode=pl.Buffered(buffer_count=1)
    )


def columns(rows, width):
    return pl.BlockSpec((rows, width), lambda step, *_: (0, step))


def leading(shape):
    return pl.BlockSpec(shape, lambda step, *_: (step,) + (0,) * (len(shape) - 1))


def struct(shape, dtype):
    return jax.ShapeDtypeStruct(shape, dtype)


ANYWHERE = pl.BlockSpec(memory_space=pltpu.HBM)


def kernel_call(kernel, steps, in_specs, out_specs, out_shape, scratch, flops, prefetch=0):
    return pl.pallas_call(
        kernel,
        grid_spec=pltpu.PrefetchScalarGridSpec(
            num_scalar_prefetch=prefetch,
            grid=(steps,),
            in_specs=in_specs,
            out_specs=out_specs,
            scratch_shapes=scratch,
        ),
        out_shape=out_shape,
        compiler_params=pltpu.CompilerParams(vmem_limit_bytes=VMEM_BYTES),
        cost_estimate=pl.CostEstimate(flops=flops, bytes_accessed=flops // 600, transcendentals=0),
    )


def run_attention_forward(state, gains, pieces, places, table, *, tables, ids, scale):
    rows, width = state.shape
    wide = tables[0].shape[1]
    groups, deep, small = table.shape
    blocks = rows // QUERY_ROWS
    return kernel_call(
        functools.partial(attention_forward, scale, len(pieces)),
        groups,
        [
            whole((rows, width)),
            whole((1, width)),
            whole((1, width)),
            leading((1, deep, small)),
            whole((rows, wide)),
            whole((rows, wide)),
            whole((rows, 1)),
            whole((blocks, 1, KEY_ROWS)),
            *[ANYWHERE for _ in pieces],
        ],
        [
            ANYWHERE,
            whole((rows, width)),
            columns(rows, wide),
            columns(rows, wide),
            columns(rows, wide),
            columns(rows, wide),
            whole((rows, width)),
            whole((rows, width)),
        ],
        [
            struct((width, 4 * width), BF16),
            struct((rows, width), BF16),
            struct((rows, width), F32),
            struct((rows, width), F32),
            struct((rows, width), BF16),
            struct((rows, width), BF16),
            struct((rows, width), F32),
            struct((rows, width), BF16),
        ],
        [
            pltpu.VMEM((groups, width, 4 * wide), BF16),
            pltpu.VMEM((rows, width), F32),
            pltpu.VMEM((rows, 3 * wide), F32),
            pltpu.VMEM((2 * rows, deep), BF16),
            pltpu.VMEM((2 * rows, small), BF16),
            pltpu.SemaphoreType.DMA((groups, len(pieces))),
            pltpu.SemaphoreType.DMA((groups,)),
        ],
        FORWARD_COST,
        1,
    )(places, state, gains[0], gains[1], table, *tables, *ids, *pieces)


def run_attention_backward(
    groups,
    carried,
    *,
    grad_middle,
    branch,
    state,
    gain,
    weights,
    places,
    table,
    back_table,
    tables,
    ids,
    kept,
    scale,
):
    rows, width = state.shape
    wide = tables[0].shape[1]
    all_groups, deep, small = table.shape
    first, last = groups[0] == 0, groups[-1] == all_groups - 1
    count = len(groups)
    normed_a, query, key, value, mixed = kept
    own_rows = rows - 2 * MOST
    blocks = rows // QUERY_ROWS
    copied = [branch, weights, mixed, query, key, value, normed_a, *tables]
    ending = [grad_middle, state, gain] if last else []
    split = places.shape[0] > 1
    halves = 1 + split
    return kernel_call(
        functools.partial(attention_backward, first, last, scale, groups, split),
        1,
        [
            *[ANYWHERE] * (len(copied) + (not first)),
            *([whole((rows, width)), whole((rows, width)), whole((1, width))] if last else []),
            pl.BlockSpec((count, deep, small), lambda *_: (groups[0] // count, 0, 0)),
            pl.BlockSpec((count,) + back_table.shape[1:], lambda *_: (groups[0] // count, 0, 0)),
            whole((rows, 1)),
            whole((blocks, 1, KEY_ROWS)),
        ],
        [
            *([whole((rows, width)), whole((1, width))] if last else [whole((rows, width))]),
            *[ANYWHERE] * halves,
        ],
        [
            struct((rows, width), F32),
            *([struct((1, width), F32)] if last else []),
            *[struct((width // halves, count * 4 * wide), BF16)] * halves,
        ],
        [
            pltpu.VMEM((rows, width), BF16),
            pltpu.VMEM((count, width, 4 * wide), BF16),
            pltpu.VMEM((count, own_rows, wide), BF16),
            pltpu.VMEM((count, rows, wide), F32),
            pltpu.VMEM((count, rows, wide), F32),
            pltpu.VMEM((count, rows, wide), BF16),
            pltpu.VMEM((own_rows, width), BF16),
            pltpu.VMEM((rows, wide), F32),
            pltpu.VMEM((rows, wide), F32),
            pltpu.VMEM((rows, width), F32),
            pltpu.VMEM((count, width, 4 * wide), BF16),
            pltpu.VMEM((rows, wide), BF16),
            pltpu.VMEM((2 * rows, deep), BF16),
            pltpu.VMEM((2 * rows, small), F32),
            pltpu.VMEM((2 * rows, small), F32),
            pltpu.VMEM((rows, wide), F32),
            pltpu.VMEM((2 * rows, 2 * small), BF16),
            pltpu.VMEM((rows, 3 * wide), BF16),
            pltpu.SemaphoreType.DMA((5 + 6 * count,)),
            pltpu.SemaphoreType.DMA((count,) + places.shape),
        ],
        BACKWARD_COST // 3 * count,
        1,
    )(
        places,
        *copied,
        *([] if first else [carried]),
        *ending,
        table,
        back_table,
        *ids,
    )


def run_feed_forward(carried, normed_c, pieces):
    rows, width = carried.shape
    count = sum(piece.shape[0] for piece in pieces)
    return kernel_call(
        functools.partial(feed_forward, len(pieces)),
        1,
        [ANYWHERE] * (2 + len(pieces)),
        [ANYWHERE] * 3,
        [
            struct((rows, count), BF16),
            struct((rows, count), BF16),
            struct((rows, width), F32),
        ],
        [
            pltpu.VMEM((count, 2 * width), BF16),
            pltpu.VMEM((rows, width), F32),
            pltpu.VMEM((rows, width), BF16),
            pltpu.VMEM((rows, count), F32),
            pltpu.VMEM((rows, count), BF16),
            pltpu.VMEM((rows, count), BF16),
            pltpu.SemaphoreType.DMA((len(pieces) + 2,)),
            pltpu.SemaphoreType.DMA((2 * len(hidden_chunks(count)) + 1,)),
        ],
        FORWARD_COST // 3,
    )(carried, normed_c, *pieces)


def kept_stretches(near_kept, far_kept, corner_kept):
    side, corner = near_kept[0].shape[1], corner_kept[0].shape[1] // 2
    return [
        (near_kept[:2], 0, side),
        (far_kept[:2], 0, side),
        (corner_kept[:2], 0, corner),
        (corner_kept[:2], corner, corner),
    ]


def run_feed_back(gradient, middle, gain, normed_c, stretches, pieces, places, carried, last):
    rows, width = middle.shape
    count = sum(piece.shape[0] for piece in pieces)
    first = carried is None
    kept = [array for arrays, _, _ in stretches for array in arrays]
    segments = [(column, size) for _, column, size in stretches]
    arrivals = 2 + not_first(first) + 2 * len(pieces) + len(kept)
    return kernel_call(
        functools.partial(feed_back, first, last, segments, len(pieces)),
        1,
        [
            ANYWHERE,
            whole((rows, width)),
            whole((1, width)),
            *[ANYWHERE] * (1 + len(kept) + not_first(first) + len(pieces)),
        ],
        [
            ANYWHERE,
            whole((rows, width)),
            *([whole((1, width)), whole((rows, width))] if last else []),
        ],
        [
            struct((count, 2 * width), BF16),
            struct((rows, width), F32),
            *([struct((1, width), F32), struct((rows, width), BF16)] if last else []),
        ],
        [
            pltpu.VMEM((count, 2 * width), BF16),
            pltpu.VMEM((rows, width), F32),
            pltpu.VMEM((rows - 2 * MOST, width), BF16),
            pltpu.VMEM((rows - 2 * MOST, count), BF16),
            pltpu.VMEM((rows, count), BF16),
            pltpu.VMEM((rows, width), F32),
            pltpu.VMEM((rows, width), BF16),
            pltpu.VMEM((rows, count), BF16),
            pltpu.VMEM((count, 2 * width), BF16),
            pltpu.SemaphoreType.DMA((arrivals,)),
            pltpu.SemaphoreType.DMA((2 * len(pieces),)),
        ],
        FORWARD_COST // 2,
        1,
    )(
        places,
        gradient,
        middle,
        gain,
        normed_c,
        *kept,
        *([] if first else [carried]),
        *pieces,
    )


def not_first(first):
    return 0 if first else 1


HEAD_DEVICES = 4
CHUNK = 512
GAIN_ROWS = 16
X, Y, CORE = 2, 4, 1
FORWARD_COST = 29_000_000_000
BACKWARD_COST = 40_000_000_000


def hop(values, bit):
    count = lax.axis_size("dp")
    return lax.ppermute(values, "dp", [(i, i ^ bit) for i in range(count)])


def exchange(values):
    return lax.all_to_all(values, "head", split_axis=0, concat_axis=0, tiled=True)


def together(*values):
    return lax.optimization_barrier(values)


def by_permutes():
    return lax.axis_size("dp") == 8 and lax.axis_size("head") == HEAD_DEVICES


def group_width(parts, width, wide):
    return wide if parts == 4 else width


def join_columns(source, parts, begin, rows, width, wide):
    count = source.shape[0]
    return kernel_call(
        functools.partial(joining, parts, begin, group_width(parts, count * width, wide)),
        1,
        [ANYWHERE],
        whole((rows, parts * count * width)),
        struct((rows, parts * count * width), BF16),
        [pltpu.VMEM(source.shape, BF16), pltpu.SemaphoreType.DMA],
        1_000_000,
    )(source)


def feature_tables(source, begin, shapes):
    return kernel_call(
        functools.partial(tabulating, begin),
        1,
        [whole(source.shape)],
        [whole(shape) for shape in shapes],
        [struct(shape, BF16) for shape in shapes],
        [],
        1_000_000,
    )(source)


def block_of(rows, columns_all, index):
    return pl.BlockSpec((rows, columns_all), lambda *_: (index, 0))


def part_columns(pieces, parts, wide, gain=None):
    rows = pieces[0][-1].shape[0]
    columns_all = sum(piece[0].shape[1] for piece in pieces)
    gains = 0 if gain is None else gain.shape[0]
    shape = (
        HEAD_DEVICES,
        rows + (GAIN_ROWS if gains else 0),
        columns_all // HEAD_DEVICES,
    )
    return kernel_call(
        functools.partial(
            parting, parts, group_width(parts, columns_all // parts, wide), len(pieces), gains
        ),
        1,
        [
            *([whole(gain.shape)] if gains else []),
            *[block_of(rows, source.shape[1], 0) for piece in pieces for source in piece],
        ],
        whole(shape),
        struct(shape, BF16),
        [],
        1_000_000,
    )(*([gain] if gains else []), *[source for piece in pieces for source in piece])


def finish(sources, parts, rows, gains=0, turned=False):
    all_width = sources[0].shape[2]
    width = all_width // sum(parts)
    shapes = [
        (len(sources), count, rows, width) if count > 1 else (len(sources), rows, width)
        for count in parts
    ]
    if turned:
        shapes = [(len(sources), width, rows) for _ in parts]
    if gains:
        shapes.append((gains, all_width))
    return kernel_call(
        functools.partial(finishing, parts, gains, turned),
        1,
        [whole(source.shape) for source in sources],
        [whole(shape) for shape in shapes],
        [struct(shape, F32) for shape in shapes],
        [],
        1_000_000,
    )(*sources)


def next_chips(own):
    return hop(own, X), hop(own, Y), hop(own, CORE)


def halves_to_pass(over_x, over_y):
    half = over_x.shape[0] // 2
    return over_x[:half], over_y[half:]


def chip_across(passed):
    to_y, to_x = passed
    return hop(to_y, Y), hop(to_x, X)


def other_core(pieces):
    return tuple(hop(piece, CORE) for piece in pieces)


def piece_places(rows, order=range(10)):
    own = lax.axis_index("dp")
    bits = [(0, 0), (X, 0), (Y, 0), (X | Y, 0), (X | Y, rows // 2)]
    places = [(own ^ (bit | core)) * rows + begin for core in (0, CORE) for bit, begin in bits]
    return jnp.stack([places[at] for at in order]).astype(jnp.int32)


def block_places(rows):
    own = lax.axis_index("dp")
    return jnp.stack(
        [(own ^ (bit | core)) * rows for core in (CORE, 0) for bit in (0, X, Y, X | Y)]
    ).astype(jnp.int32)


class Reduction:
    def __init__(self, far, slow):
        self.slow, self.stage, self.left = slow, 0, 1
        self.came = hop(far, CORE)

    def operands(self):
        rows = self.near.shape[0] // 4
        half = rows // 2
        if self.stage == 0:
            self.far = self.came
            return [(self.near, rows, 3), (self.far, rows, 3)], half
        sides = [(array, rows, at) for at in (1, 2) for array in (self.near, self.far)]
        return sides + [(array, half, 0) for array in self.came], rows

    def send(self):
        to_x, to_y = self.sent
        self.came = hop(to_x, X), hop(to_y, Y)
        self.stage += 1
        self.left = self.slow[self.stage - 1]

    def arrays(self):
        return [self.near, self.far, *self.came]


def prepare(reductions):
    arrays, in_specs, out_specs, shapes = [], [], [], []
    for reduction in reductions:
        operands, out_rows = reduction.operands()
        width = reduction.near.shape[1]
        for array, rows, at in operands:
            arrays.append(array)
            in_specs.append(block_of(rows, width, at))
        out_specs += [whole((out_rows, width))] * 2
        shapes += [struct((out_rows, width), BF16)] * 2
    sent = kernel_call(
        functools.partial(adding, [reduction.stage for reduction in reductions]),
        1,
        in_specs,
        out_specs,
        shapes,
        [],
        1_000_000,
    )(*arrays)
    for index, reduction in enumerate(reductions):
        reduction.sent = sent[2 * index : 2 * index + 2]


class Sharing:
    def __init__(self, reductions, parts, wide, slow):
        self.reductions, self.parts, self.wide, self.slow = reductions, parts, wide, slow
        self.stage, self.left, self.came, self.gain = 0, 0, (), None

    def prepare(self):
        pieces = [reduction.arrays() for reduction in self.reductions]
        self.sent = part_columns(pieces, self.parts, self.wide, self.gain)

    def send(self):
        self.came = exchange(self.sent)
        self.stage, self.left = 1, self.slow


class Traffic:
    def __init__(self):
        self.moving = []

    def slot(self, values):
        ready = []
        for item in self.moving:
            item.left -= 1
            if item.left <= 0:
                ready.append(item)
        values, came = together(values, [item.came for item in ready])
        for item, arrived in zip(ready, came):
            item.came = arrived
        sending = []
        for item in ready:
            if isinstance(item, Sharing):
                if item.stage == 0 and all(r.stage == 3 for r in item.reductions):
                    sending.append(item)
            elif item.stage < 2:
                sending.append(item)
            else:
                item.stage = 3
        for item in ready:
            if isinstance(item, Sharing) and item.stage == 0 and item not in sending:
                if all(r.stage == 3 for r in item.reductions):
                    sending.append(item)
        reductions = [item for item in sending if isinstance(item, Reduction)]
        if reductions:
            prepare(reductions)
        for item in sending:
            if isinstance(item, Sharing):
                item.prepare()
        values, sent = together(values, [item.sent for item in sending])
        for item, prepared in zip(sending, sent):
            item.sent = prepared
            item.send()
        self.moving = [
            item
            for item in self.moving
            if item.stage < (1 if isinstance(item, Sharing) else 3) or item.left > 0
        ]
        return values


def grouped_columns(values, parts, wide):
    rows = values.shape[0]
    return values.reshape(rows, parts, -1, wide).swapaxes(1, 2).reshape(rows, -1)


def over_heads(part, parts, wide):
    rows = part.shape[0]
    if parts == 4:
        part = part.reshape(rows, -1, parts, wide).swapaxes(1, 2)
    part = part.reshape(rows, parts, -1)
    part = lax.psum_scatter(part, "head", scatter_dimension=2, tiled=True)
    return part.swapaxes(0, 1).astype(F32)


def shared_gain(values, bit):
    return values + hop(values, bit)


def with_halo(inputs, cotangent):
    count = lax.axis_size("head")
    both = jnp.concatenate([inputs, cotangent], axis=1)
    before = lax.ppermute(both[-MOST:], "head", [(i, i + 1) for i in range(count - 1)])
    after = lax.ppermute(both[:MOST], "head", [(i + 1, i) for i in range(count - 1)])
    joined = jnp.concatenate([before, both, after], axis=0).astype(F32)
    return joined[:, : inputs.shape[1]], joined[:, inputs.shape[1] :]


def window_ids(segment_ids, own_rows):
    padded = jnp.pad(segment_ids[0], (MOST, MOST), constant_values=-1)
    begin = lax.axis_index("head") * own_rows
    ids = lax.dynamic_slice(padded, (begin,), (own_rows + 2 * MOST,))
    place = jnp.arange(ids.shape[0])
    earlier = (ids[:, None] == ids[None, :]) & (place[None, :] < place[:, None])
    position = jnp.sum(earlier.astype(F32), axis=1)
    used = (ids >= ids[MOST]) & (ids <= ids[MOST + own_rows - 1])
    column = jnp.where(used, ids, -1)
    row = jnp.where(used, ids, -2)
    starts = [
        min(max(b * QUERY_ROWS - MOST, 0), ids.shape[0] - KEY_ROWS)
        for b in range(ids.shape[0] // QUERY_ROWS)
    ]
    rows = jnp.stack([row[start : start + KEY_ROWS] for start in starts])[:, None, :]
    return position, (column, rows)


def rotary_tables(position, ids, head_width):
    halves = head_width // 2
    frequency = jnp.exp(jnp.arange(halves, dtype=F32) * (-2.0 * math.log(10000.0) / head_width))
    angles = frequency[:, None] * position[None, :]
    column, rows = ids
    count = position.shape[0]
    wide = (count, GROUP * head_width)
    spread = jnp.broadcast_to(column.astype(F32)[None], (8, count))
    cosine, sine, column = kernel_call(
        turning,
        1,
        [whole(angles.shape)] * 2 + [whole(spread.shape)],
        [whole(wide), whole(wide), whole((count, 1))],
        [struct(wide, F32), struct(wide, F32), struct((count, 1), jnp.int32)],
        [],
        1_000_000,
    )(jnp.cos(angles), jnp.sin(angles), spread)
    return (cosine, sine), (column, rows)


def body(
    inputs,
    segment_ids,
    features,
    norm_gain,
    query_key_value,
    output_weight,
    up_weight,
    down_weight,
    cotangent,
):
    layer_count = norm_gain.shape[0]
    own_rows = inputs.shape[0]
    head_width = features.shape[3]
    feature_count = features.shape[2]
    scale = head_width ** (-0.25)
    own_place = slice(MOST, MOST + own_rows)

    in_rows, part_width = output_weight.shape[1:]
    groups = inputs.shape[1] // (GROUP * head_width)
    wide, small = GROUP * head_width, GROUP * feature_count
    table_shapes = [(groups, 4 * wide, small)] * layer_count + [
        (groups, 2 * wide, 2 * small)
    ] * layer_count
    chunks = []
    for layer in range(layer_count):
        chunks.append((4, *query_key_value[layer], output_weight[layer]))
        chunks.append((2, up_weight[layer], down_weight[layer]))
    stored = []
    if by_permutes():
        attention_places = piece_places(in_rows)
        grad_places = block_places(in_rows)
        gain_rows = [[norm_gain[layer, at][None] for at in range(2)] for layer in range(layer_count)]
        feed_places = piece_places(up_weight.shape[1], (0, 1, 2, 5, 6, 7, 3, 4, 8, 9))
        feature_rows = jnp.moveaxis(features, 3, 0).reshape(4, head_width // 4, -1)
        feature_rows = jnp.concatenate(list(feature_rows), axis=1)

        def join(index, came, begin=0):
            parts, *weights = chunks[index]
            return join_columns(came, parts, begin, *weights[-1].shape, wide)

        def gathered_columns(sent):
            return lax.all_gather(sent, "head", axis=0, tiled=False)

        sent = jnp.concatenate([jnp.concatenate(chunks[0][1:], axis=1), feature_rows])
        sent = jnp.broadcast_to(sent[None], (HEAD_DEVICES,) + sent.shape)
        first_feed = jnp.concatenate(chunks[1][1:], axis=1)
        sent, inputs, cotangent = together(sent, inputs, cotangent)
        came = exchange(sent)
        first_feed, inputs, cotangent = together(first_feed, inputs, cotangent)
        came_feed = gathered_columns(first_feed)
        state, gradient = with_halo(inputs, cotangent)
        position, ids = window_ids(segment_ids, own_rows)
        tables, ids = rotary_tables(position, ids, head_width)
        both = []
        for layer in range(1, layer_count):
            q, k, v, o = chunks[2 * layer][1:]
            both.append(
                jnp.concatenate(
                    [
                        jnp.concatenate(pair, axis=1)
                        for pair in ((q, k), (v, o), chunks[2 * layer + 1][1:])
                    ]
                )
            )
        came, state, gradient, tables, ids, gain_rows, attention_places = together(
            came, state, gradient, tables, ids, gain_rows, attention_places
        )
        attend = functools.partial(run_attention_forward, tables=tables, ids=ids, scale=scale)
        own = join(0, came)
        over_x, over_y, over_core = next_chips(own)
        made = feature_tables(came, in_rows, table_shapes)
        over_x, over_y, over_core, made, both = together(over_x, over_y, over_core, made, both)
        blocks, back_blocks = made[:layer_count], made[layer_count:]
        passed = halves_to_pass(over_x, over_y)
        across = chip_across(passed)
        own_feed = join(1, came_feed)
        for layer in range(layer_count):
            more = layer + 1 < layer_count
            near = (own, over_x, over_y) + tuple(across)
            far = (over_core,) + other_core(near[1:])
            attention_pieces = near + far
            own = own_feed
            state, own, sent = together(state, own, both[layer] if more else ())
            over_x, over_y, over_core = next_chips(own)
            came = gathered_columns(sent) if more else ()
            weights, *kept, middle, normed_c = attend(
                state,
                gain_rows[layer],
                attention_pieces,
                attention_places,
                blocks[layer],
            )

            middle, over_x, over_y, over_core = together(middle, over_x, over_y, over_core)
            sides = own, over_x, over_y
            passed = halves_to_pass(over_x, over_y)
            carried, passed = together(middle, passed)
            across = chip_across(passed)
            far_sides = (over_core,) + other_core(sides[1:])
            near_kept = run_feed_forward(carried, normed_c, sides)

            carried, across, far_sides = together(near_kept[2], across, far_sides)
            far_across = other_core(across)
            if more:
                carried, came = together(carried, came)
                carried, own = together(carried, join(2 * layer + 2, came))
                over_x, over_y, over_core = next_chips(own)
            last_pieces = across + far_across
            feed_pieces = sides, far_sides, across, far_across
            if not more:
                rest = run_feed_forward(carried, normed_c, far_sides + last_pieces)
                side = near_kept[0].shape[1]
                stretches = [(near_kept[:2], 0, side), (rest[:2], 0, rest[0].shape[1])]
                stored.append((state, weights, kept, middle, normed_c, stretches, feed_pieces))
                state = rest[2]
                break
            far_kept = run_feed_forward(carried, normed_c, far_sides)

            carried = far_kept[2]
            if more:
                carried, over_x, over_y, over_core = together(carried, over_x, over_y, over_core)
                passed = halves_to_pass(over_x, over_y)
                carried, passed = together(carried, passed)
                across = chip_across(passed)
            last_kept = run_feed_forward(carried, normed_c, last_pieces)
            stretches = kept_stretches(near_kept, far_kept, last_kept)
            stored.append((state, weights, kept, middle, normed_c, stretches, feed_pieces))
            state = last_kept[2]
            if more:
                state, across, came = together(state, across, came)
                own_feed = join(2 * layer + 3, came, 2 * in_rows)
    else:
        gain_rows = [[norm_gain[layer, at][None] for at in range(2)] for layer in range(layer_count)]
        state, gradient = with_halo(inputs, cotangent)
        position, ids = window_ids(segment_ids, own_rows)
        tables, ids = rotary_tables(position, ids, head_width)
        attend = functools.partial(run_attention_forward, tables=tables, ids=ids, scale=scale)
        all_features = lax.all_gather(features, "head", axis=1, tiled=True)
        shaped = all_features.reshape(layer_count, -1, GROUP, feature_count, head_width)
        eye = jnp.eye(GROUP, dtype=BF16)
        block = jnp.einsum("lghmw,hk->lghwkm", shaped, eye).reshape(layer_count, groups, wide, small)
        ones = jnp.kron(eye, jnp.ones((head_width, feature_count), BF16))
        ones = jnp.broadcast_to(ones, block.shape)
        blocks = jnp.concatenate([block, block, ones * -0.5, ones * -0.5], axis=2)
        back_blocks = jnp.concatenate([block, ones], axis=2)
        back_blocks = jnp.concatenate([back_blocks, back_blocks], axis=3)
        owned = []
        for parts, *weights in chunks:
            rows = weights[-1].shape[0]
            joined = jnp.stack(weights)
            joined = lax.all_gather(joined, "head", axis=2, tiled=True)
            joined = lax.all_gather(joined, "dp", axis=1, tiled=True)
            joined = joined.swapaxes(0, 1).reshape(joined.shape[1], -1)
            owned.append(grouped_columns(joined, parts, wide) if parts == 4 else joined)
        middle_row = inputs.shape[1] // 2
        attention_places = jnp.array([0, middle_row], jnp.int32)
        size = up_weight.shape[1] * lax.axis_size("dp") // 8
        feed_places = jnp.array([0, 4 * size, 3 * size, 7 * size], jnp.int32)
        for layer in range(layer_count):
            own_attention, own_feed = owned[2 * layer], owned[2 * layer + 1]
            weights, *kept, middle, normed_c = attend(
                state,
                gain_rows[layer],
                (own_attention[:middle_row], own_attention[middle_row:]),
                attention_places,
                blocks[layer],
            )
            size = own_feed.shape[0] // 8
            feed_pieces = [
                (own_feed[begin * size : end * size],) for begin, end in ((0, 3), (4, 7), (3, 4), (7, 8))
            ]
            near_kept = run_feed_forward(middle, normed_c, feed_pieces[0])
            far_kept = run_feed_forward(near_kept[2], normed_c, feed_pieces[1])
            last_kept = run_feed_forward(far_kept[2], normed_c, feed_pieces[2] + feed_pieces[3])
            stretches = kept_stretches(near_kept, far_kept, last_kept)
            stored.append((state, weights, kept, middle, normed_c, stretches, feed_pieces))
            state = last_kept[2]
    outputs = state[own_place].astype(BF16)

    gains = [None] * layer_count
    shares = [None] * layer_count
    traffic = Traffic()
    summing = []
    for layer in reversed(range(layer_count)):
        before, weights, kept, middle, normed_c, stretches, feed_pieces = stored[layer]
        feed = (middle, gain_rows[layer][1], normed_c)
        attend_back = functools.partial(
            run_attention_backward,
            state=before,
            gain=gain_rows[layer][0],
            weights=weights,
            table=blocks[layer],
            back_table=back_blocks[layer],
            tables=tables,
            ids=ids,
            kept=kept,
            scale=scale,
        )
        if layer > 0 or not by_permutes():
            pieces = [piece for part in feed_pieces for piece in part]
            feed_grad, grad_middle, gain_c, branch = run_feed_back(
                gradient, *feed, stretches, pieces, feed_places, None, True
            )
            feed_part = lax.psum_scatter(feed_grad, "dp", scatter_dimension=0, tiled=True)
            gradient, gain_a, *grad = attend_back(
                tuple(range(groups)),
                None,
                grad_middle=grad_middle,
                branch=branch,
                places=grad_places if by_permutes() else jnp.zeros((1,), jnp.int32),
            )
            if by_permutes():
                gains[layer] = jnp.concatenate([gain_a, gain_c])
                attention_sum = Reduction(grad[0], (1, 1))
                attention_sum.near, attention_sum.left = grad[1], 2
                traffic.moving.append(attention_sum)
                summing.append((layer, feed_part, attention_sum))
                continue
            [grad] = grad
            attention_part = lax.psum_scatter(grad, "dp", scatter_dimension=0, tiled=True)
            gains[layer] = jnp.concatenate([gain_a, gain_c])
            shares[layer] = over_heads(feed_part, 2, wide), over_heads(attention_part, 4, wide)
            continue
        relative = [
            jnp.array(begins_of(feed_pieces[at] + feed_pieces[2 + at])[:-1], jnp.int32) for at in (0, 1)
        ]
        gradient = traffic.slot(gradient)
        feed_far, carried = run_feed_back(
            gradient,
            *feed,
            [stretches[1], stretches[3]],
            feed_pieces[1] + feed_pieces[3],
            relative[1],
            None,
            False,
        )
        carried, feed_far = traffic.slot((carried, feed_far))
        feed_sum = Reduction(feed_far, (1, 1))
        traffic.moving.append(feed_sum)
        feed_near, grad_middle, gain_c, branch = run_feed_back(
            gradient,
            *feed,
            [stretches[0], stretches[2]],
            feed_pieces[0] + feed_pieces[2],
            relative[0],
            carried,
            True,
        )
        feed_sum.near = feed_near
        feed_share = Sharing([feed_sum], 2, wide, 2)
        traffic.moving.append(feed_share)
        carried, attention_sums = None, []
        for call_groups in (tuple(range(groups - 1)), (groups - 1,)):
            if attention_sums:
                for index, (later, feed_part, attention_sum) in enumerate(summing):
                    carried, feed_part = together(carried, feed_part)
                    parted = part_columns([[feed_part]], 2, wide)
                    share = Sharing([], 2, wide, 2)
                    carried, share.sent = together(carried, parted)
                    share.send()
                    traffic.moving.append(share)
                    summing[index] = later, share, attention_sum
            branch, grad_middle, carried = traffic.slot((branch, grad_middle, carried))
            if attention_sums:
                traffic.moving.append(attention_sums[-1])
            carried, *gain_a, far, near = attend_back(
                call_groups, carried, grad_middle=grad_middle, branch=branch, places=grad_places
            )
            carried, far, near = together(carried, far, near)
            attention_sums.append(Reduction(far, (1, 1)))
            attention_sums[-1].near = near
        gradient = carried
        gains[layer] = jnp.concatenate([*gain_a, gain_c])
        traffic.moving.append(attention_sums[-1])
        attention_share = Sharing(attention_sums, 4, wide, 1)
        traffic.moving.append(attention_share)
        shares[layer] = feed_share, attention_share
    if by_permutes():
        gain_all = jnp.concatenate(gains)
        input_grad = gradient[own_place]
        gain_all = traffic.slot(gain_all)
        attention_parts = []
        for later, share, attention_sum in reversed(summing):
            parted = part_columns([attention_sum.arrays()], 4, wide)
            gain_all, parted = together(gain_all, parted)
            parted = lax.psum_scatter(parted, "head", scatter_dimension=0, tiled=True)
            attention_parts.append(parted)
            shares[later] = share, parted
        gain_all = shared_gain(shared_gain(gain_all, CORE), X)
        gain_all = traffic.slot(gain_all)
        gain_all, outputs, input_grad = together(gain_all, outputs, input_grad)
        gain_all = shared_gain(gain_all, Y)
        attention_share.gain = gain_all
        attention_parts = traffic.slot(attention_parts)
        feed_shares = [share[0].came for share in shares]
        turned = finish(feed_shares, (1, 1), up_weight.shape[1], turned=True)
        up_grad, down_grad = traffic.slot(turned)
        up_grad, down_grad = up_grad.swapaxes(1, 2), down_grad.swapaxes(1, 2)
        assert not traffic.moving
        qkv_grad, out_grad, gain_total = finish(
            [shares[0][1].came] + attention_parts, (3, 1), in_rows, 2 * layer_count
        )
        gain_total = gain_total.reshape(layer_count, 2, -1)
    else:
        gain_total = lax.psum(jnp.stack(gains), ("dp", "head"))
        input_grad = gradient[own_place]
        results = [(a[:3], a[3], f[0], f[1]) for f, a in shares]
        qkv_grad, out_grad, up_grad, down_grad = (
            jnp.stack(list(kind)) for kind in zip(*results)
        )
    return (
        outputs,
        input_grad,
        gain_total[:, 0],
        gain_total[:, 1],
        qkv_grad,
        out_grad,
        up_grad,
        down_grad,
    )


def solution(mesh):
    in_specs = (
        P(("dp", "head"), None),
        P("dp", None),
        P(None, "head", None, None),
        P(),
        P(None, None, "dp", "head"),
        P(None, "dp", "head"),
        P(None, "dp", "head"),
        P(None, "dp", "head"),
        P(("dp", "head"), None),
    )
    out_specs = (
        P(("dp", "head"), None),
        P(("dp", "head"), None),
        P(),
        P(),
        P(None, None, "dp", "head"),
        P(None, "dp", "head"),
        P(None, "dp", "head"),
        P(None, "dp", "head"),
    )
    return jax.shard_map(body, mesh=mesh, in_specs=in_specs, out_specs=out_specs, check_vma=False)
```
